32 devices in a mesh: seq: 8 (over z, y), dp: 4 (over x, core).
Axes of the slice: x: 2, y: 2, z: 4, core: 2. Of those that a mesh axis runs over, the one named last changes fastest.
Arguments:
- inputs: bfloat16 [4, 2048, 324], P('dp', 'seq'), may hold values from -6 to 6
- w_qkv: bfloat16 [324, 972], replicated, may hold values from -0.3125 to 0.3125
- w_pos: bfloat16 [324, 324], replicated, may hold values from -0.625 to 0.625
- w_out: bfloat16 [324, 324], replicated, may hold values from -1.25 to 1.25
- rel_bias: float32 [2, 324], replicated, may hold values from -3 to 3
- ffn_in: bfloat16 [2, 324, 1296], replicated, may hold values from -0.3125 to 0.3125
- ffn_out: bfloat16 [2, 1296, 324], replicated, may hold values from -0.15625 to 0.15625
- conv_in: bfloat16 [324, 648], replicated, may hold values from -0.3125 to 0.3125
- conv_depth: float32 [31, 324], replicated, may hold values from -1 to 1
- conv_out: bfloat16 [324, 324], replicated, may hold values from -0.3125 to 0.3125
- bn_gain: float32 [324], replicated, may hold values from 0.5 to 1.5
- bn_bias: float32 [324], replicated, may hold values from -2 to 2
- norm_gain: float32 [4, 324], replicated, may hold values from 0.5 to 1.5
- norm_bias: float32 [4, 324], replicated, may hold values from -2 to 2
- lengths: int32 [4, 8], P('dp'), may hold values from 1 to 1920, as said below
- cotangent: float32 [4, 2048, 324], P('dp', 'seq'), may hold values from -6 to 6
Outputs:
- layer_out: float32 [4, 2048, 324], P('dp', 'seq')
- input_grad: float32 [4, 2048, 324], P('dp', 'seq')
- grad_w_qkv: float32 [324, 972], replicated
- grad_w_pos: float32 [324, 324], replicated
- grad_w_out: float32 [324, 324], replicated
- grad_rel_bias: float32 [2, 324], replicated
- grad_ffn_in: float32 [2, 324, 1296], replicated
- grad_ffn_out: float32 [2, 1296, 324], replicated
- grad_conv_in: float32 [324, 648], replicated
- grad_conv_depth: float32 [31, 324], replicated
- grad_conv_out: float32 [324, 324], replicated
- grad_bn_gain: float32 [324], replicated
- grad_bn_bias: float32 [324], replicated
- grad_norm_gain: float32 [4, 324], replicated
- grad_norm_bias: float32 [4, 324], replicated
The draws below stay inside these ranges and needn't reach their ends.
Inputs may be any that keep to these rules, and one draw needn't show every extreme that they name: `lengths`: in each stream one clip has exactly 1920 frames and starts within the first 128 frames; every other clip has at most 16 frames, and the one after the longest (cyclically) has 1; all clips together leave 1 to 127 unused frames at the end of the stream.
All inputs are finite; a program needn't handle non-finite values.
Results may differ from the reference program's by a relative error of at most 0.02.
Values may be sent and summed in bfloat16 or wider, within the bound.
No kernel may reach another device: no remote copies, remote signals or barrier semaphores. Data moves between devices by JAX's collectives and lax.ppermute only.
A program may use at most 192 MiB of HBM per device.

```python
import math
import jax
import jax.numpy as jnp
from jax import lax

D = 324
HEADS = 4
FF = 1296
KERNEL = 31
CLIPS = 8
TOK_DEV = 256
HEAD_DIM = 81
STREAMS = 4
FRAMES = 2048


def draw_lengths(key, part):
    key = jax.random.fold_in(key, 7)
    short_key, place_key = jax.random.split(key, 2)
    short_most = TOK_DEV // (2 * CLIPS)
    shorter = jax.random.randint(short_key, (STREAMS, CLIPS), 1, short_most + 1)
    placed = jax.random.randint(place_key, (STREAMS, 1), 0, CLIPS)
    columns = jnp.arange(CLIPS)[None, :]
    longest = columns == placed
    single = columns == (placed + 1) % CLIPS
    shorter = jnp.where(single, 1, shorter)
    return jnp.where(longest, FRAMES - TOK_DEV // 2, shorter).astype(jnp.int32)


def block_scale(stream_key, extent, shards, low, largest):
    level, own = 1.0, jax.random.fold_in(stream_key, 6)
    for axis_at, parts in shards:
        steps = jnp.exp(jax.random.uniform(jax.random.fold_in(own, axis_at), (parts,), jnp.float32, low / len(shards), largest / len(shards)))
        level = level * jnp.repeat(steps, extent[axis_at] // parts).reshape([-1 if axis == axis_at else 1 for axis in range(len(extent))])
    return level


def scatter_about(rng, extent, scale, limit, cuts=(), kind=jnp.bfloat16):
    loudness = block_scale(rng, extent, cuts, -0.22, 0.18) if cuts else 1.0
    drawn = jax.random.normal(rng, extent, jnp.float32) * scale * loudness
    return jnp.minimum(jnp.maximum(drawn, -limit), limit).astype(kind)


def setup_inputs(seed: int = 0) -> dict:
    arg_keys = jax.random.split(jax.random.key(seed), 17)
    return {
        "inputs": scatter_about(arg_keys[0], (STREAMS, FRAMES, D), 1.0, 6.0, ((0, 4), (1, 8))),
        "w_qkv": scatter_about(arg_keys[1], (D, 3 * D), D ** -0.5, 0.3125),
        "w_pos": scatter_about(arg_keys[2], (D, D), HEAD_DIM ** -0.5, 0.625),
        "w_out": scatter_about(arg_keys[3], (D, D), (D // 16) ** -0.5, 1.25),
        "rel_bias": scatter_about(arg_keys[4], (2, D), 0.5, 3.0, (), jnp.float32),
        "ffn_in": scatter_about(arg_keys[5], (2, D, FF), D ** -0.5, 0.3125),
        "ffn_out": scatter_about(arg_keys[6], (2, FF, D), FF ** -0.5, 0.15625),
        "conv_in": scatter_about(arg_keys[7], (D, 2 * D), D ** -0.5, 0.3125),
        "conv_depth": scatter_about(arg_keys[8], (KERNEL, D), KERNEL ** -0.5, 1.0, (), jnp.float32),
        "conv_out": scatter_about(arg_keys[9], (D, D), D ** -0.5, 0.3125),
        "bn_gain": jnp.clip(1.0 + 0.1 * jax.random.normal(arg_keys[10], (D,), jnp.float32), 0.5, 1.5),
        "bn_bias": scatter_about(arg_keys[11], (D,), 0.3, 2.0, (), jnp.float32),
        "norm_gain": jnp.clip(1.0 + 0.1 * jax.random.normal(arg_keys[12], (4, D), jnp.float32), 0.5, 1.5),
        "norm_bias": scatter_about(arg_keys[13], (4, D), 0.3, 2.0, (), jnp.float32),
        "lengths": draw_lengths(jax.random.fold_in(arg_keys[16], 71), 0),
        "cotangent": scatter_about(arg_keys[15], (STREAMS, FRAMES, D), 1.0, 6.0, ((0, 4), (1, 8)), jnp.float32),
    }


@jax.custom_vjp
def low(v):
    return lax.optimization_barrier(v.astype(jnp.bfloat16)).astype(jnp.float32)

@jax.custom_vjp
def low_back(v):
    return v

def low_keep(v):
    return (low(v), None)

def low_pass(kept, grad):
    return (grad,)

def back_keep(v):
    return (v, None)

def back_low(kept, grad):
    return (low(grad),)
low.defvjp(low_keep, low_pass)
low_back.defvjp(back_keep, back_low)

def layer_norm(summed, gain_row, bias_row):
    average = lax.optimization_barrier(jnp.mean(summed, axis=-1, keepdims=True))
    centered = summed - average
    variance = lax.optimization_barrier(jnp.mean(centered * centered, axis=-1, keepdims=True))
    return centered * lax.rsqrt(variance + 1e-05) * gain_row + bias_row

def matmul(left, right):
    return jnp.einsum('sfd,de->sfe', left, right, precision=lax.Precision.HIGHEST)

def frame_tables(positions, model_width):
    frequency = jnp.exp(jnp.arange(model_width // 2, dtype=jnp.float32) * (-2.0 * math.log(10000.0) / model_width))
    angles = positions.astype(jnp.float32)[:, None] * frequency[None, :]
    return (jnp.sin(angles), jnp.cos(angles))

def clip_of(positions, clip_ends):
    return lax.optimization_barrier(jnp.sum((positions[:, None] >= clip_ends[None, :]).astype(jnp.int32), axis=1))

def rotate(shifted, sines, cosines):
    half_width = shifted.shape[-1] // 2
    first_half = shifted[..., :half_width]
    second_half = shifted[..., half_width:]
    return jnp.concatenate([first_half * sines + second_half * cosines, second_half * sines - first_half * cosines], axis=-1)

def feed_forward(hidden, weight_in, weight_out):
    inner = low_back(matmul(low(hidden), weight_in))
    return low_back(matmul(low(jax.nn.silu(inner)), weight_out))

def stream_attention(query_unit, query_pos, keys, values, key_table, clips):
    total_frames = query_unit.shape[0]
    block_count = total_frames // TOK_DEV

    def one_block(pieces):
        unit_block, pos_block, clip_block = pieces
        raw = jnp.einsum('qhd,khd->hqk', unit_block, keys, precision=lax.Precision.HIGHEST)
        raw = raw + jnp.einsum('qhc,kc->hqk', pos_block, key_table, precision=lax.Precision.HIGHEST)
        raw = low_back(raw)
        scores = raw / math.sqrt(keys.shape[-1])
        same_clip = clip_block[:, None] == clips[None, :]
        masked = jnp.where(same_clip[None], scores, -1e+30)
        highest = lax.optimization_barrier(jnp.max(masked, axis=-1, keepdims=True))
        total = lax.optimization_barrier(jnp.sum(jnp.exp(masked - highest), axis=-1, keepdims=True))
        log_total = highest + jnp.log(total)
        weights = low(jnp.exp(masked - log_total))
        return jnp.einsum('hqk,khd->qhd', weights, values, precision=lax.Precision.HIGHEST)
    pieces = (query_unit.reshape(block_count, TOK_DEV, query_unit.shape[1], -1), query_pos.reshape(block_count, TOK_DEV, query_pos.shape[1], -1), clips.reshape(block_count, TOK_DEV))
    result = lax.map(jax.checkpoint(one_block), pieces)
    return result.reshape(total_frames, query_unit.shape[1], -1)

def reference(inputs, w_qkv, w_pos, w_out, rel_bias, ffn_in, ffn_out, conv_in, conv_depth, conv_out, bn_gain, bn_bias, norm_gain, norm_bias, lengths, cotangent):
    stream_count, total_frames, model_width = inputs.shape
    positions = jnp.arange(total_frames, dtype=jnp.int32)
    clip_ends = jnp.cumsum(lengths, axis=1).astype(jnp.int32)
    clips = jax.vmap(lambda ends_row: clip_of(positions, ends_row))(clip_ends)
    valid_rows = (positions[None, :] < clip_ends[:, -1:]).astype(jnp.float32)[..., None]
    sines, cosines = frame_tables(positions, model_width)
    key_table = low(jnp.concatenate([cosines, sines], axis=1))
    reach = KERNEL // 2
    padded_clips = jnp.pad(clips, ((0, 0), (reach, reach)), constant_values=-1)

    def layer(signal, qkv_weight, pos_weight, out_weight, biases, inner_weight, outer_weight, gate_weight, depth_weight, point_weight, batch_gain, batch_bias, gains, shifts):
        projected = low_back(matmul(signal, qkv_weight))
        query_part = projected[..., :model_width]
        keys = low(projected[..., model_width:2 * model_width]).reshape(stream_count, total_frames, HEADS, -1)
        values = low(projected[..., 2 * model_width:]).reshape(stream_count, total_frames, HEADS, -1)
        query_unit = low(query_part + biases[0]).reshape(stream_count, total_frames, HEADS, -1)
        query_shift = low(query_part + biases[1]).reshape(stream_count, total_frames, HEADS, -1)
        pos_grid = pos_weight.reshape(model_width, HEADS, -1)
        shifted = low_back(jnp.einsum('sfhd,chd->sfhc', query_shift, pos_grid, precision=lax.Precision.HIGHEST))
        query_pos = low(rotate(shifted, sines[:, None, :], cosines[:, None, :]))
        attended = lax.map(lambda pieces: stream_attention(pieces[0], pieces[1], pieces[2], pieces[3], key_table, pieces[4]), (query_unit, query_pos, keys, values, clips))
        branch = low_back(matmul(low(attended.reshape(stream_count, total_frames, model_width)), out_weight))
        first_norm = layer_norm(signal + branch, gains[0], shifts[0])
        second_norm = layer_norm(first_norm + feed_forward(first_norm, inner_weight[0], outer_weight[0]), gains[1], shifts[1])
        gate_values = low_back(matmul(low(second_norm), gate_weight))
        gated = low(gate_values[..., :model_width] * jax.nn.sigmoid(gate_values[..., model_width:]))
        padded = jnp.pad(gated, ((0, 0), (reach, reach), (0, 0)))
        convolved = jnp.zeros_like(gated)
        for offset in range(2 * reach + 1):
            same_clip = (padded_clips[:, offset:offset + total_frames] == clips)[..., None]
            convolved = convolved + depth_weight[offset] * jnp.where(same_clip, padded[:, offset:offset + total_frames], 0.0)
        convolved = low_back(convolved)
        frame_count = jnp.sum(valid_rows)
        batch_mean = lax.optimization_barrier(jnp.sum(convolved * valid_rows, axis=(0, 1))) / frame_count
        batch_var = lax.optimization_barrier(jnp.sum(convolved * convolved * valid_rows, axis=(0, 1))) / frame_count - batch_mean * batch_mean
        normed = (convolved - batch_mean) * lax.rsqrt(batch_var + 1e-05) * batch_gain + batch_bias
        conv_branch = low_back(matmul(low(jax.nn.silu(normed)), point_weight))
        third_norm = layer_norm(second_norm + conv_branch, gains[2], shifts[2])
        return layer_norm(third_norm + feed_forward(third_norm, inner_weight[1], outer_weight[1]), gains[3], shifts[3])
    floats = (inputs.astype(jnp.float32), w_qkv.astype(jnp.float32), w_pos.astype(jnp.float32), w_out.astype(jnp.float32), rel_bias.astype(jnp.float32), ffn_in.astype(jnp.float32), ffn_out.astype(jnp.float32), conv_in.astype(jnp.float32), conv_depth.astype(jnp.float32), conv_out.astype(jnp.float32), bn_gain.astype(jnp.float32), bn_bias.astype(jnp.float32), norm_gain.astype(jnp.float32), norm_bias.astype(jnp.float32))
    layer_out, pull_back = jax.vjp(layer, *floats)
    grads = pull_back(cotangent.astype(jnp.float32))
    return (layer_out, grads[0], grads[1], grads[2], grads[3], grads[4], grads[5], grads[6], grads[7], grads[8], grads[9], grads[10], grads[11], grads[12], grads[13])
```

```python
import math

import jax
import jax.numpy as jnp
from jax import lax
from jax.sharding import PartitionSpec as P

HEADS = 4

MODEL_AXES = ("seq", "dp")


def device_count():
    return lax.axis_size("seq") * lax.axis_size("dp")


def flat_index():
    return lax.axis_index("seq") * lax.axis_size("dp") + lax.axis_index("dp")


def swap_flat(block, distance):
    pairs = [(i, i ^ distance) for i in range(device_count())]
    return lax.ppermute(block, MODEL_AXES, pairs)


def swap_seq(block, distance):
    pairs = [(i, i ^ distance) for i in range(lax.axis_size("seq"))]
    return lax.ppermute(block, "seq", pairs)


def pick(stacked, index):
    return lax.dynamic_index_in_dim(stacked, index, 0, keepdims=False)


def stage_radices(devices):
    radices = [2]
    left = devices // 2
    while left > 1:
        radix = 4 if left % 4 == 0 else 2
        radices.append(radix)
        left = left // radix
    return radices


def sum_everywhere(pieces):
    devices, rows, width = pieces.shape
    radices = stage_radices(devices)
    place = flat_index()
    held = pieces
    strides = []
    stride = 1
    for radix in radices:
        digit = (place // stride) % radix
        held = held.reshape(radix, held.shape[0] // radix, rows, width)
        total = pick(held, digit).astype(jnp.float32)
        arrived = [
            swap_flat(pick(held, digit ^ step), step * stride) for step in range(radix - 1, 0, -1)
        ]
        for part in arrived:
            total = total + part.astype(jnp.float32)
        held = total.astype(pieces.dtype)
        strides.append(stride)
        stride = stride * radix
    for radix, stride in zip(radices[::-1], strides[::-1]):
        digit = (place // stride) % radix
        arrived = [held] + [swap_flat(held, step * stride) for step in range(1, radix)]
        gathered = jnp.zeros((radix,) + held.shape, held.dtype)
        for step in range(radix):
            gathered = lax.dynamic_update_index_in_dim(gathered, arrived[step], digit ^ step, 0)
        held = gathered.reshape(radix * held.shape[0], rows, width)
    return held


def sum_rows_everywhere(parts):
    devices = device_count()
    width = parts[0].shape[1]
    rows = sum(part.shape[0] for part in parts)
    share = -(-rows // (16 * devices)) * 16
    padding = jnp.zeros((share * devices - rows, width), jnp.bfloat16)
    packed = jnp.concatenate([part.astype(jnp.bfloat16) for part in parts] + [padding], axis=0)
    summed = sum_everywhere(packed.reshape(devices, share, width)).reshape(share * devices, width)
    result = []
    start = 0
    for part in parts:
        result.append(summed[start : start + part.shape[0]].astype(jnp.float32))
        start = start + part.shape[0]
    return result


def sum_small(rows_list):
    flat = jnp.concatenate([jnp.ravel(row) for row in rows_list])
    tiles = -(-flat.shape[0] // 1024)
    tile = jnp.pad(flat, (0, tiles * 1024 - flat.shape[0])).reshape(tiles * 8, 128)
    devices = device_count()
    spread = jnp.broadcast_to(tile[None], (devices,) + tile.shape)
    summed = jnp.sum(lax.all_to_all(spread, MODEL_AXES, 0, 0), axis=0).reshape(-1)
    result = []
    start = 0
    for row in rows_list:
        size = math.prod(row.shape)
        result.append(summed[start : start + size].reshape(row.shape))
        start = start + size
    return result


def gather_frames(shard):
    count = lax.axis_size("seq")
    across = [shard] + [swap_seq(shard, 2 * step) for step in range(1, count // 2)]
    blocks = []
    for block in across:
        blocks.append(block)
        blocks.append(swap_seq(block, 1))
    return jnp.stack(blocks)


def scatter_frames(partials):
    count = lax.axis_size("seq")
    total = None
    for step in range(count // 2 - 1, -1, -1):
        joined = partials[2 * step].astype(jnp.float32) + swap_seq(
            partials[2 * step + 1], 1
        ).astype(jnp.float32)
        if step > 0:
            joined = swap_seq(joined.astype(jnp.bfloat16), 2 * step).astype(jnp.float32)
        total = joined if total is None else total + joined
    return total


def column_tiles(array, width):
    return [array[:, start : start + width] for start in range(0, array.shape[1], width)]


def with_halo(block, sides, width):
    for axis, dim in sides:
        count = lax.axis_size(axis)
        forward = [(i, i + 1) for i in range(count - 1)]
        backward = [(target, source) for source, target in forward]
        low = lax.ppermute(
            lax.slice_in_dim(block, block.shape[dim] - width, None, axis=dim), axis, forward
        )
        high = lax.ppermute(lax.slice_in_dim(block, 0, width, axis=dim), axis, backward)
        block = jnp.concatenate([low, block, high], axis=dim)
    return block


def layer_norm(summed, gain_row, bias_row):
    average = jnp.mean(summed, axis=-1, keepdims=True)
    centered = summed - average
    variance = jnp.mean(centered * centered, axis=-1, keepdims=True)
    return centered * lax.rsqrt(variance + 1e-05) * gain_row + bias_row


def norm_back(summed, gain_row, bias_row, incoming):
    return jax.vjp(layer_norm, summed, gain_row, bias_row)[1](incoming)


def frame_tables(positions, model_width):
    frequency = jnp.exp(
        jnp.arange(model_width // 2, dtype=jnp.float32) * (-2.0 * math.log(10000.0) / model_width)
    )
    angles = positions.astype(jnp.float32)[:, None] * frequency[None, :]
    return (jnp.sin(angles), jnp.cos(angles))


def clip_of(positions, clip_ends):
    return jnp.sum((positions[:, None] >= clip_ends[None, :]).astype(jnp.int32), axis=1)


def rotate(shifted, sines, cosines):
    half_width = shifted.shape[-1] // 2
    first_half = shifted[..., :half_width]
    second_half = shifted[..., half_width:]
    return jnp.concatenate(
        [first_half * sines + second_half * cosines, second_half * sines - first_half * cosines],
        axis=-1,
    )


def plain_product(left, right):
    return jnp.dot(left, right, preferred_element_type=jnp.float32)


def times_transposed(left, right):
    return lax.dot_general(
        left, right, (((1,), (1,)), ((), ())), preferred_element_type=jnp.float32
    )


def transposed_times(left, right):
    return lax.dot_general(
        left, right, (((0,), (0,)), ((), ())), preferred_element_type=jnp.float32
    )


def gated_half(projected):
    half_width = projected.shape[1] // 2
    return projected[:, :half_width] * jax.nn.sigmoid(projected[:, half_width:])


def feed_forward(hidden_low, weight_in, weight_out):
    inner = plain_product(hidden_low, weight_in)
    activated = jax.nn.silu(inner).astype(jnp.bfloat16)
    return (inner, activated, plain_product(activated, weight_out))


def feed_back(hidden_low, inner, activated, weight_in, weight_out, incoming):
    incoming_low = incoming.astype(jnp.bfloat16)
    grad_out = transposed_times(activated, incoming_low)
    grad_act = times_transposed(incoming_low, weight_out)
    grad_inner = jax.vjp(jax.nn.silu, inner)[1](grad_act)[0].astype(jnp.bfloat16)
    grad_in = transposed_times(hidden_low, grad_inner)
    return (times_transposed(grad_inner, weight_in), grad_in, grad_out)


def block_scores(query_unit, query_pos, key_block, table_block, same_clip):
    raw = jnp.einsum("qhd,khd->hqk", query_unit, key_block, preferred_element_type=jnp.float32)
    raw = raw + jnp.einsum(
        "qhc,kc->hqk", query_pos, table_block, preferred_element_type=jnp.float32
    )
    return jnp.where(same_clip[None], raw / math.sqrt(query_unit.shape[2]), -1e30)


def block_rows(shard_rows, shard_count):
    parts = max(1, 512 // shard_rows)
    while shard_count % parts != 0:
        parts = parts - 1
    return shard_rows * parts


def local(
    inputs,
    w_qkv,
    w_pos,
    w_out,
    rel_bias,
    ffn_in,
    ffn_out,
    conv_in,
    conv_depth,
    conv_out,
    bn_gain,
    bn_bias,
    norm_gain,
    norm_bias,
    lengths,
    cotangent,
):
    input_low = inputs[0]
    input_float = input_low.astype(jnp.float32)
    frame_rows, model_width = input_low.shape
    head_count = HEADS
    head_width = model_width // head_count
    shard_count = lax.axis_size("seq")
    total_frames = frame_rows * shard_count
    first_frame = lax.axis_index("seq") * frame_rows
    clip_ends = jnp.cumsum(lengths[0])
    local_frames = first_frame + jnp.arange(frame_rows, dtype=jnp.int32)
    local_clip = clip_of(local_frames, clip_ends)
    valid_rows = (local_frames < clip_ends[-1]).astype(jnp.float32)[:, None]
    block_order = lax.axis_index("seq") ^ jnp.arange(shard_count, dtype=jnp.int32)
    all_frames = (
        block_order[:, None] * frame_rows + jnp.arange(frame_rows, dtype=jnp.int32)[None, :]
    ).reshape(total_frames)
    key_span = block_rows(frame_rows, shard_count)
    block_count = total_frames // key_span
    key_clip = clip_of(all_frames, clip_ends).reshape(block_count, key_span)
    all_sines, all_cosines = frame_tables(all_frames, model_width)
    key_table = (
        jnp.concatenate([all_cosines, all_sines], axis=1)
        .astype(jnp.bfloat16)
        .reshape(block_count, key_span, model_width)
    )
    local_sines, local_cosines = frame_tables(local_frames, model_width)

    def rotate_local(grid):
        return rotate(grid, local_sines[:, None, :], local_cosines[:, None, :])

    def split_keys(array):
        return array.reshape(block_count, key_span, head_count, head_width)

    frames_all = gather_frames(input_low)
    query_part = plain_product(input_low, w_qkv[:, :model_width])
    pair_all = plain_product(
        frames_all.reshape(total_frames, model_width), w_qkv[:, model_width:]
    ).astype(jnp.bfloat16)
    keys_all = pair_all[:, :model_width]
    values_all = pair_all[:, model_width:]
    query_unit = (
        (query_part + rel_bias[0]).astype(jnp.bfloat16).reshape(frame_rows, head_count, head_width)
    )
    query_shift = (
        (query_part + rel_bias[1]).astype(jnp.bfloat16).reshape(frame_rows, head_count, head_width)
    )
    pos_grid = w_pos.reshape(model_width, head_count, head_width)
    shifted = jnp.einsum("fhd,chd->fhc", query_shift, pos_grid, preferred_element_type=jnp.float32)
    query_pos = rotate_local(shifted).astype(jnp.bfloat16)
    def scores_of(key_block, table_block, clip_block):
        same_clip = local_clip[:, None] == clip_block[None, :]
        return block_scores(query_unit, query_pos, key_block, table_block, same_clip)

    def norm_step(carry, pieces):
        highest, total = carry
        key_block, table_block, clip_block = pieces
        scores = scores_of(key_block, table_block, clip_block)
        new_highest = jnp.maximum(highest, jnp.max(scores, axis=2))
        total = total * jnp.exp(highest - new_highest) + jnp.sum(
            jnp.exp(scores - new_highest[..., None]), axis=2
        )
        return ((new_highest, total), None)

    start_carry = (
        jnp.full((head_count, frame_rows), -1e30, jnp.float32),
        jnp.zeros((head_count, frame_rows), jnp.float32),
    )
    (highest, total), _ = lax.scan(
        norm_step, start_carry, (split_keys(keys_all), key_table, key_clip)
    )
    log_total = highest + jnp.log(total)

    def value_step(summed, pieces):
        key_block, value_block, table_block, clip_block = pieces
        weights = jnp.exp(
            scores_of(key_block, table_block, clip_block) - log_total[..., None]
        ).astype(jnp.bfloat16)
        return (
            summed
            + jnp.einsum("hqk,khd->qhd", weights, value_block, preferred_element_type=jnp.float32),
            None,
        )

    attended, _ = lax.scan(
        value_step,
        jnp.zeros((frame_rows, head_count, head_width), jnp.float32),
        (split_keys(keys_all), split_keys(values_all), key_table, key_clip),
    )
    attended_low = attended.reshape(frame_rows, model_width).astype(jnp.bfloat16)
    first_sum = input_float + plain_product(attended_low, w_out)
    first_norm = layer_norm(first_sum, norm_gain[0], norm_bias[0])
    first_low = first_norm.astype(jnp.bfloat16)
    inner_early, act_early, out_early = feed_forward(first_low, ffn_in[0], ffn_out[0])
    second_sum = first_norm + out_early
    second_norm = layer_norm(second_sum, norm_gain[1], norm_bias[1])
    second_low = second_norm.astype(jnp.bfloat16)
    gate_values = plain_product(second_low, conv_in)
    gated = gated_half(gate_values).astype(jnp.bfloat16)
    reach = conv_depth.shape[0] // 2
    ext_clip = clip_of(
        first_frame - reach + jnp.arange(frame_rows + 2 * reach, dtype=jnp.int32), clip_ends
    )
    gated_ext = with_halo(gated, (("seq", 0),), reach)
    convolved = jnp.zeros((frame_rows, model_width), jnp.float32)
    for offset in range(2 * reach + 1):
        same_clip = (ext_clip[offset : offset + frame_rows] == local_clip)[:, None]
        convolved = convolved + conv_depth[offset] * jnp.where(
            same_clip, gated_ext[offset : offset + frame_rows].astype(jnp.float32), 0.0
        )
    frame_count, first_moment, second_moment = sum_small(
        (
            jnp.sum(valid_rows),
            jnp.sum(convolved * valid_rows, axis=0),
            jnp.sum(convolved * convolved * valid_rows, axis=0),
        )
    )
    batch_mean = first_moment / frame_count
    batch_var = second_moment / frame_count - batch_mean * batch_mean
    inverse_std = lax.rsqrt(batch_var + 1e-05)
    centered_conv = (convolved - batch_mean) * inverse_std
    normed = centered_conv * bn_gain + bn_bias
    swished = jax.nn.silu(normed).astype(jnp.bfloat16)
    third_sum = second_norm + plain_product(swished, conv_out)
    third_norm = layer_norm(third_sum, norm_gain[2], norm_bias[2])
    third_low = third_norm.astype(jnp.bfloat16)
    inner_late, act_late, out_late = feed_forward(third_low, ffn_in[1], ffn_out[1])
    fourth_sum = third_norm + out_late
    result = layer_norm(fourth_sum, norm_gain[3], norm_bias[3])
    grad_fourth, gain_three, bias_three = norm_back(
        fourth_sum, norm_gain[3], norm_bias[3], cotangent[0]
    )
    from_late, d_in_late, d_out_late = feed_back(
        third_low, inner_late, act_late, ffn_in[1], ffn_out[1], grad_fourth
    )
    grad_third, gain_two, bias_two = norm_back(
        third_sum, norm_gain[2], norm_bias[2], grad_fourth + from_late
    )
    third_grad_low = grad_third.astype(jnp.bfloat16)
    d_conv_out = transposed_times(swished, third_grad_low)
    d_swished = times_transposed(third_grad_low, conv_out)
    late_sums = sum_rows_everywhere(column_tiles(d_in_late, model_width) + [d_out_late, d_conv_out])
    d_normed = jax.vjp(jax.nn.silu, normed)[1](d_swished)[0]
    scaled = d_normed * bn_gain
    d_bn_gain, d_bn_bias = sum_small(
        (jnp.sum(d_normed * centered_conv, axis=0), jnp.sum(d_normed, axis=0))
    )
    sum_scaled = d_bn_bias * bn_gain
    sum_product = d_bn_gain * bn_gain
    d_conv = (
        inverse_std
        * (scaled - valid_rows * (sum_scaled + centered_conv * sum_product) / frame_count)
    ).astype(jnp.bfloat16)
    d_conv_ext = with_halo(d_conv, (("seq", 0),), reach)
    d_conv_float = d_conv.astype(jnp.float32)
    d_gated = jnp.zeros((frame_rows, model_width), jnp.float32)
    depth_terms = []
    for offset in range(2 * reach + 1):
        same_clip = (ext_clip[offset : offset + frame_rows] == local_clip)[:, None]
        depth_terms.append(
            jnp.sum(
                jnp.where(
                    same_clip, gated_ext[offset : offset + frame_rows].astype(jnp.float32), 0.0
                )
                * d_conv_float,
                axis=0,
            )
        )
        mirror = 2 * reach - offset
        mirror_clip = (ext_clip[mirror : mirror + frame_rows] == local_clip)[:, None]
        d_gated = d_gated + conv_depth[offset] * jnp.where(
            mirror_clip, d_conv_ext[mirror : mirror + frame_rows].astype(jnp.float32), 0.0
        )
    d_depth = jnp.stack(depth_terms)
    d_gates = jax.vjp(gated_half, gate_values)[1](d_gated)[0].astype(jnp.bfloat16)
    d_conv_in = transposed_times(second_low, d_gates)
    grad_second, gain_one, bias_one = norm_back(
        second_sum, norm_gain[1], norm_bias[1], grad_third + times_transposed(d_gates, conv_in)
    )
    from_early, d_in_early, d_out_early = feed_back(
        first_low, inner_early, act_early, ffn_in[0], ffn_out[0], grad_second
    )
    grad_first, gain_zero, bias_zero = norm_back(
        first_sum, norm_gain[0], norm_bias[0], grad_second + from_early
    )
    first_grad_low = grad_first.astype(jnp.bfloat16)
    d_w_out = transposed_times(attended_low, first_grad_low)
    d_attended = (
        times_transposed(first_grad_low, w_out)
        .astype(jnp.bfloat16)
        .reshape(frame_rows, head_count, head_width)
    )
    keys_back, values_back = (keys_all, values_all)

    key_pieces = (split_keys(keys_back), split_keys(values_back), key_table, key_clip)
    delta = jnp.einsum("qhd,qhd->hq", d_attended.astype(jnp.float32), attended)
    early_sums = sum_rows_everywhere(
        column_tiles(d_in_early, model_width)
        + [d_out_early]
        + column_tiles(d_conv_in, model_width)
        + [d_w_out]
        + [jnp.stack([gain_zero, gain_one, gain_two, gain_three, bias_zero, bias_one, bias_two, bias_three])]
    )

    def grad_step(carry, pieces):
        d_unit, d_pos = carry
        key_block, value_block, table_block, clip_block = pieces
        probs = jnp.exp(scores_of(key_block, table_block, clip_block) - log_total[..., None])
        slope = jnp.einsum(
            "qhd,khd->hqk", d_attended, value_block, preferred_element_type=jnp.float32
        )
        d_raw = (probs * (slope - delta[..., None]) / math.sqrt(head_width)).astype(jnp.bfloat16)
        d_value = jnp.einsum(
            "hqk,qhd->khd",
            probs.astype(jnp.bfloat16),
            d_attended,
            preferred_element_type=jnp.float32,
        )
        d_key = jnp.einsum("hqk,qhd->khd", d_raw, query_unit, preferred_element_type=jnp.float32)
        d_unit = d_unit + jnp.einsum(
            "hqk,khd->qhd", d_raw, key_block, preferred_element_type=jnp.float32
        )
        d_pos = d_pos + jnp.einsum(
            "hqk,kc->qhc", d_raw, table_block, preferred_element_type=jnp.float32
        )
        return ((d_unit, d_pos), (d_key, d_value))

    start_grads = (
        jnp.zeros((frame_rows, head_count, head_width), jnp.float32),
        jnp.zeros((frame_rows, head_count, model_width), jnp.float32),
    )
    (d_unit, d_pos), (key_blocks, value_blocks) = lax.scan(grad_step, start_grads, key_pieces)
    d_pair = jnp.concatenate(
        [
            key_blocks.reshape(total_frames, model_width),
            value_blocks.reshape(total_frames, model_width),
        ],
        axis=1,
    ).astype(jnp.bfloat16)
    d_frames = times_transposed(d_pair, w_qkv[:, model_width:]).astype(jnp.bfloat16)
    from_pair = scatter_frames(d_frames.reshape(shard_count, frame_rows, model_width))
    d_w_pair = transposed_times(frames_all.reshape(total_frames, model_width), d_pair)
    d_shifted = jax.vjp(rotate_local, shifted)[1](d_pos)[0].astype(jnp.bfloat16)
    d_w_pos = jnp.einsum(
        "fhc,fhd->chd", d_shifted, query_shift, preferred_element_type=jnp.float32
    ).reshape(model_width, model_width)
    d_from_pos = jnp.einsum("fhc,chd->fhd", d_shifted, pos_grid, preferred_element_type=jnp.float32)
    d_rel = jnp.stack(
        [
            jnp.sum(d_unit, axis=0).reshape(model_width),
            jnp.sum(d_from_pos, axis=0).reshape(model_width),
        ]
    )
    d_query = (d_unit + d_from_pos).reshape(frame_rows, model_width)
    d_query = d_query.astype(jnp.bfloat16)
    d_w_query = transposed_times(input_low, d_query)
    input_grad = grad_first + times_transposed(d_query, w_qkv[:, :model_width]) + from_pair
    last_sums = sum_rows_everywhere(
        [d_w_query] + column_tiles(d_w_pair, model_width) + [d_w_pos, d_depth, d_rel]
    )
    tiles = ffn_in.shape[2] // model_width
    sum_in_late = jnp.concatenate(late_sums[:tiles], axis=1)
    sum_out_late, sum_conv_out = late_sums[tiles:]
    sum_in_early = jnp.concatenate(early_sums[:tiles], axis=1)
    sum_out_early = early_sums[tiles]
    sum_conv_in = jnp.concatenate(early_sums[tiles + 1 : tiles + 3], axis=1)
    sum_wout, sum_norms = early_sums[tiles + 3 :]
    sum_gain, sum_bias = sum_norms[:4], sum_norms[4:]
    sum_qkv = jnp.concatenate(last_sums[:3], axis=1)
    sum_pos, sum_depth, sum_rel = last_sums[3:]
    return (
        result[None],
        input_grad[None],
        sum_qkv,
        sum_pos,
        sum_wout,
        sum_rel,
        jnp.stack([sum_in_early, sum_in_late]),
        jnp.stack([sum_out_early, sum_out_late]),
        sum_conv_in,
        sum_depth,
        sum_conv_out,
        d_bn_gain,
        d_bn_bias,
        sum_gain,
        sum_bias,
    )


def solution(mesh):
    placed = (
        P("dp", "seq", None),
        P(),
        P(),
        P(),
        P(),
        P(),
        P(),
        P(),
        P(),
        P(),
        P(),
        P(),
        P(),
        P(),
        P("dp", None),
        P("dp", "seq", None),
    )
    return jax.shard_map(
        local,
        mesh=mesh,
        in_specs=placed,
        out_specs=(
            P("dp", "seq", None),
            P("dp", "seq", None),
            P(),
            P(),
            P(),
            P(),
            P(),
            P(),
            P(),
            P(),
            P(),
            P(),
            P(),
            P(),
            P(),
        ),
        check_vma=False,
    )
```

```python
import functools
import math

import jax
import jax.numpy as jnp
from jax import lax
from jax.experimental import pallas as pl
from jax.experimental.pallas import tpu as pltpu
from jax.sharding import PartitionSpec as P
import numpy as np

HEADS = 4
LANES = 128
WIDE = 3 * LANES
HALO = 16
EPS = 1e-05
MODEL_AXES = ("seq", "dp")
VMEM_BYTES = 56 * 1024 * 1024
BF16 = jnp.bfloat16
F32 = jnp.float32


def device_count():
    return lax.axis_size("seq") * lax.axis_size("dp")


def flat_index():
    return lax.axis_index("seq") * lax.axis_size("dp") + lax.axis_index("dp")


def swap_flat(block, distance):
    pairs = [(i, i ^ distance) for i in range(device_count())]
    return lax.ppermute(block, MODEL_AXES, pairs)


def swap_seq(block, distance):
    pairs = [(i, i ^ distance) for i in range(lax.axis_size("seq"))]
    return lax.ppermute(block, "seq", pairs)


def shift_seq(block, step):
    count = lax.axis_size("seq")
    pairs = [(i, i + step) for i in range(count) if 0 <= i + step < count]
    return lax.ppermute(block, "seq", pairs)


def stage_radices(devices):
    radices = [2]
    left = devices // 2
    while left > 1:
        radix = 4 if left % 4 == 0 else 2
        radices.append(radix)
        left = left // radix
    return radices


def slot_pieces(devices):
    slots = jnp.arange(devices, dtype=jnp.int32)
    distance = jnp.zeros((devices,), jnp.int32)
    span = devices
    stride = 1
    for radix in stage_radices(devices):
        span = span // radix
        distance = distance + ((slots // span) % radix) * stride
        stride = stride * radix
    return flat_index() ^ distance


def add_kernel(radix, *refs):
    parts = refs[: len(refs) - radix]
    outs = refs[len(refs) - radix :]
    total = parts[0][...].astype(F32)
    for part in parts[1:]:
        total = total + part[...].astype(F32)
    total = total.astype(BF16)
    span = outs[0].shape[0]
    for place, out in enumerate(outs):
        out[...] = total[place * span : (place + 1) * span]


def add_parts(parts, radix):
    shape = parts[0].shape
    piece = jax.ShapeDtypeStruct((shape[0] // radix,) + shape[1:], BF16)
    return call(
        functools.partial(add_kernel, radix), [piece] * radix, parts, flops=parts[0].size
    )


class SumStages:
    def __init__(self, keep, send):
        radices = stage_radices(device_count())
        strides = [1]
        for radix in radices[:-1]:
            strides.append(strides[-1] * radix)
        self.down = list(zip(radices[1:], strides[1:]))
        self.up = self.down[::-1]
        self.parts = [keep, swap_flat(send, 1)]
        self.held = None
        self.last = None

    def mark(self):
        return self.last

    def step(self, *earlier):
        parts = self.parts
        if earlier and parts is not None:
            parts = [after(parts[0], *earlier)] + parts[1:]
        if self.down:
            radix, stride = self.down.pop(0)
            pieces = add_parts(parts, radix)
            self.parts = [pieces[0]] + [
                swap_flat(pieces[step], step * stride) for step in range(radix - 1, 0, -1)
            ]
            self.last = pieces[0]
        elif self.parts is not None:
            self.held = add_parts(parts, 1)[0]
            self.parts = None
            self.last = self.held
            self.spread()
        elif self.up:
            self.collect(*earlier)
            self.spread()

    def spread(self):
        if self.up:
            radix, stride = self.up[0]
            self.arrived = [self.held] + [
                swap_flat(self.held, step * stride) for step in range(1, radix)
            ]
        else:
            self.other = swap_flat(self.held, 1)

    def collect(self, *earlier):
        self.up.pop(0)
        arrived = self.arrived
        if earlier:
            arrived = [after(arrived[0], *earlier)] + arrived[1:]
        self.held = jnp.concatenate(arrived, axis=0)
        self.last = self.held

    def finish(self):
        while self.down or self.parts is not None or self.up:
            self.step()
        return self.held, self.other


def exchange_small(spread):
    return lax.all_to_all(spread, MODEL_AXES, 0, 0)


def after(value, *earlier):
    return lax.optimization_barrier((value,) + earlier)[0]


def gather_frames(shard):
    count = lax.axis_size("seq")
    across = [shard] + [swap_seq(shard, 2 * step) for step in range(1, count // 2)]
    blocks = []
    for block in across:
        blocks.append(block)
        blocks.append(swap_seq(block, 1))
    return blocks


def scatter_frames(partials):
    count = lax.axis_size("seq")
    total = None
    for step in range(count // 2 - 1, -1, -1):
        joined = partials[2 * step].astype(F32) + swap_seq(partials[2 * step + 1], 1).astype(F32)
        if step > 0:
            joined = swap_seq(joined.astype(BF16), 2 * step).astype(F32)
        total = joined if total is None else total + joined
    return total


def call(body, outs, args, scratch=(), flops=0, smem=0):
    out_bytes = sum(math.prod(out.shape) * out.dtype.itemsize for out in outs)
    arg_bytes = sum(arg.size * arg.dtype.itemsize for arg in args)
    specs = [
        pl.BlockSpec(memory_space=pltpu.SMEM if place < smem else pltpu.VMEM)
        for place in range(len(args))
    ]
    return pl.pallas_call(
        body,
        out_shape=tuple(outs),
        in_specs=specs,
        out_specs=tuple(pl.BlockSpec(memory_space=pltpu.VMEM) for _ in outs),
        scratch_shapes=list(scratch),
        compiler_params=pltpu.CompilerParams(vmem_limit_bytes=VMEM_BYTES),
        cost_estimate=pl.CostEstimate(
            flops=int(flops), bytes_accessed=int(out_bytes + arg_bytes), transcendentals=0
        ),
    )(*args)


def struct(shape, dtype):
    return jax.ShapeDtypeStruct(tuple(shape), dtype)


def nn(left, right):
    return lax.dot_general(left, right, (((1,), (0,)), ((), ())), preferred_element_type=F32)


def nt(left, right):
    return lax.dot_general(left, right, (((1,), (1,)), ((), ())), preferred_element_type=F32)


def tn(left, right):
    return lax.dot_general(left, right, (((0,), (0,)), ((), ())), preferred_element_type=F32)


def norm_parts(summed):
    average = jnp.mean(summed, axis=-1, keepdims=True)
    centered = summed - average
    variance = jnp.mean(centered * centered, axis=-1, keepdims=True)
    inverse = lax.rsqrt(variance + EPS)
    return centered * inverse, inverse


def norm_back(unit, inverse, gain, incoming):
    scaled = incoming * gain
    first = jnp.mean(scaled, axis=-1, keepdims=True)
    second = jnp.mean(scaled * unit, axis=-1, keepdims=True)
    grad = inverse * (scaled - first - unit * second)
    return (
        grad,
        jnp.sum(incoming * unit, axis=0, keepdims=True),
        jnp.sum(incoming, axis=0, keepdims=True),
    )


def sigmoid(value):
    return 1.0 / (1.0 + jnp.exp(-value))


def silu_back(value):
    gate = sigmoid(value)
    return gate * (1.0 + value * (1.0 - gate))


def store_tile(ref, rows, copies):
    tile = jnp.zeros((8, LANES), F32)
    parts = []
    for row in rows:
        width = row.shape[1]
        blocks = -(-width // LANES)
        wide = row
        if blocks * LANES > width:
            wide = jnp.concatenate([row, jnp.zeros((1, blocks * LANES - width), F32)], axis=1)
        for block in range(blocks):
            parts.append(wide[:, block * LANES : (block + 1) * LANES])
    for place, part in enumerate(parts):
        tile = jnp.where(
            lax.broadcasted_iota(jnp.int32, (8, LANES), 0) == place,
            jnp.broadcast_to(part, (8, LANES)),
            tile,
        )
    ref[...] = jnp.broadcast_to(tile[None], (copies, 8, LANES))


def tile_row(tile, place, width):
    blocks = -(-width // LANES)
    parts = [tile[place * blocks + block : place * blocks + block + 1] for block in range(blocks)]
    return jnp.concatenate(parts, axis=1)[:, :width]


def spread_pieces(slots_ref, packed, keep_ref, send_ref):
    share = keep_ref.shape[1]
    half = keep_ref.shape[0]

    def one(slot, nothing):
        low = pl.multiple_of(slots_ref[slot] * share, HALO)
        keep_ref[slot] = packed[pl.ds(low, share), :]
        high = pl.multiple_of(slots_ref[slot + half] * share, HALO)
        send_ref[slot] = packed[pl.ds(high, share), :]
        return nothing

    lax.fori_loop(0, half, one, 0)


def collect_pieces(slots_ref, keep_ref, send_ref, packed):
    share = keep_ref.shape[1]
    half = keep_ref.shape[0]

    def one(slot, nothing):
        low = pl.multiple_of(slots_ref[slot] * share, HALO)
        packed[pl.ds(low, share), :] = keep_ref[slot]
        high = pl.multiple_of(slots_ref[slot + half] * share, HALO)
        packed[pl.ds(high, share), :] = send_ref[slot]
        return nothing

    lax.fori_loop(0, half, one, 0)


def share_rows(rows, devices):
    return -(-rows // (HALO * devices)) * HALO


def half_slots(rows, width, devices):
    share = share_rows(rows, devices)
    del width
    return [struct((devices // 2, share, WIDE), BF16)] * 2, pltpu.VMEM((devices * share, WIDE), BF16)


def wave_tables(rows, blocks, width):
    half = width // 2
    frequency = np.exp(np.arange(half) * (-2.0 * math.log(10000.0) / width))
    tail = np.zeros(LANES // 2)
    tail[: half - LANES] = frequency[LANES:]
    lanes = np.concatenate([frequency[:LANES], frequency[:LANES], tail, tail])[None]
    row_angles = np.arange(rows)[:, None] * lanes
    block_angles = (np.arange(blocks) * rows)[:, None] * lanes
    return [
        jnp.asarray(table.astype(np.float32))
        for table in (
            np.cos(row_angles),
            np.sin(row_angles),
            np.cos(block_angles),
            np.sin(block_angles),
        )
    ]


def half_pieces(width):
    half = width // 2
    rest = half - LANES
    return (
        (0, 0, LANES),
        (half, LANES, LANES),
        (LANES, 2 * LANES, rest),
        (half + LANES, 2 * LANES + LANES // 2, rest),
    )


def half_sign():
    lane = lax.broadcasted_iota(jnp.int32, (1, LANES), 1)
    return jnp.where(lane < LANES // 2, 1.0, -1.0)


def prepare_kernel(where, lengths, turned, w_qkv, w_pos, w_out, bias, depth, base_cos, base_sin, block_cos, block_sin, block, query, shift, w_query, w_pair, w_pos_wide, w_out_wide, depth_wide, table, own_cos, own_sin, clip_rows, clip_columns, clip_wide, valid_wide):
    place = where[0]
    width, rows = turned.shape
    size = width // HEADS
    blocks = block_cos.shape[0]
    w_query[...] = jnp.zeros_like(w_query)
    w_pair[...] = jnp.zeros_like(w_pair)
    w_pos_wide[...] = jnp.zeros_like(w_pos_wide)
    w_out_wide[...] = jnp.zeros_like(w_out_wide)
    depth_wide[...] = jnp.zeros_like(depth_wide)
    depth_wide[:, :width] = depth[...]
    for head in range(HEADS):
        natural = slice(head * size, (head + 1) * size)
        low = head * LANES
        w_query[:, low : low + size] = w_qkv[:, head * size : (head + 1) * size]
        w_pair[head, :, :size] = w_qkv[:, width + head * size : width + (head + 1) * size]
        w_pair[head, :, LANES : LANES + size] = w_qkv[
            :, 2 * width + head * size : 2 * width + (head + 1) * size
        ]
        w_out_wide[low : low + size] = w_out[natural]
        for source, target, length in half_pieces(width):
            w_pos_wide[target : target + length, low : low + size] = w_pos[
                source : source + length, natural
            ]
    lane = lax.broadcasted_iota(jnp.int32, (1, WIDE), 1)
    on_cosine = (lane < LANES) | ((lane >= 2 * LANES) & (lane < 2 * LANES + LANES // 2))
    row_cos, row_sin = base_cos[...], base_sin[...]
    ends = [lengths[0, 0]]
    for clip in range(1, lengths.shape[1]):
        ends.append(ends[-1] + lengths[0, clip])

    def clip_at(frames):
        clip = jnp.zeros_like(frames)
        for end in ends:
            clip = clip + (frames >= end).astype(jnp.int32)
        return clip

    for step in range(blocks):
        here = place ^ step
        cosine = block_cos[pl.ds(here, 1), :]
        sine = block_sin[pl.ds(here, 1), :]
        one = jnp.where(on_cosine, cosine, sine)
        two = jnp.where(on_cosine, -sine, cosine)
        table[:, step * rows : (step + 1) * rows] = (one * row_cos + two * row_sin).astype(BF16).T
        clip_columns[:, step * rows : (step + 1) * rows] = clip_at(
            here * rows + lax.broadcasted_iota(jnp.int32, (1, rows), 1)
        )
    reached = place * rows - HALO + lax.broadcasted_iota(jnp.int32, (rows + 2 * HALO, LANES), 0)
    inside = (reached >= 0) & (reached < blocks * rows)
    reached_clip = jnp.where(inside, clip_at(reached), -1)
    clip_wide[...] = reached_clip
    clip_rows[...] = reached_clip[HALO : HALO + rows, 0:1]
    valid_wide[...] = (inside & (reached < ends[-1])).astype(F32)[:, 0:1]
    block_cosine = block_cos[pl.ds(place, 1), :]
    block_sine = block_sin[pl.ds(place, 1), :]
    cosines = block_cosine * row_cos - block_sine * row_sin
    sines = block_sine * row_cos + block_cosine * row_sin
    own_cos[...] = cosines
    own_sin[...] = sines
    frames = turned[...].T
    block[...] = frames
    projected = nn(frames, w_query[...])
    sign = half_sign()
    for head in range(HEADS):
        lanes = slice(head * LANES, (head + 1) * LANES)
        natural = slice(head * size, (head + 1) * size)
        wide = jnp.zeros((2, LANES - size), F32)
        added = jnp.concatenate([bias[:, natural], wide], axis=1)
        unit = (projected[:, lanes] + added[0:1]).astype(BF16)
        moved = (projected[:, lanes] + added[1:2]).astype(BF16)
        shift[:, lanes] = moved
        shifted = nt(moved, w_pos_wide[:, lanes])
        first, second = shifted[:, :LANES], shifted[:, LANES : 2 * LANES]
        tail = shifted[:, 2 * LANES :]
        sine, cosine = sines[:, :LANES], cosines[:, :LANES]
        query[head, :, :LANES] = unit
        query[head, :, LANES : 2 * LANES] = (first * sine + second * cosine).astype(BF16)
        query[head, :, 2 * LANES : 3 * LANES] = (second * sine - first * cosine).astype(BF16)
        query[head, :, 3 * LANES :] = (
            tail * sines[:, 2 * LANES :]
            + pltpu.roll(tail, LANES // 2, 1) * cosines[:, 2 * LANES :] * sign
        ).astype(BF16)


def masked_scores(query, key, table, clip_rows, clip_columns, scale):
    upper = jnp.concatenate([key, table[:LANES]], axis=0)
    raw = nn(query[:, : 2 * LANES], upper) + nn(query[:, 2 * LANES :], table[LANES:])
    return jnp.where(clip_rows == clip_columns, raw * scale, -1e30)


def attend_kernel(scale, chunks, count, *refs):
    blocks = refs[:count]
    query, w_pair, table, clip_rows, clip_columns = refs[count : count + 5]
    attended, log_total, pair, frames_all, highest, total, summed = refs[count + 5 :]
    head = pl.program_id(0)
    chunk = pl.program_id(1)
    span = table.shape[1]
    rows = blocks[0].shape[1]

    @pl.when((chunk == 0) & (head == 0))
    def _():
        for step in range(count):
            frames_all[:, step * rows : (step + 1) * rows] = blocks[step][...]

    @pl.when(chunk == 0)
    def _():
        highest[...] = jnp.full_like(highest, -1e30)
        total[...] = jnp.zeros_like(total)
        summed[...] = jnp.zeros_like(summed)

    frames = frames_all[:, pl.ds(pl.multiple_of(chunk * span, LANES), span)]
    both = tn(w_pair[0], frames).astype(BF16)
    pair[0] = both
    scores = masked_scores(
        query[0], both[:LANES], table[...], clip_rows[...], clip_columns[...], scale
    )
    old = highest[...]
    new = jnp.maximum(old, jnp.max(scores, axis=1, keepdims=True))
    weights = jnp.exp(scores - new)
    fade = jnp.exp(old - new)
    highest[...] = new
    total[...] = total[...] * fade + jnp.sum(weights, axis=1, keepdims=True)
    summed[...] = summed[...] * fade + nt(weights.astype(BF16), both[LANES:])

    @pl.when(chunk == chunks - 1)
    def _():
        attended[...] = summed[...] / total[...]
        log_total[0] = highest[...] + jnp.log(total[...])


def attend(blocks, query, w_pair, table, clip_rows, clip_columns, head_width):
    rows = query.shape[1]
    frames = table.shape[1]
    width = w_pair.shape[1]
    span = min(frames, 2048)
    chunks = frames // span
    return pl.pallas_call(
        functools.partial(attend_kernel, 1.0 / math.sqrt(head_width), chunks, len(blocks)),
        grid=(HEADS, chunks),
        in_specs=[pl.BlockSpec((width, rows), lambda h, c: (0, 0)) for _ in blocks]
        + [
            pl.BlockSpec((1, rows, 4 * LANES), lambda h, c: (h, 0, 0)),
            pl.BlockSpec((1, width, 2 * LANES), lambda h, c: (h, 0, 0)),
            pl.BlockSpec((WIDE, span), lambda h, c: (0, c)),
            pl.BlockSpec((rows, 1), lambda h, c: (0, 0)),
            pl.BlockSpec((1, span), lambda h, c: (0, c)),
        ],
        out_specs=(
            pl.BlockSpec((rows, LANES), lambda h, c: (0, h)),
            pl.BlockSpec((1, rows, 1), lambda h, c: (h, 0, 0)),
            pl.BlockSpec((1, 2 * LANES, span), lambda h, c: (h, 0, c)),
        ),
        out_shape=(
            struct((rows, HEADS * LANES), F32),
            struct((HEADS, rows, 1), F32),
            struct((HEADS, 2 * LANES, frames), BF16),
        ),
        scratch_shapes=[
            pltpu.VMEM((width, frames), BF16),
            pltpu.VMEM((rows, 1), F32),
            pltpu.VMEM((rows, 1), F32),
            pltpu.VMEM((rows, LANES), F32),
        ],
        compiler_params=pltpu.CompilerParams(vmem_limit_bytes=VMEM_BYTES),
        cost_estimate=pl.CostEstimate(
            flops=2 * HEADS * rows * frames * 960, bytes_accessed=frames * 4096, transcendentals=0
        ),
    )(*blocks, query, w_pair, table, clip_rows, clip_columns)


def early_kernel(block, attended, w_out, gains, biases, ffn_in, ffn_out, gates, first_sum, second_sum, second_norm, left, right, gated, attended_low):
    low = attended[...].astype(BF16)
    attended_low[...] = low
    summed = block[...].astype(F32) + nn(low, w_out[...])
    first_sum[...] = summed
    unit, _ = norm_parts(summed)
    first = unit * gains[0:1] + biases[0:1]
    inner = nn(first.astype(BF16), ffn_in[...])
    act = (inner * sigmoid(inner)).astype(BF16)
    summed = first + nt(act, ffn_out[...])
    second_sum[...] = summed
    unit, _ = norm_parts(summed)
    second = unit * gains[1:2] + biases[1:2]
    second_norm[...] = second
    second_low = second.astype(BF16)
    half = gates.shape[0] // 2
    one = nt(second_low, gates[:half])
    two = nt(second_low, gates[half:])
    left[...] = one
    right[...] = two
    gated[...] = jnp.zeros_like(gated)
    gated[:, : one.shape[1]] = (one * sigmoid(two)).astype(BF16)


def conv_kernel(copies, low, middle, high, clip, depth, valid, convolved, tile, extended):
    rows = middle.shape[0]
    width = convolved.shape[1]
    reach = depth.shape[0] // 2
    extended[0:HALO] = low[...].astype(F32)
    extended[HALO : HALO + rows] = middle[...].astype(F32)
    extended[HALO + rows :] = high[...].astype(F32)
    step = 64
    for start in range(0, rows, step):
        own = clip[HALO + start : HALO + start + step]
        sums = [jnp.zeros((step, LANES), F32) for _ in range(3)]
        for tap in range(2 * reach + 1):
            place = HALO - reach + tap + start
            same = clip[place : place + step] == own
            for block in range(3):
                lanes = slice(block * LANES, (block + 1) * LANES)
                sums[block] = sums[block] + depth[tap : tap + 1, lanes] * jnp.where(
                    same, extended[place : place + step, lanes], 0.0
                )
        convolved[start : start + step] = jnp.concatenate(sums, axis=1)[:, :width]
    value = convolved[...]
    kept = value * valid[...]
    count = jnp.zeros((1, width), F32) + jnp.sum(valid[...], axis=0, keepdims=True)
    store_tile(
        tile,
        [
            jnp.sum(kept, axis=0, keepdims=True),
            jnp.sum(kept * value, axis=0, keepdims=True),
            count[:, :LANES],
        ],
        copies,
    )


def late_kernel(copies, arrived, convolved, second_norm, bn_gain, bn_bias, conv_out, gains, biases, ffn_in, ffn_out, cotangent, result, act_out, d_inner_out, third_low_out, fourth_grad_out, swished_out, third_grad_out, third_grad, d_normed_out, unit_out, tile, norm_grads, statistics, edge_low, edge_high):
    width = convolved.shape[1]
    rows = convolved.shape[0]
    sums = jnp.sum(arrived[...], axis=0)
    frames = sums[6:7, 0:1]
    mean = tile_row(sums, 0, width) / frames
    variance = tile_row(sums, 1, width) / frames - mean * mean
    inverse = lax.rsqrt(variance + EPS)
    unit = (convolved[...] - mean) * inverse
    unit_out[...] = unit
    statistics[...] = jnp.zeros_like(statistics)
    statistics[0:1, :width] = inverse
    statistics[1:2, :width] = jnp.broadcast_to(frames, (1, width))
    normed = unit * bn_gain[...] + bn_bias[...]
    swished = (normed * sigmoid(normed)).astype(BF16)
    swished_out[...] = swished
    third_unit, third_inverse = norm_parts(second_norm[...] + nn(swished, conv_out[...]))
    third = third_unit * gains[2:3] + biases[2:3]
    third_low = third.astype(BF16)
    third_low_out[...] = third_low
    inner = nn(third_low, ffn_in[...])
    gate = sigmoid(inner)
    act = (inner * gate).astype(BF16)
    act_out[...] = act
    fourth_unit, fourth_inverse = norm_parts(third + nt(act, ffn_out[...]))
    result[...] = (fourth_unit * gains[3:4] + biases[3:4]).T
    fourth_grad, gain_three, bias_three = norm_back(
        fourth_unit, fourth_inverse, gains[3:4], cotangent[...].T
    )
    fourth_low = fourth_grad.astype(BF16)
    fourth_grad_out[...] = fourth_low
    d_act = nn(fourth_low, ffn_out[...])
    d_inner = (d_act * (gate * (1.0 + inner * (1.0 - gate)))).astype(BF16)
    d_inner_out[...] = d_inner
    grad, gain_two, bias_two = norm_back(
        third_unit, third_inverse, gains[2:3], fourth_grad + nt(d_inner, ffn_in[...])
    )
    third_grad[...] = grad
    grad_low = grad.astype(BF16)
    third_grad_out[...] = grad_low
    d_normed = nt(grad_low, conv_out[...]) * silu_back(normed)
    d_normed_out[...] = d_normed
    store_tile(
        tile,
        [
            jnp.sum(d_normed * unit, axis=0, keepdims=True),
            jnp.sum(d_normed, axis=0, keepdims=True),
        ],
        copies,
    )
    norm_grads[0:1] = gain_two
    norm_grads[1:2] = gain_three
    norm_grads[2:3] = bias_two
    norm_grads[3:4] = bias_three
    edge_low[0] = d_normed[:HALO]
    edge_low[1] = unit[:HALO]
    edge_high[0] = d_normed[rows - HALO :]
    edge_high[1] = unit[rows - HALO :]


def store_column_tiles(packed, start, value, width):
    rows = value.shape[0]
    for place in range(value.shape[1] // width):
        packed[start : start + rows, :width] = value[
            :, place * width : (place + 1) * width
        ].astype(BF16)
        start = start + rows
    return start


def late_grads_kernel(slots, third_low, d_inner, act, fourth_grad, swished, third_grad, keep, send, packed):
    width = third_low.shape[1]
    packed[...] = jnp.zeros_like(packed)
    start = store_column_tiles(packed, 0, tn(third_low[...], d_inner[...]), width)
    start = store_column_tiles(packed, start, tn(fourth_grad[...], act[...]), width)
    store_column_tiles(packed, start, tn(swished[...], third_grad[...]), width)
    spread_pieces(slots, packed, keep, send)


def middle_kernel(arrived, statistics, bn_gain, bn_bias, d_normed, unit, from_low, from_high, clip, valid, depth, gated_low, gated, gated_high, left, right, gates, third_grad, second_sum, first_sum, gains, biases, ffn_in, ffn_out, w_out, attended, first_grad, d_attended, delta, act_out, d_inner_out, first_low_out, second_grad_out, d_left_out, d_right_out, second_low_out, first_grad_out, norm_grads, d_depth, bn_grads, d_conv_wide, gated_wide):
    rows, width = left.shape
    reach = depth.shape[0] // 2
    sums = jnp.sum(arrived[...], axis=0)
    gain_sum = tile_row(sums, 0, width)
    bias_sum = tile_row(sums, 1, width)
    bn_grads[0:1] = gain_sum
    bn_grads[1:2] = bias_sum
    gain = bn_gain[...]
    sum_scaled = bias_sum * gain
    sum_product = gain_sum * gain
    inverse = statistics[0:1, :width]
    frames = statistics[1:2, :width]

    def conv_grad(d_rows, unit_rows, valid_rows):
        return (
            inverse
            * (d_rows * gain - valid_rows * (sum_scaled + unit_rows * sum_product) / frames)
        ).astype(BF16).astype(F32)

    d_conv_wide[...] = jnp.zeros_like(d_conv_wide)
    d_conv_wide[0:HALO, :width] = conv_grad(from_low[0], from_low[1], valid[0:HALO])
    d_conv_wide[HALO : HALO + rows, :width] = conv_grad(
        d_normed[...], unit[...], valid[HALO : HALO + rows]
    )
    d_conv_wide[HALO + rows :, :width] = conv_grad(
        from_high[0], from_high[1], valid[HALO + rows :]
    )
    gated_wide[0:HALO] = gated_low[...].astype(F32)
    gated_wide[HALO : HALO + rows] = gated[...].astype(F32)
    gated_wide[HALO + rows :] = gated_high[...].astype(F32)
    step = 64
    d_gated_parts = []
    depth_sums = [[jnp.zeros((8, LANES), F32) for _ in range(3)] for _ in range(2 * reach + 1)]
    for start in range(0, rows, step):
        own = clip[HALO + start : HALO + start + step]
        sums3 = [jnp.zeros((step, LANES), F32) for _ in range(3)]
        here = [
            d_conv_wide[HALO + start : HALO + start + step, block * LANES : (block + 1) * LANES]
            for block in range(3)
        ]
        for tap in range(2 * reach + 1):
            place = HALO - reach + tap + start
            same = clip[place : place + step] == own
            mirror = 2 * reach - tap
            for block in range(3):
                lanes = slice(block * LANES, (block + 1) * LANES)
                sums3[block] = sums3[block] + depth[mirror : mirror + 1, lanes] * jnp.where(
                    same, d_conv_wide[place : place + step, lanes], 0.0
                )
                product = jnp.where(same, gated_wide[place : place + step, lanes], 0.0) * here[block]
                depth_sums[tap][block] = depth_sums[tap][block] + jnp.sum(
                    product.reshape(step // 8, 8, LANES), axis=0
                )
        d_gated_parts.append(jnp.concatenate(sums3, axis=1)[:, :width])
    d_depth[...] = jnp.zeros_like(d_depth)
    for tap in range(2 * reach + 1):
        d_depth[tap : tap + 1] = jnp.concatenate(
            [jnp.sum(part, axis=0, keepdims=True) for part in depth_sums[tap]], axis=1
        )[:, :width]
    d_gated = jnp.concatenate(d_gated_parts, axis=0)
    gate = sigmoid(right[...])
    d_left = (d_gated * gate).astype(BF16)
    d_right = (d_gated * left[...] * gate * (1.0 - gate)).astype(BF16)
    d_left_out[...] = d_left
    d_right_out[...] = d_right
    second_unit, second_inverse = norm_parts(second_sum[...])
    second_low_out[...] = (second_unit * gains[1:2] + biases[1:2]).astype(BF16)
    half = gates.shape[0] // 2
    incoming = third_grad[...] + nn(d_left, gates[:half]) + nn(d_right, gates[half:])
    second_grad, gain_one, bias_one = norm_back(
        second_unit, second_inverse, gains[1:2], incoming
    )
    second_grad_low = second_grad.astype(BF16)
    second_grad_out[...] = second_grad_low
    first_unit, first_inverse = norm_parts(first_sum[...])
    first_low = (first_unit * gains[0:1] + biases[0:1]).astype(BF16)
    first_low_out[...] = first_low
    inner = nn(first_low, ffn_in[...])
    inner_gate = sigmoid(inner)
    act_out[...] = (inner * inner_gate).astype(BF16)
    d_act = nn(second_grad_low, ffn_out[...])
    d_inner = (d_act * (inner_gate * (1.0 + inner * (1.0 - inner_gate)))).astype(BF16)
    d_inner_out[...] = d_inner
    grad, gain_zero, bias_zero = norm_back(
        first_unit, first_inverse, gains[0:1], second_grad + nt(d_inner, ffn_in[...])
    )
    first_grad[...] = grad
    grad_low = grad.astype(BF16)
    first_grad_out[...] = grad_low
    norm_grads[0:1] = gain_zero
    norm_grads[1:2] = gain_one
    norm_grads[2:3] = bias_zero
    norm_grads[3:4] = bias_one
    back = nt(grad_low, w_out[...]).astype(BF16)
    d_attended[...] = back
    product = back.astype(F32) * attended[...]
    for head in range(HEADS):
        delta[head] = jnp.sum(
            product[:, head * LANES : (head + 1) * LANES], axis=1, keepdims=True
        )


def early_grads_kernel(slots, first_low, d_inner, act, second_grad, second_low, d_left, d_right, attended_low, first_grad, keep, send, packed):
    width = first_low.shape[1]
    packed[...] = jnp.zeros_like(packed)
    start = store_column_tiles(packed, 0, tn(first_low[...], d_inner[...]), width)
    start = store_column_tiles(packed, start, tn(second_grad[...], act[...]), width)
    start = store_column_tiles(packed, start, tn(d_left[...], second_low[...]), width)
    start = store_column_tiles(packed, start, tn(d_right[...], second_low[...]), width)
    d_out = tn(attended_low[...], first_grad[...]).astype(BF16)
    for head in range(HEADS):
        size = width // HEADS
        packed[start : start + size, :width] = d_out[head * LANES : head * LANES + size]
        start = start + size
    spread_pieces(slots, packed, keep, send)


def attend_back_kernel(scale, chunks, query, pair, table, clip_rows, clip_columns, log_total, delta, d_attended, shift, w_pos, own_cos, own_sin, d_pair, d_query, d_pos_weight, d_bias, unit_sum, rest_sum):
    chunk = pl.program_id(1)
    key = pair[0, :LANES]
    scores = masked_scores(
        query[0], key, table[...], clip_rows[...], clip_columns[...], scale
    )
    probs = jnp.exp(scores - log_total[0])
    slope = nn(d_attended[...], pair[0, LANES:])
    d_raw = (probs * (slope - delta[0]) * scale).astype(BF16)
    d_pair[0, :, :LANES] = tn(d_raw, query[0, :, :LANES]).astype(BF16)
    d_pair[0, :, LANES:] = tn(probs.astype(BF16), d_attended[...]).astype(BF16)

    @pl.when(chunk == 0)
    def _():
        unit_sum[...] = jnp.zeros_like(unit_sum)
        rest_sum[...] = jnp.zeros_like(rest_sum)

    unit_sum[...] += nt(d_raw, jnp.concatenate([key, table[:LANES]], axis=0))
    rest_sum[...] += nt(d_raw, table[LANES:])

    @pl.when(chunk == chunks - 1)
    def _():
        d_unit = unit_sum[:, :LANES]
        first, second = unit_sum[:, LANES:], rest_sum[:, :LANES]
        tail = rest_sum[:, LANES:]
        cosines, sines = own_cos[...], own_sin[...]
        sine, cosine = sines[:, :LANES], cosines[:, :LANES]
        d_shifted = jnp.concatenate(
            [
                first * sine - second * cosine,
                first * cosine + second * sine,
                tail * sines[:, 2 * LANES :]
                - pltpu.roll(tail, LANES // 2, 1) * cosines[:, 2 * LANES :] * half_sign(),
            ],
            axis=1,
        ).astype(BF16)
        d_from_pos = nn(d_shifted, w_pos[...])
        d_query[...] = (d_unit + d_from_pos).astype(BF16)
        d_pos_weight[...] = tn(d_shifted, shift[...]).astype(BF16)
        d_bias[0:1] = jnp.sum(d_unit, axis=0, keepdims=True)
        d_bias[1:2] = jnp.sum(d_from_pos, axis=0, keepdims=True)


def attend_back(first, heads, query, pair, table, clip_rows, clip_columns, log_total, delta, d_attended, shift, w_pos, own_cos, own_sin, head_width):
    rows = query.shape[1]
    frames = table.shape[1]
    span = min(frames, 2048)
    chunks = frames // span
    wide = heads * LANES
    return pl.pallas_call(
        functools.partial(attend_back_kernel, 1.0 / math.sqrt(head_width), chunks),
        grid=(heads, chunks),
        in_specs=[
            pl.BlockSpec((1, rows, 4 * LANES), lambda h, c: (h + first, 0, 0)),
            pl.BlockSpec((1, 2 * LANES, span), lambda h, c: (h + first, 0, c)),
            pl.BlockSpec((WIDE, span), lambda h, c: (0, c)),
            pl.BlockSpec((rows, 1), lambda h, c: (0, 0)),
            pl.BlockSpec((1, span), lambda h, c: (0, c)),
            pl.BlockSpec((1, rows, 1), lambda h, c: (h + first, 0, 0)),
            pl.BlockSpec((1, rows, 1), lambda h, c: (h + first, 0, 0)),
            pl.BlockSpec((rows, LANES), lambda h, c: (0, h + first)),
            pl.BlockSpec((rows, LANES), lambda h, c: (0, h + first)),
            pl.BlockSpec((WIDE, LANES), lambda h, c: (0, h + first)),
            pl.BlockSpec((rows, WIDE), lambda h, c: (0, 0)),
            pl.BlockSpec((rows, WIDE), lambda h, c: (0, 0)),
        ],
        out_specs=(
            pl.BlockSpec((1, span, 2 * LANES), lambda h, c: (h, c, 0)),
            pl.BlockSpec((rows, LANES), lambda h, c: (0, h)),
            pl.BlockSpec((WIDE, LANES), lambda h, c: (0, h)),
            pl.BlockSpec((2, LANES), lambda h, c: (0, h)),
        ),
        out_shape=(
            struct((heads, frames, 2 * LANES), BF16),
            struct((rows, wide), BF16),
            struct((WIDE, wide), BF16),
            struct((2, wide), F32),
        ),
        scratch_shapes=[pltpu.VMEM((rows, 2 * LANES), F32), pltpu.VMEM((rows, 2 * LANES), F32)],
        compiler_params=pltpu.CompilerParams(vmem_limit_bytes=VMEM_BYTES),
        cost_estimate=pl.CostEstimate(
            flops=2 * heads * rows * frames * 1408, bytes_accessed=frames * 3072, transcendentals=0
        ),
    )(query, pair, table, clip_rows, clip_columns, log_total, delta, d_attended, shift, w_pos, own_cos, own_sin)


def frames_back_kernel(parts, count, *refs):
    d_pairs = refs[:parts]
    w_pair = refs[parts]
    blocks = refs[parts + 1 : parts + 1 + count]
    d_frames = refs[parts + 1 + count : parts + 1 + 2 * count]
    d_weight = refs[parts + 1 + 2 * count]
    rows = blocks[0].shape[1]
    each = HEADS // parts
    for step in range(count):
        here = slice(step * rows, (step + 1) * rows)
        frames = blocks[step][...]
        total = None
        for head in range(HEADS):
            part = d_pairs[head // each][head % each, here]
            term = nt(w_pair[head], part)
            total = term if total is None else total + term
            grad = nn(frames, part)
            if step == 0:
                d_weight[head] = grad
            else:
                d_weight[head] += grad
        d_frames[step][...] = total.astype(BF16)


def frames_back(d_pairs, w_pair, blocks):
    width, rows = blocks[0].shape
    frames = rows * len(blocks)
    return call(
        functools.partial(frames_back_kernel, len(d_pairs), len(blocks)),
        [struct((width, rows), BF16)] * len(blocks) + [struct((HEADS, width, 2 * LANES), F32)],
        list(d_pairs) + [w_pair] + list(blocks),
        flops=4 * frames * width * 1024,
    )


def last_grads_kernel(slots, turned, d_query_one, d_query_two, w_query, d_pair_weight, d_pos_one, d_pos_two, d_bias_one, d_bias_two, d_depth, late_norms, early_norms, first_grad, keep, send, own_grad, packed):
    width = turned.shape[0]
    size = width // HEADS
    each = HEADS // 2
    half_wide = each * LANES
    grad = first_grad[...] + nt(d_query_one[...], w_query[:, :half_wide])
    own_grad[...] = (grad + nt(d_query_two[...], w_query[:, half_wide:])).T
    packed[...] = jnp.zeros_like(packed)
    for head in range(HEADS):
        lanes = slice(head * size, (head + 1) * size)
        low = (head % each) * LANES
        d_query = (d_query_one, d_query_two)[head // each]
        d_pos = (d_pos_one, d_pos_two)[head // each]
        d_bias = (d_bias_one, d_bias_two)[head // each]
        d_weight = nn(turned[...], d_query[:, low : low + LANES]).astype(BF16)
        packed[0:width, lanes] = d_weight[:, :size]
        packed[width : 2 * width, lanes] = d_pair_weight[head, :, :size].astype(BF16)
        packed[2 * width : 3 * width, lanes] = d_pair_weight[head, :, LANES : LANES + size].astype(
            BF16
        )
        for natural, spread, length in half_pieces(width):
            packed[3 * width + natural : 3 * width + natural + length, lanes] = d_pos[
                spread : spread + length, low : low + size
            ]
        packed[4 * width : 4 * width + 2, lanes] = d_bias[:, low : low + size].astype(BF16)
    start = 4 * width + 2
    packed[start : start + 4, :width] = early_norms[...].astype(BF16)
    packed[start + 4 : start + 8, :width] = late_norms[...].astype(BF16)
    taps = d_depth.shape[0]
    packed[start + 8 : start + 8 + taps, :width] = d_depth[...].astype(BF16)
    spread_pieces(slots, packed, keep, send)


def finish_two_kernel(slots, late_keep, late_send, early_keep, early_send, in_early, in_late, out_early, out_late, conv_in, conv_out, w_out, late, early):
    width, inner = in_early.shape
    tiles = inner // width
    collect_pieces(slots, late_keep, late_send, late)
    collect_pieces(slots, early_keep, early_send, early)
    for packed, ffn_in, ffn_out in ((early, in_early, out_early), (late, in_late, out_late)):
        for tile in range(tiles):
            lanes = slice(tile * width, (tile + 1) * width)
            ffn_in[:, lanes] = packed[tile * width : (tile + 1) * width, :width].astype(F32)
            ffn_out[:, lanes] = packed[
                inner + tile * width : inner + (tile + 1) * width, :width
            ].astype(F32)
    start = 2 * inner
    conv_out[...] = late[start : start + width, :width].astype(F32)
    conv_in[...] = early[start : start + 2 * width, :width].astype(F32)
    start = start + 2 * width
    w_out[...] = early[start : start + width, :width].astype(F32)


def finish_last_kernel(slots, keep, send, w_qkv, w_pos, d_bias, gains, biases, d_depth, packed):
    width = w_pos.shape[1]
    collect_pieces(slots, keep, send, packed)
    for tile in range(3):
        w_qkv[:, tile * width : (tile + 1) * width] = packed[
            tile * width : (tile + 1) * width, :width
        ].astype(F32)
    start = 3 * width
    w_pos[...] = packed[start : start + width, :width].astype(F32)
    start = start + width
    small = packed[start : start + 48, :width].astype(F32)
    d_bias[...] = small[0:2]
    gains[0:2] = small[2:4]
    biases[0:2] = small[4:6]
    gains[2:4] = small[6:8]
    biases[2:4] = small[8:10]
    taps = d_depth.shape[0]
    d_depth[...] = small[10 : 10 + taps]


def local(inputs, w_qkv, w_pos, w_out, rel_bias, ffn_in, ffn_out, conv_in, conv_depth, conv_out, bn_gain, bn_bias, norm_gain, norm_bias, lengths, cotangent):
    _, rows, width = inputs.shape
    inner = ffn_in.shape[2]
    taps = conv_depth.shape[0]
    head_width = width // HEADS
    seq_count = lax.axis_size("seq")
    devices = device_count()
    slots = slot_pieces(devices)
    place = lax.axis_index("seq").astype(jnp.int32).reshape(1)
    total = seq_count * rows

    turned = inputs[0].T
    blocks = gather_frames(turned)
    in_both = ffn_in.transpose(1, 0, 2)
    in_early, in_late = in_both[:, 0], in_both[:, 1]
    out_both = ffn_out.transpose(2, 0, 1)
    out_early, out_late = out_both[:, 0], out_both[:, 1]
    gates = conv_in.T
    cotangent_turned = cotangent[0].T
    bn_gain_row, bn_bias_row = bn_gain[None], bn_bias[None]

    model = struct((rows, width), F32)
    model_low = struct((rows, width), BF16)
    inner_low = struct((rows, inner), BF16)
    head_low = struct((rows, HEADS * LANES), BF16)
    tile = struct((devices, 8, LANES), F32)
    reached = rows + 2 * HALO
    (
        block,
        query,
        shift,
        w_query,
        w_pair,
        w_pos_wide,
        w_out_wide,
        depth_wide,
        table,
        own_cos,
        own_sin,
        clip_rows,
        clip_columns,
        clip_wide,
        valid_wide,
    ) = call(
        prepare_kernel,
        [
            model_low,
            struct((HEADS, rows, 4 * LANES), BF16),
            head_low,
            struct((width, HEADS * LANES), BF16),
            struct((HEADS, width, 2 * LANES), BF16),
            struct((WIDE, HEADS * LANES), BF16),
            struct((HEADS * LANES, width), BF16),
            struct((taps, WIDE), F32),
            struct((WIDE, total), BF16),
            struct((rows, WIDE), F32),
            struct((rows, WIDE), F32),
            struct((rows, 1), jnp.int32),
            struct((1, total), jnp.int32),
            struct((reached, LANES), jnp.int32),
            struct((reached, 1), F32),
        ],
        [place, lengths, turned, w_qkv, w_pos, w_out, rel_bias, conv_depth]
        + wave_tables(rows, seq_count, width),
        flops=2 * rows * (width * 512 + 512 * WIDE),
        smem=2,
    )
    valid_rows = valid_wide[HALO : HALO + rows]
    attended, log_total, pair = attend(
        blocks, query, w_pair, table, clip_rows, clip_columns, head_width
    )
    first_sum, second_sum, second_norm, left, right, gated, attended_low = call(
        early_kernel,
        [model, model, model, model, model, struct((rows, WIDE), BF16), head_low],
        [block, attended, w_out_wide, norm_gain, norm_bias, in_early, out_early, gates],
        flops=2 * rows * width * (512 + 2 * inner + 2 * width),
    )
    gated_low = shift_seq(gated[rows - HALO :], 1)
    gated_high = shift_seq(gated[:HALO], -1)
    convolved, spread = call(
        functools.partial(conv_kernel, devices),
        [model, tile],
        [gated_low, gated, gated_high, clip_wide, depth_wide, valid_rows],
        scratch=[pltpu.VMEM((reached, WIDE), F32)],
        flops=rows * WIDE * taps * 8,
    )
    arrived = exchange_small(spread)
    edge = struct((2, HALO, width), F32)
    (
        result,
        act_late,
        d_inner_late,
        third_low,
        fourth_grad,
        swished,
        third_grad_low,
        third_grad,
        d_normed,
        unit,
        spread,
        late_norms,
        statistics,
        edge_low,
        edge_high,
    ) = call(
        functools.partial(late_kernel, devices),
        [struct((width, rows), F32), inner_low, inner_low, model_low, model_low, model_low]
        + [model_low, model, model, model]
        + [tile, struct((4, width), F32), struct((8, WIDE), F32), edge, edge],
        [arrived, convolved, second_norm, bn_gain_row, bn_bias_row, conv_out, norm_gain, norm_bias]
        + [in_late, out_late, cotangent_turned],
        flops=2 * rows * width * (2 * width + 4 * inner),
    )
    from_low = shift_seq(edge_high, 1)
    from_high = shift_seq(edge_low, -1)
    arrived = exchange_small(spread)
    late_rows = 2 * inner + width
    outs, packed = half_slots(late_rows, width, devices)
    late_keep, late_send = call(
        late_grads_kernel,
        outs,
        [slots, third_low, d_inner_late, act_late, fourth_grad, swished, third_grad_low],
        scratch=[packed],
        flops=2 * rows * width * late_rows,
        smem=1,
    )
    late_sum = SumStages(late_keep, late_send)
    stat = struct((HEADS, rows, 1), F32)
    (
        first_grad,
        d_attended,
        delta,
        act_early,
        d_inner_early,
        first_low,
        second_grad,
        d_left,
        d_right,
        second_low,
        first_grad_low,
        early_norms,
        d_depth,
        bn_grads,
    ) = call(
        middle_kernel,
        [model, head_low, stat, inner_low, inner_low, model_low, model_low, model_low, model_low]
        + [model_low, model_low, struct((4, width), F32), struct((taps, width), F32)]
        + [struct((2, width), F32)],
        [after(arrived, late_keep), statistics, bn_gain_row, bn_bias_row, d_normed, unit]
        + [from_low, from_high]
        + [clip_wide, valid_wide, depth_wide, gated_low, gated, gated_high, left, right]
        + [gates, third_grad, second_sum, first_sum, norm_gain, norm_bias]
        + [in_early, out_early, w_out_wide, attended],
        scratch=[pltpu.VMEM((reached, WIDE), F32)] * 2,
        flops=2 * rows * width * (2 * width + 3 * inner) + rows * WIDE * taps * 16,
    )
    late_sum.step(first_grad)
    early_rows = 2 * inner + 3 * width
    outs, packed = half_slots(early_rows, width, devices)
    early_keep, early_send = call(
        early_grads_kernel,
        outs,
        [slots, after(first_low, late_sum.mark()), d_inner_early, act_early, second_grad]
        + [second_low, d_left, d_right, attended_low, first_grad_low],
        scratch=[packed],
        flops=2 * rows * width * early_rows,
        smem=1,
    )
    early_sum = SumStages(early_keep, early_send)
    late_sum.step(early_keep)

    def back(first, query):
        return attend_back(
            first, HEADS // 2, query, pair, table, clip_rows, clip_columns, log_total, delta,
            d_attended, shift, w_pos_wide, own_cos, own_sin, head_width,
        )

    d_pair_one, d_query_one, d_pos_one, d_bias_one = back(
        0, after(query, early_keep, late_sum.mark())
    )
    late_sum.step(d_query_one)
    early_sum.step(d_query_one)
    d_pair_two, d_query_two, d_pos_two, d_bias_two = back(
        HEADS // 2, after(query, d_query_one, late_sum.mark(), early_sum.mark())
    )
    late_sum.step(d_query_two)
    early_sum.step(d_query_two)
    *d_frames, d_pair_weight = frames_back(
        [after(d_pair_one, late_sum.mark(), early_sum.mark()), d_pair_two], w_pair, blocks
    )
    last_rows = 4 * width + 10 + taps
    outs, packed = half_slots(last_rows, width, devices)
    last_keep, last_send, own_grad = call(
        last_grads_kernel,
        outs + [struct((width, rows), F32)],
        [slots, turned, d_query_one, d_query_two, w_query, d_pair_weight, d_pos_one, d_pos_two]
        + [d_bias_one, d_bias_two, d_depth, late_norms, early_norms, first_grad],
        scratch=[packed],
        flops=2 * rows * width * 1024,
        smem=1,
    )
    last_sum = SumStages(last_keep, last_send)
    input_grad = own_grad + scatter_frames(d_frames)
    late_keep, late_send = late_sum.finish()
    early_keep, early_send = early_sum.finish()
    last_keep, last_send = last_sum.finish()

    late_share = share_rows(late_rows, devices) * devices
    early_share = share_rows(early_rows, devices) * devices
    last_share = share_rows(last_rows, devices) * devices
    ffn_shape = struct((width, inner), F32)
    square = struct((width, width), F32)
    (
        sum_in_early,
        sum_in_late,
        sum_out_early,
        sum_out_late,
        sum_conv_in,
        sum_conv_out,
        sum_w_out,
    ) = call(
        finish_two_kernel,
        [ffn_shape] * 4 + [struct((2 * width, width), F32), square, square],
        [slots, late_keep, late_send, early_keep, early_send],
        scratch=[pltpu.VMEM((late_share, WIDE), BF16), pltpu.VMEM((early_share, WIDE), BF16)],
        smem=1,
    )
    sum_qkv, sum_pos, sum_rel, sum_gain, sum_bias, sum_depth = call(
        finish_last_kernel,
        [struct(w_qkv.shape, F32), struct(w_pos.shape, F32), struct(rel_bias.shape, F32)]
        + [struct(norm_gain.shape, F32), struct(norm_bias.shape, F32)]
        + [struct(conv_depth.shape, F32)],
        [slots, last_keep, last_send],
        scratch=[pltpu.VMEM((last_share, WIDE), BF16)],
        smem=1,
    )
    return (
        result.T[None],
        input_grad.T[None],
        sum_qkv,
        sum_pos,
        sum_w_out,
        sum_rel,
        jnp.stack([sum_in_early, sum_in_late], axis=1).transpose(1, 0, 2),
        jnp.stack([sum_out_early, sum_out_late], axis=1).transpose(1, 2, 0),
        sum_conv_in.T,
        sum_depth,
        sum_conv_out,
        bn_grads[0],
        bn_grads[1],
        sum_gain,
        sum_bias,
    )


def solution(mesh):
    whole = P()
    split = P("dp", "seq", None)
    return jax.shard_map(
        local,
        mesh=mesh,
        in_specs=(split,) + (whole,) * 13 + (P("dp", None), split),
        out_specs=(split, split) + (whole,) * 13,
        check_vma=False,
    )
```

```python
import functools
import math

import jax
import jax.numpy as jnp
from jax import lax
from jax.experimental import pallas as pl
from jax.experimental.pallas import tpu as pltpu
from jax.sharding import PartitionSpec as P
import numpy as np

HEADS = 4
LANES = 128
WIDE = 3 * LANES
HALO = 16
SMALL = 48
EPS = 1e-05
MODEL_AXES = ("seq", "dp")
VMEM_BYTES = 56 * 1024 * 1024
BF16 = jnp.bfloat16
F32 = jnp.float32


def device_count():
    return lax.axis_size("seq") * lax.axis_size("dp")


def flat_index():
    return lax.axis_index("seq") * lax.axis_size("dp") + lax.axis_index("dp")


def swap_flat(block, distance):
    pairs = [(i, i ^ distance) for i in range(device_count())]
    return lax.ppermute(block, MODEL_AXES, pairs)


def swap_seq(block, distance):
    pairs = [(i, i ^ distance) for i in range(lax.axis_size("seq"))]
    return lax.ppermute(block, "seq", pairs)


def shift_seq(block, step):
    count = lax.axis_size("seq")
    pairs = [(i, i + step) for i in range(count) if 0 <= i + step < count]
    return lax.ppermute(block, "seq", pairs)


def stage_radices(devices):
    radices = [2]
    left = devices // 2
    while left > 1:
        radix = 4 if left % 4 == 0 else 2
        radices.append(radix)
        left = left // radix
    return radices


def slot_pieces(devices):
    slots = jnp.arange(devices, dtype=jnp.int32)
    distance = jnp.zeros((devices,), jnp.int32)
    span = devices
    stride = 1
    for radix in stage_radices(devices):
        span = span // radix
        distance = distance + ((slots // span) % radix) * stride
        stride = stride * radix
    return flat_index() ^ distance


def add_kernel(counts, radix, *refs):
    outs = refs[sum(counts) :]
    start = 0
    row = 0
    for count in counts:
        parts = refs[start : start + count]
        start = start + count
        total = parts[0][...].astype(F32)
        for part in parts[1:]:
            total = total + part[...].astype(F32)
        total = total.astype(BF16)
        span, share = total.shape[0] // radix, total.shape[1]
        for place, out in enumerate(outs):
            out[:, row : row + share] = total[place * span : (place + 1) * span]
        row = row + share


class SlotSum:
    def __init__(self, keep, send):
        self.others = []
        radices = stage_radices(device_count())
        strides = [1]
        for radix in radices[:-1]:
            strides.append(strides[-1] * radix)
        self.stages = list(zip(radices, strides))
        self.next = 1
        self.parts = self.scatter(0, [keep, send])
        self.mark = keep

    def join(self, other):
        self.others.append(other.parts)

    def scatter(self, stage, pieces):
        radix, stride = self.stages[stage]
        return [pieces[0]] + [
            swap_flat(pieces[step], step * stride) for step in range(radix - 1, 0, -1)
        ]

    def spread(self, stage, piece):
        radix, stride = self.stages[stage]
        return [piece] + [swap_flat(piece, step * stride) for step in range(1, radix)]

    def step(self, *earlier):
        count = len(self.stages)
        parts = self.parts
        if self.next >= 2 * count:
            return self.mark
        if earlier:
            parts = [after(parts[0], *earlier)] + parts[1:]
        if self.next <= count:
            radix = self.stages[self.next][0] if self.next < count else 1
            groups = [parts] + self.others
            self.others = []
            slots = parts[0].shape[0]
            share = sum(group[0].shape[1] for group in groups)
            pieces = call(
                functools.partial(add_kernel, [len(group) for group in groups], radix),
                [struct((slots // radix, share, LANES), BF16)] * radix,
                [part for group in groups for part in group],
                micros=2.0,
            )
            self.mark = pieces[0]
            if radix > 1:
                self.parts = self.scatter(self.next, pieces)
            else:
                self.parts = self.spread(count - 1, pieces[0])
        else:
            self.mark = jnp.concatenate(parts, axis=0)
            self.parts = self.spread(2 * count - 1 - self.next, self.mark)
        self.next = self.next + 1
        return self.mark

    def finish(self):
        while self.next < 2 * len(self.stages):
            self.step()
        return self.parts


def exchange_small(spread):
    return lax.all_to_all(spread, MODEL_AXES, 0, 0)


def after(value, *earlier):
    return lax.optimization_barrier((value,) + earlier)[0]


def gather_frames(shard, meanwhile):
    count = lax.axis_size("seq")
    across = [shard] + [swap_seq(shard, 2 * step) for step in range(1, count // 2)]
    made = meanwhile()
    blocks = []
    for step, block in enumerate(across):
        blocks.append(block)
        passed = block if step < count // 2 - 1 else after(block, made[0])
        blocks.append(swap_seq(passed, 1))
    return blocks, made


class FrameSum:
    def __init__(self, partials):
        count = lax.axis_size("seq") // 2
        self.kept = partials[0::2]
        self.passed = [swap_seq(partials[2 * step + 1], 1) for step in range(count - 1, 0, -1)]
        self.passed = [swap_seq(partials[1], 1)] + self.passed[::-1]

    def step(self, *earlier):
        count = len(self.kept)
        self.arrived, self.joined = [], []
        for step in range(count - 1, 0, -1):
            joined = self.kept[step].astype(F32) + self.passed[step].astype(F32)
            if earlier:
                joined = after(joined, *earlier)
            self.joined.append(joined.astype(BF16))
            self.arrived.append(swap_seq(self.joined[-1], 2 * step))

    def finish(self, own):
        total = own + self.kept[0].astype(F32) + self.passed[0].astype(F32)
        for block in self.arrived:
            total = total + block.astype(F32)
        return total


def cost(micros):
    return pl.CostEstimate(flops=int(micros * 1.15e9), bytes_accessed=0, transcendentals=0)


def call(body, outs, args, scratch=(), micros=2.0, smem=0):
    specs = [
        pl.BlockSpec(memory_space=pltpu.SMEM if place < smem else pltpu.VMEM)
        for place in range(len(args))
    ]
    return pl.pallas_call(
        body,
        out_shape=tuple(outs),
        in_specs=specs,
        out_specs=tuple(pl.BlockSpec(memory_space=pltpu.VMEM) for _ in outs),
        scratch_shapes=list(scratch),
        compiler_params=pltpu.CompilerParams(vmem_limit_bytes=VMEM_BYTES),
        cost_estimate=cost(micros),
    )(*args)


def struct(shape, dtype):
    return jax.ShapeDtypeStruct(tuple(shape), dtype)


def nn(left, right):
    return lax.dot_general(left, right, (((1,), (0,)), ((), ())), preferred_element_type=F32)


def nt(left, right):
    return lax.dot_general(left, right, (((1,), (1,)), ((), ())), preferred_element_type=F32)


def tn(left, right):
    return lax.dot_general(left, right, (((0,), (0,)), ((), ())), preferred_element_type=F32)


def norm_parts(summed):
    average = jnp.mean(summed, axis=-1, keepdims=True)
    centered = summed - average
    variance = jnp.mean(centered * centered, axis=-1, keepdims=True)
    inverse = lax.rsqrt(variance + EPS)
    return centered * inverse, inverse


def norm_back(unit, inverse, gain, incoming):
    scaled = incoming * gain
    first = jnp.mean(scaled, axis=-1, keepdims=True)
    second = jnp.mean(scaled * unit, axis=-1, keepdims=True)
    grad = inverse * (scaled - first - unit * second)
    return (
        grad,
        jnp.sum(incoming * unit, axis=0, keepdims=True),
        jnp.sum(incoming, axis=0, keepdims=True),
    )


def sigmoid(value):
    return 1.0 / (1.0 + jnp.exp(-value))


def silu_back(value):
    gate = sigmoid(value)
    return gate * (1.0 + value * (1.0 - gate))


def store_tile(ref, rows, copies):
    tile = jnp.zeros((8, LANES), F32)
    parts = []
    for row in rows:
        width = row.shape[1]
        blocks = -(-width // LANES)
        wide = row
        if blocks * LANES > width:
            wide = jnp.concatenate([row, jnp.zeros((1, blocks * LANES - width), F32)], axis=1)
        for block in range(blocks):
            parts.append(wide[:, block * LANES : (block + 1) * LANES])
    for place, part in enumerate(parts):
        tile = jnp.where(
            lax.broadcasted_iota(jnp.int32, (8, LANES), 0) == place,
            jnp.broadcast_to(part, (8, LANES)),
            tile,
        )
    ref[...] = jnp.broadcast_to(tile[None], (copies, 8, LANES))


def tile_row(tile, place, width):
    blocks = -(-width // LANES)
    parts = [tile[place * blocks + block : place * blocks + block + 1] for block in range(blocks)]
    return jnp.concatenate(parts, axis=1)[:, :width]


def plan_blocks(columns):
    runs = []
    block = 0
    for count in columns:
        full = count // LANES
        runs.append([(block + place, 0, place * LANES, LANES) for place in range(full)])
        block = block + full
    open_block, lane = None, LANES
    for place, count in enumerate(columns):
        rest = count % LANES
        if rest:
            if lane + rest > LANES:
                open_block, lane = block, 0
                block = block + 1
            runs[place].append((open_block, lane, count - rest, rest))
            lane = lane + rest
    return runs, block


def block_rows(rows):
    return -(-rows // 8) * 8


def store_matrix(packed, runs, value):
    rows = value.shape[0]
    low = value.astype(BF16)
    for block, lane, column, count in runs:
        start = block * block_rows(rows)
        packed[start : start + rows, lane : lane + count] = low[:, column : column + count]


def load_matrix(packed, runs, out, rows, row=0):
    for block, lane, column, count in runs:
        start = block * block_rows(rows)
        out[row : row + rows, column : column + count] = packed[
            start : start + rows, lane : lane + count
        ].astype(F32)


def load_layer(packed, runs, out, layer):
    rows = out.shape[0]
    for block, lane, column, count in runs:
        start = block * block_rows(rows)
        out[:, layer, column : column + count] = packed[
            start : start + rows, lane : lane + count
        ].astype(F32)


def spread_pieces(slots_ref, packed, keep_ref, send_ref):
    half, share = keep_ref.shape[:2]

    def one(slot, nothing):
        low = pl.multiple_of(slots_ref[slot] * share, HALO)
        keep_ref[slot] = packed[pl.ds(low, share), :]
        high = pl.multiple_of(slots_ref[slot + half] * share, HALO)
        send_ref[slot] = packed[pl.ds(high, share), :]
        return nothing

    lax.fori_loop(0, half, one, 0)


def collect_pieces(slots_ref, keep_ref, send_ref, packed, row=0):
    half = keep_ref.shape[0]
    share = packed.shape[0] // (2 * half)

    def one(slot, nothing):
        low = pl.multiple_of(slots_ref[slot] * share, HALO)
        packed[pl.ds(low, share), :] = keep_ref[slot, row : row + share]
        high = pl.multiple_of(slots_ref[slot + half] * share, HALO)
        packed[pl.ds(high, share), :] = send_ref[slot, row : row + share]
        return nothing

    lax.fori_loop(0, half, one, 0)


def share_rows(rows, devices):
    return -(-rows // (HALO * devices)) * HALO


def half_slots(rows, devices):
    share = share_rows(rows, devices)
    return [struct((devices // 2, share, LANES), BF16)] * 2, pltpu.VMEM((devices * share, LANES), BF16)


def wave_tables(rows, blocks, width):
    half = width // 2
    frequency = np.exp(np.arange(half) * (-2.0 * math.log(10000.0) / width))
    tail = np.zeros(LANES // 2)
    tail[: half - LANES] = frequency[LANES:]
    lanes = np.concatenate([frequency[:LANES], frequency[:LANES], tail, tail])[None]
    row_angles = np.arange(rows)[:, None] * lanes
    block_angles = (np.arange(blocks) * rows)[:, None] * lanes
    return [
        jnp.asarray(table.astype(np.float32))
        for table in (
            np.cos(row_angles),
            np.sin(row_angles),
            np.cos(block_angles),
            np.sin(block_angles),
        )
    ]


def half_pieces(width):
    half = width // 2
    rest = half - LANES
    return (
        (0, 0, LANES),
        (half, LANES, LANES),
        (LANES, 2 * LANES, rest),
        (half + LANES, 2 * LANES + LANES // 2, rest),
    )


def half_sign():
    lane = lax.broadcasted_iota(jnp.int32, (1, LANES), 1)
    return jnp.where(lane < LANES // 2, 1.0, -1.0)


def prepare_kernel(where, lengths, turned, w_qkv, w_pos, w_out, bias, depth, base_cos, base_sin, block_cos, block_sin, block, query, shift, w_query, w_pair, w_pos_wide, w_out_wide, depth_wide, table, own_cos, own_sin, clip_rows, clip_columns, clip_wide, valid_wide):
    place = where[0]
    width, rows = turned.shape
    size = width // HEADS
    blocks = block_cos.shape[0]
    w_query[...] = jnp.zeros_like(w_query)
    w_pair[...] = jnp.zeros_like(w_pair)
    w_pos_wide[...] = jnp.zeros_like(w_pos_wide)
    w_out_wide[...] = jnp.zeros_like(w_out_wide)
    depth_wide[...] = jnp.zeros_like(depth_wide)
    depth_wide[:, :width] = depth[...]
    for head in range(HEADS):
        natural = slice(head * size, (head + 1) * size)
        low = head * LANES
        w_query[:, low : low + size] = w_qkv[:, head * size : (head + 1) * size]
        w_pair[head, :, :size] = w_qkv[:, width + head * size : width + (head + 1) * size]
        w_pair[head, :, LANES : LANES + size] = w_qkv[
            :, 2 * width + head * size : 2 * width + (head + 1) * size
        ]
        w_out_wide[low : low + size] = w_out[natural]
        for source, target, length in half_pieces(width):
            w_pos_wide[target : target + length, low : low + size] = w_pos[
                source : source + length, natural
            ]
    lane = lax.broadcasted_iota(jnp.int32, (1, WIDE), 1)
    on_cosine = (lane < LANES) | ((lane >= 2 * LANES) & (lane < 2 * LANES + LANES // 2))
    row_cos, row_sin = base_cos[...], base_sin[...]
    ends = [lengths[0, 0]]
    for clip in range(1, lengths.shape[1]):
        ends.append(ends[-1] + lengths[0, clip])

    def clip_at(frames):
        clip = jnp.zeros_like(frames)
        for end in ends:
            clip = clip + (frames >= end).astype(jnp.int32)
        return clip

    for step in range(blocks):
        here = place ^ step
        cosine = block_cos[pl.ds(here, 1), :]
        sine = block_sin[pl.ds(here, 1), :]
        one = jnp.where(on_cosine, cosine, sine)
        two = jnp.where(on_cosine, -sine, cosine)
        table[:, step * rows : (step + 1) * rows] = (one * row_cos + two * row_sin).astype(BF16).T
        clip_columns[:, step * rows : (step + 1) * rows] = clip_at(
            here * rows + lax.broadcasted_iota(jnp.int32, (1, rows), 1)
        )
    reached = place * rows - HALO + lax.broadcasted_iota(jnp.int32, (rows + 2 * HALO, LANES), 0)
    inside = (reached >= 0) & (reached < blocks * rows)
    reached_clip = jnp.where(inside, clip_at(reached), -1)
    clip_wide[...] = reached_clip
    clip_rows[...] = reached_clip[HALO : HALO + rows, 0:1]
    valid_wide[...] = (inside & (reached < ends[-1])).astype(F32)[:, 0:1]
    block_cosine = block_cos[pl.ds(place, 1), :]
    block_sine = block_sin[pl.ds(place, 1), :]
    cosines = block_cosine * row_cos - block_sine * row_sin
    sines = block_sine * row_cos + block_cosine * row_sin
    own_cos[...] = cosines
    own_sin[...] = sines
    frames = turned[...].T
    block[...] = frames
    projected = nn(frames, w_query[...])
    sign = half_sign()
    for head in range(HEADS):
        lanes = slice(head * LANES, (head + 1) * LANES)
        natural = slice(head * size, (head + 1) * size)
        wide = jnp.zeros((2, LANES - size), F32)
        added = jnp.concatenate([bias[:, natural], wide], axis=1)
        unit = (projected[:, lanes] + added[0:1]).astype(BF16)
        moved = (projected[:, lanes] + added[1:2]).astype(BF16)
        shift[:, lanes] = moved
        shifted = nt(moved, w_pos_wide[:, lanes])
        first, second = shifted[:, :LANES], shifted[:, LANES : 2 * LANES]
        tail = shifted[:, 2 * LANES :]
        sine, cosine = sines[:, :LANES], cosines[:, :LANES]
        query[head, :, :LANES] = unit
        query[head, :, LANES : 2 * LANES] = (first * sine + second * cosine).astype(BF16)
        query[head, :, 2 * LANES : 3 * LANES] = (second * sine - first * cosine).astype(BF16)
        query[head, :, 3 * LANES :] = (
            tail * sines[:, 2 * LANES :]
            + pltpu.roll(tail, LANES // 2, 1) * cosines[:, 2 * LANES :] * sign
        ).astype(BF16)


def masked_scores(query, key, table, clip_rows, clip_columns, scale):
    upper = jnp.concatenate([key, table[:LANES]], axis=0)
    raw = nn(query[:, : 2 * LANES], upper) + nn(query[:, 2 * LANES :], table[LANES:])
    return jnp.where(clip_rows == clip_columns, raw * scale, -1e30)


def attend_kernel(scale, chunks, count, *refs):
    blocks = refs[:count]
    query, w_pair, table, clip_rows, clip_columns = refs[count : count + 5]
    attended, log_total, pair, frames_all, highest, total, summed = refs[count + 5 :]
    head = pl.program_id(0)
    chunk = pl.program_id(1)
    span = table.shape[1]
    rows = blocks[0].shape[1]

    @pl.when((chunk == 0) & (head == 0))
    def _():
        for step in range(count):
            frames_all[:, step * rows : (step + 1) * rows] = blocks[step][...]

    @pl.when(chunk == 0)
    def _():
        highest[...] = jnp.full_like(highest, -1e30)
        total[...] = jnp.zeros_like(total)
        summed[...] = jnp.zeros_like(summed)

    frames = frames_all[:, pl.ds(pl.multiple_of(chunk * span, LANES), span)]
    both = tn(w_pair[0], frames).astype(BF16)
    pair[0] = both
    scores = masked_scores(
        query[0], both[:LANES], table[...], clip_rows[...], clip_columns[...], scale
    )
    old = highest[...]
    new = jnp.maximum(old, jnp.max(scores, axis=1, keepdims=True))
    weights = jnp.exp(scores - new)
    fade = jnp.exp(old - new)
    highest[...] = new
    total[...] = total[...] * fade + jnp.sum(weights, axis=1, keepdims=True)
    summed[...] = summed[...] * fade + nt(weights.astype(BF16), both[LANES:])

    @pl.when(chunk == chunks - 1)
    def _():
        attended[...] = summed[...] / total[...]
        log_total[0] = highest[...] + jnp.log(total[...])


def attend(blocks, query, w_pair, table, clip_rows, clip_columns, head_width):
    rows = query.shape[1]
    frames = table.shape[1]
    width = w_pair.shape[1]
    span = min(frames, 2048)
    chunks = frames // span
    return pl.pallas_call(
        functools.partial(attend_kernel, 1.0 / math.sqrt(head_width), chunks, len(blocks)),
        grid=(HEADS, chunks),
        in_specs=[pl.BlockSpec((width, rows), lambda h, c: (0, 0)) for _ in blocks]
        + [
            pl.BlockSpec((1, rows, 4 * LANES), lambda h, c: (h, 0, 0)),
            pl.BlockSpec((1, width, 2 * LANES), lambda h, c: (h, 0, 0)),
            pl.BlockSpec((WIDE, span), lambda h, c: (0, c)),
            pl.BlockSpec((rows, 1), lambda h, c: (0, 0)),
            pl.BlockSpec((1, span), lambda h, c: (0, c)),
        ],
        out_specs=(
            pl.BlockSpec((rows, LANES), lambda h, c: (0, h)),
            pl.BlockSpec((1, rows, 1), lambda h, c: (h, 0, 0)),
            pl.BlockSpec((1, 2 * LANES, span), lambda h, c: (h, 0, c)),
        ),
        out_shape=(
            struct((rows, HEADS * LANES), F32),
            struct((HEADS, rows, 1), F32),
            struct((HEADS, 2 * LANES, frames), BF16),
        ),
        scratch_shapes=[
            pltpu.VMEM((width, frames), BF16),
            pltpu.VMEM((rows, 1), F32),
            pltpu.VMEM((rows, 1), F32),
            pltpu.VMEM((rows, LANES), F32),
        ],
        compiler_params=pltpu.CompilerParams(vmem_limit_bytes=VMEM_BYTES),
        cost_estimate=cost(12.0),
    )(*blocks, query, w_pair, table, clip_rows, clip_columns)


def early_kernel(block, attended, w_out, gains, biases, ffn_in, ffn_out, gates, first_sum, second_sum, second_norm, left, right, gated, attended_low):
    low = attended[...].astype(BF16)
    attended_low[...] = low
    summed = block[...].astype(F32) + nn(low, w_out[...])
    first_sum[...] = summed
    unit, _ = norm_parts(summed)
    first = unit * gains[0:1] + biases[0:1]
    inner = nn(first.astype(BF16), ffn_in[...])
    act = (inner * sigmoid(inner)).astype(BF16)
    summed = first + nt(act, ffn_out[...])
    second_sum[...] = summed
    unit, _ = norm_parts(summed)
    second = unit * gains[1:2] + biases[1:2]
    second_norm[...] = second
    second_low = second.astype(BF16)
    half = gates.shape[0] // 2
    one = nt(second_low, gates[:half])
    two = nt(second_low, gates[half:])
    left[...] = one
    right[...] = two
    gated[...] = jnp.zeros_like(gated)
    gated[:, : one.shape[1]] = (one * sigmoid(two)).astype(BF16)


def again_kernel(first_sum, second_sum, gains, biases, ffn_in, first_low_out, second_low_out, act_out, slope_out):
    unit, _ = norm_parts(second_sum[...])
    second_low_out[...] = (unit * gains[1:2] + biases[1:2]).astype(BF16)
    unit, _ = norm_parts(first_sum[...])
    first_low = (unit * gains[0:1] + biases[0:1]).astype(BF16)
    first_low_out[...] = first_low
    inner = nn(first_low, ffn_in[...])
    gate = sigmoid(inner)
    act_out[...] = (inner * gate).astype(BF16)
    slope_out[...] = (gate * (1.0 + inner * (1.0 - gate))).astype(BF16)


def lane_blocks(width):
    return [(lane, min(LANES, width - lane)) for lane in range(0, width, LANES)]


def extend(extended, low, middle, high):
    rows, width = middle.shape
    for block, (lane, count) in enumerate(lane_blocks(width)):
        if count < LANES:
            extended[block] = jnp.zeros((rows + 2 * HALO, LANES), F32)
        extended[block, 0:HALO, :count] = low[:, lane : lane + count].astype(F32)
        extended[block, HALO : HALO + rows, :count] = middle[:, lane : lane + count].astype(F32)
        extended[block, HALO + rows :, :count] = high[:, lane : lane + count].astype(F32)


def convolve(extended, clip, depth, mirrored, store):
    taps = depth.shape[0]
    blocks, rows, _ = extended.shape
    rows = rows - 2 * HALO
    step = 64
    for start in range(0, rows, step):
        own = clip[HALO + start : HALO + start + step]
        sums = [jnp.zeros((step, LANES), F32) for _ in range(blocks)]
        for tap in range(taps):
            place = HALO - taps // 2 + tap + start
            same = clip[place : place + step] == own
            row = taps - 1 - tap if mirrored else tap
            for block in range(blocks):
                lanes = slice(block * LANES, (block + 1) * LANES)
                sums[block] = sums[block] + depth[row : row + 1, lanes] * jnp.where(
                    same, extended[block, place : place + step], 0.0
                )
        store(start, step, jnp.concatenate(sums, axis=1))


def conv_kernel(copies, low, middle, high, clip, depth, valid, convolved, tile, extended):
    rows, width = convolved.shape
    extend(extended, low[...], middle[...], high[...])

    def store(start, step, value):
        convolved[start : start + step] = value[:, :width]

    convolve(extended, clip, depth, False, store)
    value = convolved[...]
    kept = value * valid[...]
    count = jnp.zeros((1, width), F32) + jnp.sum(valid[...], axis=0, keepdims=True)
    store_tile(
        tile,
        [
            jnp.sum(kept, axis=0, keepdims=True),
            jnp.sum(kept * value, axis=0, keepdims=True),
            count[:, :LANES],
        ],
        copies,
    )


def taps_kernel(taps, count, low, middle, high, clip, *refs):
    factors, outs, extended = refs[:count], refs[count : 2 * count], refs[2 * count]
    rows, width = factors[0].shape
    extend(extended, low[...], middle[...], high[...])
    step = 64
    sums = [[[None] * 3 for _ in range(taps)] for _ in range(count)]
    for start in range(0, rows, step):
        own = clip[HALO + start : HALO + start + step]
        for block, (lane, lanes) in enumerate(lane_blocks(width)):
            here = []
            for factor in factors:
                part = factor[start : start + step, lane : lane + lanes]
                if lanes < LANES:
                    part = jnp.concatenate([part, jnp.zeros((step, LANES - lanes), F32)], axis=1)
                here.append(part)
            for tap in range(taps):
                place = HALO - taps // 2 + tap + start
                same = clip[place : place + step] == own
                there = jnp.where(same, extended[block, place : place + step], 0.0)
                for which in range(count):
                    part = jnp.sum((there * here[which]).reshape(step // 8, 8, LANES), axis=0)
                    old = sums[which][tap][block]
                    sums[which][tap][block] = part if old is None else old + part
    for which in range(count):
        for tap in range(taps):
            outs[which][tap : tap + 1] = jnp.concatenate(
                [jnp.sum(part, axis=0, keepdims=True) for part in sums[which][tap]], axis=1
            )[:, :width]


def late_kernel(copies, arrived, convolved, second_norm, bn_gain, bn_bias, conv_out, gains, biases, ffn_in, ffn_out, cotangent, result, act_out, d_inner_out, third_low_out, fourth_grad_out, swished_out, third_grad_out, third_grad, d_normed_out, unit_out, tile, norm_grads, statistics, edge_low, edge_high):
    width = convolved.shape[1]
    rows = convolved.shape[0]
    sums = jnp.sum(arrived[...], axis=0)
    frames = sums[6:7, 0:1]
    mean = tile_row(sums, 0, width) / frames
    variance = tile_row(sums, 1, width) / frames - mean * mean
    inverse = lax.rsqrt(variance + EPS)
    unit = (convolved[...] - mean) * inverse
    unit_out[...] = unit
    statistics[...] = jnp.zeros_like(statistics)
    statistics[0:1, :width] = inverse
    statistics[1:2, :width] = jnp.broadcast_to(frames, (1, width))
    statistics[2:3, :width] = mean
    normed = unit * bn_gain[...] + bn_bias[...]
    swished = (normed * sigmoid(normed)).astype(BF16)
    swished_out[...] = swished
    third_unit, third_inverse = norm_parts(second_norm[...] + nn(swished, conv_out[...]))
    third = third_unit * gains[2:3] + biases[2:3]
    third_low = third.astype(BF16)
    third_low_out[...] = third_low
    inner = nn(third_low, ffn_in[...])
    gate = sigmoid(inner)
    act = (inner * gate).astype(BF16)
    act_out[...] = act
    fourth_unit, fourth_inverse = norm_parts(third + nt(act, ffn_out[...]))
    result[...] = (fourth_unit * gains[3:4] + biases[3:4]).T
    fourth_grad, gain_three, bias_three = norm_back(
        fourth_unit, fourth_inverse, gains[3:4], cotangent[...].T
    )
    fourth_low = fourth_grad.astype(BF16)
    fourth_grad_out[...] = fourth_low
    d_act = nn(fourth_low, ffn_out[...])
    d_inner = (d_act * (gate * (1.0 + inner * (1.0 - gate)))).astype(BF16)
    d_inner_out[...] = d_inner
    grad, gain_two, bias_two = norm_back(
        third_unit, third_inverse, gains[2:3], fourth_grad + nt(d_inner, ffn_in[...])
    )
    third_grad[...] = grad
    grad_low = grad.astype(BF16)
    third_grad_out[...] = grad_low
    d_normed = nt(grad_low, conv_out[...]) * silu_back(normed)
    d_normed_out[...] = d_normed
    store_tile(
        tile,
        [
            jnp.sum(d_normed * unit, axis=0, keepdims=True),
            jnp.sum(d_normed, axis=0, keepdims=True),
        ],
        copies,
    )
    norm_grads[0:1] = gain_two
    norm_grads[1:2] = gain_three
    norm_grads[2:3] = bias_two
    norm_grads[3:4] = bias_three
    edge_low[0] = d_normed[:HALO]
    edge_low[1] = unit[:HALO]
    edge_high[0] = d_normed[rows - HALO :]
    edge_high[1] = unit[rows - HALO :]


def late_columns(width, inner):
    return (inner, inner, width)


def early_columns(width, inner):
    return (inner, inner, width, width, width)


def last_columns(width):
    return (3 * width, width)


def packed_rows(columns, width, small=0):
    _, blocks = plan_blocks(columns)
    return blocks * block_rows(width) + small


def late_grads_kernel(slots, third_low, d_inner, act, fourth_grad, swished, third_grad, keep, send, packed):
    width = third_low.shape[1]
    runs, _ = plan_blocks(late_columns(width, act.shape[1]))
    store_matrix(packed, runs[0], tn(third_low[...], d_inner[...]))
    store_matrix(packed, runs[1], tn(fourth_grad[...], act[...]))
    store_matrix(packed, runs[2], tn(swished[...], third_grad[...]))
    spread_pieces(slots, packed, keep, send)


def gates_back_kernel(arrived, statistics, bn_gain, d_normed, unit, from_low, from_high, clip, valid, depth, left, right, gates, third_grad, second_sum, gains, second_grad_out, second_grad_low_out, d_left_out, d_right_out, norm_grads, bn_grads, extended, d_gated):
    rows, width = left.shape
    sums = jnp.sum(arrived[...], axis=0)
    gain_sum = tile_row(sums, 0, width)
    bias_sum = tile_row(sums, 1, width)
    bn_grads[0:1] = gain_sum
    bn_grads[1:2] = bias_sum
    gain = bn_gain[...]
    inverse = statistics[0:1, :width]
    frames = statistics[1:2, :width]

    def conv_grad(d_rows, unit_rows, valid_rows):
        return (
            inverse * gain * (d_rows - valid_rows * (bias_sum + unit_rows * gain_sum) / frames)
        ).astype(BF16)

    extend(
        extended,
        conv_grad(from_low[0], from_low[1], valid[0:HALO]),
        conv_grad(d_normed[...], unit[...], valid[HALO : HALO + rows]),
        conv_grad(from_high[0], from_high[1], valid[HALO + rows :]),
    )

    def store(start, step, value):
        d_gated[start : start + step] = value[:, :width]

    convolve(extended, clip, depth, True, store)
    gate = sigmoid(right[...])
    d_left = (d_gated[...] * gate).astype(BF16)
    d_right = (d_gated[...] * left[...] * gate * (1.0 - gate)).astype(BF16)
    d_left_out[...] = d_left
    d_right_out[...] = d_right
    second_unit, second_inverse = norm_parts(second_sum[...])
    half = gates.shape[0] // 2
    incoming = third_grad[...] + nn(d_left, gates[:half]) + nn(d_right, gates[half:])
    second_grad, gain_one, bias_one = norm_back(
        second_unit, second_inverse, gains[1:2], incoming
    )
    second_grad_out[...] = second_grad
    second_grad_low_out[...] = second_grad.astype(BF16)
    norm_grads[0:1] = gain_one
    norm_grads[1:2] = bias_one


def early_back_kernel(second_grad, slope, first_sum, gains, ffn_in, ffn_out, w_out, attended, first_grad, first_grad_out, d_inner_out, d_attended, delta, norm_grads):
    d_act = nn(second_grad[...].astype(BF16), ffn_out[...])
    d_inner = (d_act * slope[...].astype(F32)).astype(BF16)
    d_inner_out[...] = d_inner
    first_unit, first_inverse = norm_parts(first_sum[...])
    grad, gain_zero, bias_zero = norm_back(
        first_unit, first_inverse, gains[0:1], second_grad[...] + nt(d_inner, ffn_in[...])
    )
    first_grad[...] = grad
    grad_low = grad.astype(BF16)
    first_grad_out[...] = grad_low
    norm_grads[0:1] = gain_zero
    norm_grads[1:2] = bias_zero
    back = nt(grad_low, w_out[...]).astype(BF16)
    d_attended[...] = back
    product = back.astype(F32) * attended[...]
    for head in range(HEADS):
        delta[head] = jnp.sum(
            product[:, head * LANES : (head + 1) * LANES], axis=1, keepdims=True
        )


def early_grads_kernel(slots, first_low, d_inner, act, second_grad, second_low, d_left, d_right, attended_low, first_grad, keep, send, packed):
    width = first_low.shape[1]
    size = width // HEADS
    runs, _ = plan_blocks(early_columns(width, act.shape[1]))
    store_matrix(packed, runs[0], tn(first_low[...], d_inner[...]))
    store_matrix(packed, runs[1], tn(second_grad[...], act[...]))
    store_matrix(packed, runs[2], tn(d_left[...], second_low[...]))
    store_matrix(packed, runs[3], tn(d_right[...], second_low[...]))
    d_out = tn(attended_low[...], first_grad[...])
    store_matrix(
        packed,
        runs[4],
        jnp.concatenate([d_out[head * LANES : head * LANES + size] for head in range(HEADS)], axis=0),
    )
    spread_pieces(slots, packed, keep, send)


def attend_back_kernel(scale, chunks, query, pair, table, clip_rows, clip_columns, log_total, delta, d_attended, shift, w_pos, own_cos, own_sin, d_pair, d_query, d_pos_weight, d_bias, unit_sum, rest_sum):
    chunk = pl.program_id(1)
    key = pair[0, :LANES]
    scores = masked_scores(
        query[0], key, table[...], clip_rows[...], clip_columns[...], scale
    )
    probs = jnp.exp(scores - log_total[0])
    slope = nn(d_attended[...], pair[0, LANES:])
    d_raw = (probs * (slope - delta[0]) * scale).astype(BF16)
    d_pair[0, :, :LANES] = tn(d_raw, query[0, :, :LANES]).astype(BF16)
    d_pair[0, :, LANES:] = tn(probs.astype(BF16), d_attended[...]).astype(BF16)

    @pl.when(chunk == 0)
    def _():
        unit_sum[...] = jnp.zeros_like(unit_sum)
        rest_sum[...] = jnp.zeros_like(rest_sum)

    unit_sum[...] += nt(d_raw, jnp.concatenate([key, table[:LANES]], axis=0))
    rest_sum[...] += nt(d_raw, table[LANES:])

    @pl.when(chunk == chunks - 1)
    def _():
        d_unit = unit_sum[:, :LANES]
        first, second = unit_sum[:, LANES:], rest_sum[:, :LANES]
        tail = rest_sum[:, LANES:]
        cosines, sines = own_cos[...], own_sin[...]
        sine, cosine = sines[:, :LANES], cosines[:, :LANES]
        d_shifted = jnp.concatenate(
            [
                first * sine - second * cosine,
                first * cosine + second * sine,
                tail * sines[:, 2 * LANES :]
                - pltpu.roll(tail, LANES // 2, 1) * cosines[:, 2 * LANES :] * half_sign(),
            ],
            axis=1,
        ).astype(BF16)
        d_from_pos = nn(d_shifted, w_pos[...])
        d_query[...] = (d_unit + d_from_pos).astype(BF16)
        d_pos_weight[...] = tn(d_shifted, shift[...]).astype(BF16)
        d_bias[0:1] = jnp.sum(d_unit, axis=0, keepdims=True)
        d_bias[1:2] = jnp.sum(d_from_pos, axis=0, keepdims=True)


def attend_back(first, heads, query, pair, table, clip_rows, clip_columns, log_total, delta, d_attended, shift, w_pos, own_cos, own_sin, head_width):
    rows = query.shape[1]
    frames = table.shape[1]
    span = min(frames, 2048)
    chunks = frames // span
    wide = heads * LANES
    return pl.pallas_call(
        functools.partial(attend_back_kernel, 1.0 / math.sqrt(head_width), chunks),
        grid=(heads, chunks),
        in_specs=[
            pl.BlockSpec((1, rows, 4 * LANES), lambda h, c: (h + first, 0, 0)),
            pl.BlockSpec((1, 2 * LANES, span), lambda h, c: (h + first, 0, c)),
            pl.BlockSpec((WIDE, span), lambda h, c: (0, c)),
            pl.BlockSpec((rows, 1), lambda h, c: (0, 0)),
            pl.BlockSpec((1, span), lambda h, c: (0, c)),
            pl.BlockSpec((1, rows, 1), lambda h, c: (h + first, 0, 0)),
            pl.BlockSpec((1, rows, 1), lambda h, c: (h + first, 0, 0)),
            pl.BlockSpec((rows, LANES), lambda h, c: (0, h + first)),
            pl.BlockSpec((rows, LANES), lambda h, c: (0, h + first)),
            pl.BlockSpec((WIDE, LANES), lambda h, c: (0, h + first)),
            pl.BlockSpec((rows, WIDE), lambda h, c: (0, 0)),
            pl.BlockSpec((rows, WIDE), lambda h, c: (0, 0)),
        ],
        out_specs=(
            pl.BlockSpec((1, span, 2 * LANES), lambda h, c: (h, c, 0)),
            pl.BlockSpec((rows, LANES), lambda h, c: (0, h)),
            pl.BlockSpec((WIDE, LANES), lambda h, c: (0, h)),
            pl.BlockSpec((2, LANES), lambda h, c: (0, h)),
        ),
        out_shape=(
            struct((heads, frames, 2 * LANES), BF16),
            struct((rows, wide), BF16),
            struct((WIDE, wide), BF16),
            struct((2, wide), F32),
        ),
        scratch_shapes=[pltpu.VMEM((rows, 2 * LANES), F32), pltpu.VMEM((rows, 2 * LANES), F32)],
        compiler_params=pltpu.CompilerParams(vmem_limit_bytes=VMEM_BYTES),
        cost_estimate=cost(9.0),
    )(query, pair, table, clip_rows, clip_columns, log_total, delta, d_attended, shift, w_pos, own_cos, own_sin)


def pair_weight_kernel(slots, turned, d_query_one, d_query_two, d_pair_one, d_pair_two, d_pos_one, d_pos_two, d_bias_one, d_bias_two, depth_valid, depth_conv, depth_grad, statistics, bn_grads, bn_gain, late_norms, second_norms, first_norms, *refs):
    count = len(refs) - 4
    blocks = refs[:count]
    keep, send, packed, natural = refs[count:]
    width, rows = turned.shape
    size = width // HEADS
    each = HEADS // 2
    runs, total = plan_blocks(last_columns(width))
    d_pos = jnp.zeros((width, width), F32)
    for head in range(HEADS):
        lanes = slice(head * size, (head + 1) * size)
        low = (head % each) * LANES
        d_query = (d_query_one, d_query_two)[head // each]
        d_pair = (d_pair_one, d_pair_two)[head // each]
        d_pos = (d_pos_one, d_pos_two)[head // each]
        d_bias = (d_bias_one, d_bias_two)[head // each]
        grad = None
        for step in range(count):
            term = nn(
                blocks[step][...], d_pair[head % each, step * rows : (step + 1) * rows]
            )
            grad = term if grad is None else grad + term
        natural[:width, lanes] = nn(turned[...], d_query[:, low : low + LANES])[:, :size]
        natural[:width, width + head * size : width + (head + 1) * size] = grad[:, :size]
        natural[:width, 2 * width + head * size : 2 * width + (head + 1) * size] = grad[
            :, LANES : LANES + size
        ]
        for start, spread, length in half_pieces(width):
            natural[start : start + length, 3 * width + head * size : 3 * width + (head + 1) * size] = (
                d_pos[spread : spread + length, low : low + size].astype(F32)
            )
        natural[width : width + 2, lanes] = d_bias[:, low : low + size]
    taps = depth_valid.shape[0]
    inverse, frames, mean = (statistics[row : row + 1, :width] for row in range(3))
    gain_sum, bias_sum = bn_grads[0:1], bn_grads[1:2]
    by_unit = (depth_conv[...] - mean * depth_valid[...]) * inverse
    d_depth = (
        inverse
        * bn_gain[...]
        * (depth_grad[...] - (bias_sum * depth_valid[...] + gain_sum * by_unit) / frames)
    )
    for place, part in enumerate((first_norms, second_norms)):
        natural[width + 2 + place : width + 3 + place, :width] = part[0:1]
        natural[width + 4 + place : width + 5 + place, :width] = part[1:2]
    natural[width + 6 : width + 10, :width] = late_norms[...]
    natural[width + 10 : width + 10 + taps, :width] = d_depth
    store_matrix(packed, runs[0], natural[:width, : 3 * width])
    store_matrix(packed, runs[1], natural[:width, 3 * width :])
    start = total * block_rows(width)
    for lane in range(0, width, LANES):
        count = min(LANES, width - lane)
        packed[start : start + 10 + taps, :count] = natural[
            width : width + 10 + taps, lane : lane + count
        ].astype(BF16)
        start = start + SMALL
    spread_pieces(slots, packed, keep, send)


def frames_back_kernel(count, d_pair_one, d_pair_two, d_query_one, d_query_two, w_pair, w_query, first_grad, *refs):
    d_frames = refs[:count]
    own_grad = refs[count]
    rows = first_grad.shape[0]
    each = HEADS // 2
    half_wide = each * LANES
    grad = first_grad[...] + nt(d_query_one[...], w_query[:, :half_wide])
    own_grad[...] = (grad + nt(d_query_two[...], w_query[:, half_wide:])).T
    for step in range(count):
        here = slice(step * rows, (step + 1) * rows)
        total = None
        for head in range(HEADS):
            part = (d_pair_one, d_pair_two)[head // each][head % each, here]
            term = nt(w_pair[head], part)
            total = term if total is None else total + term
        d_frames[step][...] = total.astype(BF16)


def finish_two_kernel(slots, keep, send, ffn_in, ffn_out, conv_in, conv_out, w_out, late, early):
    width, _, inner = ffn_in.shape
    share = late.shape[0] // (2 * keep.shape[0])
    collect_pieces(slots, keep, send, late)
    collect_pieces(slots, keep, send, early, share)
    late_runs, _ = plan_blocks(late_columns(width, inner))
    early_runs, _ = plan_blocks(early_columns(width, inner))
    for place, out in enumerate((ffn_in, ffn_out)):
        load_layer(early, early_runs[place], out, 0)
        load_layer(late, late_runs[place], out, 1)
    load_matrix(late, late_runs[2], conv_out, width)
    load_matrix(early, early_runs[2], conv_in, width)
    load_matrix(early, early_runs[3], conv_in, width, width)
    load_matrix(early, early_runs[4], w_out, width)


def finish_last_kernel(slots, keep, send, w_qkv, w_pos, d_bias, gains, biases, d_depth, packed):
    width = w_pos.shape[1]
    collect_pieces(slots, keep, send, packed)
    runs, total = plan_blocks(last_columns(width))
    load_matrix(packed, runs[0], w_qkv, width)
    load_matrix(packed, runs[1], w_pos, width)
    taps = d_depth.shape[0]
    start = total * block_rows(width)
    for lane in range(0, width, LANES):
        count = min(LANES, width - lane)
        lanes = slice(lane, lane + count)
        small = packed[start : start + SMALL, :count].astype(F32)
        d_bias[:, lanes] = small[0:2]
        gains[0:2, lanes] = small[2:4]
        biases[0:2, lanes] = small[4:6]
        gains[2:4, lanes] = small[6:8]
        biases[2:4, lanes] = small[8:10]
        d_depth[:, lanes] = small[10 : 10 + taps]
        start = start + SMALL


def local(inputs, w_qkv, w_pos, w_out, rel_bias, ffn_in, ffn_out, conv_in, conv_depth, conv_out, bn_gain, bn_bias, norm_gain, norm_bias, lengths, cotangent):
    _, rows, width = inputs.shape
    inner = ffn_in.shape[2]
    taps = conv_depth.shape[0]
    head_width = width // HEADS
    seq_count = lax.axis_size("seq")
    devices = device_count()
    slots = slot_pieces(devices)
    place = lax.axis_index("seq").astype(jnp.int32).reshape(1)
    total = seq_count * rows

    turned = inputs[0].T
    in_both = ffn_in.transpose(1, 0, 2)
    in_early, in_late = in_both[:, 0], in_both[:, 1]
    out_both = ffn_out.transpose(2, 0, 1)
    out_early, out_late = out_both[:, 0], out_both[:, 1]
    gates = conv_in.T
    cotangent_turned = cotangent[0].T
    bn_gain_row, bn_bias_row = bn_gain[None], bn_bias[None]

    model = struct((rows, width), F32)
    model_low = struct((rows, width), BF16)
    inner_low = struct((rows, inner), BF16)
    head_low = struct((rows, HEADS * LANES), BF16)
    tile = struct((devices, 8, LANES), F32)
    reached = rows + 2 * HALO
    blocks, (
        block,
        query,
        shift,
        w_query,
        w_pair,
        w_pos_wide,
        w_out_wide,
        depth_wide,
        table,
        own_cos,
        own_sin,
        clip_rows,
        clip_columns,
        clip_wide,
        valid_wide,
    ) = gather_frames(turned, lambda: call(
        prepare_kernel,
        [
            model_low,
            struct((HEADS, rows, 4 * LANES), BF16),
            head_low,
            struct((width, HEADS * LANES), BF16),
            struct((HEADS, width, 2 * LANES), BF16),
            struct((WIDE, HEADS * LANES), BF16),
            struct((HEADS * LANES, width), BF16),
            struct((taps, WIDE), F32),
            struct((WIDE, total), BF16),
            struct((rows, WIDE), F32),
            struct((rows, WIDE), F32),
            struct((rows, 1), jnp.int32),
            struct((1, total), jnp.int32),
            struct((reached, LANES), jnp.int32),
            struct((reached, 1), F32),
        ],
        [place, lengths, turned, w_qkv, w_pos, w_out, rel_bias, conv_depth]
        + wave_tables(rows, seq_count, width),
        micros=5.5,
        smem=2,
    ))
    valid_rows = valid_wide[HALO : HALO + rows]
    attended, log_total, pair = attend(
        blocks, query, w_pair, table, clip_rows, clip_columns, head_width
    )
    first_sum, second_sum, second_norm, left, right, gated, attended_low = call(
        early_kernel,
        [model, model, model, model, model, struct((rows, WIDE), BF16), head_low],
        [block, attended, w_out_wide, norm_gain, norm_bias, in_early, out_early, gates],
        micros=5.0,
    )
    gated_low = shift_seq(gated[rows - HALO :], 1)
    gated_high = shift_seq(gated[:HALO], -1)
    convolved, spread = call(
        functools.partial(conv_kernel, devices),
        [model, tile],
        [gated_low, gated, gated_high, clip_wide, depth_wide, valid_rows],
        scratch=[pltpu.VMEM((3, reached, LANES), F32)],
        micros=3.5,
    )
    arrived = exchange_small(spread)
    first_low, second_low, act_early, slope_early = call(
        again_kernel,
        [model_low, model_low, inner_low, inner_low],
        [first_sum, second_sum, norm_gain, norm_bias, in_early],
        micros=3.0,
    )

    def tap_sums(first, *factors):
        return call(
            functools.partial(taps_kernel, taps, len(factors)),
            [struct((taps, width), F32)] * len(factors),
            [first, gated, gated_high, clip_wide] + list(factors),
            scratch=[pltpu.VMEM((3, reached, LANES), F32)],
            micros=2.0 + 1.0 * len(factors),
        )

    depth_valid, depth_conv = tap_sums(
        gated_low, jnp.broadcast_to(valid_rows, (rows, width)), convolved * valid_rows
    )
    arrived = after(arrived, first_low, depth_valid)
    edge = struct((2, HALO, width), F32)
    (
        result,
        act_late,
        d_inner_late,
        third_low,
        fourth_grad,
        swished,
        third_grad_low,
        third_grad,
        d_normed,
        unit,
        spread,
        late_norms,
        statistics,
        edge_low,
        edge_high,
    ) = call(
        functools.partial(late_kernel, devices),
        [struct((width, rows), F32), inner_low, inner_low, model_low, model_low, model_low]
        + [model_low, model, model, model]
        + [tile, struct((4, width), F32), struct((8, WIDE), F32), edge, edge],
        [arrived, convolved, second_norm, bn_gain_row, bn_bias_row, conv_out, norm_gain, norm_bias]
        + [in_late, out_late, cotangent_turned],
        micros=6.4,
    )
    from_low = shift_seq(edge_high, 1)
    from_high = shift_seq(edge_low, -1)
    arrived = exchange_small(spread)
    late_rows = packed_rows(late_columns(width, inner), width)
    outs, late_scratch = half_slots(late_rows, devices)
    late_keep, late_send = call(
        late_grads_kernel,
        outs,
        [slots, third_low, d_inner_late, act_late, fourth_grad, swished, third_grad_low],
        scratch=[late_scratch],
        micros=4.3,
        smem=1,
    )
    late_sum = SlotSum(late_keep, late_send)
    stat = struct((HEADS, rows, 1), F32)
    second_grad, second_grad_low, d_left, d_right, second_norms, bn_grads = call(
        gates_back_kernel,
        [model, model_low, model_low, model_low, struct((2, width), F32), struct((2, width), F32)],
        [after(arrived, late_keep), statistics, bn_gain_row, d_normed, unit]
        + [from_low, from_high, clip_wide, valid_wide, depth_wide, left, right, gates, third_grad]
        + [second_sum, norm_gain],
        scratch=[pltpu.VMEM((3, reached, LANES), F32), pltpu.VMEM((rows, width), F32)],
        micros=5.5,
    )
    mark = late_sum.step(second_grad)
    first_grad, first_grad_low, d_inner_early, d_attended, delta, first_norms = call(
        early_back_kernel,
        [model, model_low, inner_low, head_low, stat, struct((2, width), F32)],
        [after(second_grad, mark), slope_early, first_sum, norm_gain, in_early, out_early]
        + [w_out_wide, attended],
        micros=4.0,
    )
    early_rows = packed_rows(early_columns(width, inner), width)
    outs, early_scratch = half_slots(early_rows, devices)
    early_keep, early_send = call(
        early_grads_kernel,
        outs,
        [slots, first_low, d_inner_early, act_early, second_grad_low]
        + [second_low, d_left, d_right, attended_low, first_grad_low],
        scratch=[early_scratch],
        micros=5.4,
        smem=1,
    )
    early_sum = SlotSum(early_keep, early_send)
    mark = early_keep

    def back(first, query):
        return attend_back(
            first, HEADS // 2, query, pair, table, clip_rows, clip_columns, log_total, delta,
            d_attended, shift, w_pos_wide, own_cos, own_sin, head_width,
        )

    d_pair_one, d_query_one, d_pos_one, d_bias_one = back(0, after(query, mark))
    mark = early_sum.step(d_query_one)
    d_pair_two, d_query_two, d_pos_two, d_bias_two = back(HEADS // 2, after(query, mark))
    (depth_grad,) = tap_sums(after(gated_low, d_query_two), d_normed)
    last_rows = packed_rows(last_columns(width), width, 3 * SMALL)
    outs, packed = half_slots(last_rows, devices)
    last_keep, last_send = call(
        pair_weight_kernel,
        outs,
        [slots, turned, d_query_one, d_query_two, d_pair_one, d_pair_two, d_pos_one, d_pos_two]
        + [d_bias_one, d_bias_two, depth_valid, depth_conv, depth_grad, statistics, bn_grads]
        + [bn_gain_row, late_norms, second_norms, first_norms]
        + list(blocks),
        scratch=[packed, pltpu.VMEM((block_rows(width + SMALL), 4 * width), F32)],
        micros=6.0,
        smem=1,
    )
    last_sum = SlotSum(last_keep, last_send)
    late_sum.join(early_sum)
    both_sum = late_sum
    mark = both_sum.step(last_keep)
    *d_frames, own_grad = call(
        functools.partial(frames_back_kernel, seq_count),
        [struct((width, rows), BF16)] * seq_count + [struct((width, rows), F32)],
        [after(d_pair_one, mark), d_pair_two, d_query_one, d_query_two, w_pair, w_query]
        + [first_grad],
        micros=6.0,
    )
    mark = last_sum.step(own_grad)
    frame_sum = FrameSum([after(part, mark) for part in d_frames])
    mark = both_sum.step(mark)
    mark = last_sum.step(mark)
    frame_sum.step(mark)
    mark = last_sum.step(*frame_sum.joined)
    mark = both_sum.step(mark)
    mark = last_sum.step(mark, *frame_sum.arrived)
    mark = last_sum.step(mark)
    input_grad = frame_sum.finish(own_grad)
    mark = both_sum.step(mark, input_grad)
    both_keep, both_send = both_sum.finish()
    last_keep, last_send = last_sum.finish()
    last_share = share_rows(last_rows, devices) * devices
    square = struct((width, width), F32)
    sum_in, sum_out, sum_conv_in, sum_conv_out, sum_w_out = call(
        finish_two_kernel,
        [struct((width, 2, inner), F32)] * 2 + [struct((2 * width, width), F32), square, square],
        [slots, both_keep, both_send],
        scratch=[late_scratch, early_scratch],
        micros=10.0,
        smem=1,
    )
    sum_qkv, sum_pos, sum_rel, sum_gain, sum_bias, sum_depth = call(
        finish_last_kernel,
        [struct(w_qkv.shape, F32), struct(w_pos.shape, F32), struct(rel_bias.shape, F32)]
        + [struct(norm_gain.shape, F32), struct(norm_bias.shape, F32)]
        + [struct(conv_depth.shape, F32)],
        [slots, last_keep, last_send],
        scratch=[pltpu.VMEM((last_share, LANES), BF16)],
        micros=3.0,
        smem=1,
    )
    return (
        result.T[None],
        input_grad.T[None],
        sum_qkv,
        sum_pos,
        sum_w_out,
        sum_rel,
        sum_in.transpose(1, 0, 2),
        sum_out.transpose(1, 2, 0),
        sum_conv_in.T,
        sum_depth,
        sum_conv_out,
        bn_grads[0],
        bn_grads[1],
        sum_gain,
        sum_bias,
    )


def solution(mesh):
    whole = P()
    split = P("dp", "seq", None)
    return jax.shard_map(
        local,
        mesh=mesh,
        in_specs=(split,) + (whole,) * 13 + (P("dp", None), split),
        out_specs=(split, split) + (whole,) * 13,
        check_vma=False,
    )
```

```python
import functools
import math

import jax
import jax.numpy as jnp
from jax import lax
from jax.experimental import pallas as pl
from jax.experimental.pallas import tpu as pltpu
from jax.sharding import PartitionSpec as P
import numpy as np

HEADS = 4
LANES = 128
WIDE = 3 * LANES
HALO = 16
SMALL = 48
EPS = 1e-05
MODEL_AXES = ("seq", "dp")
VMEM_BYTES = 60 * 1024 * 1024
BF16 = jnp.bfloat16
F32 = jnp.float32


def device_count():
    return lax.axis_size("seq") * lax.axis_size("dp")


def flat_index():
    return lax.axis_index("seq") * lax.axis_size("dp") + lax.axis_index("dp")


def swap_flat(block, distance):
    pairs = [(i, i ^ distance) for i in range(device_count())]
    return lax.ppermute(block, MODEL_AXES, pairs)


def swap_seq(block, distance):
    pairs = [(i, i ^ distance) for i in range(lax.axis_size("seq"))]
    return lax.ppermute(block, "seq", pairs)


def shift_seq(block, step):
    count = lax.axis_size("seq")
    pairs = [(i, i + step) for i in range(count) if 0 <= i + step < count]
    return lax.ppermute(block, "seq", pairs)


def stage_radices(devices):
    radices = [2]
    left = devices // 2
    while left > 1:
        radix = 4 if left % 4 == 0 else 2
        radices.append(radix)
        left = left // radix
    return radices


def slot_pieces(devices):
    slots = jnp.arange(devices, dtype=jnp.int32)
    distance = jnp.zeros((devices,), jnp.int32)
    span = devices
    stride = 1
    for radix in stage_radices(devices):
        span = span // radix
        distance = distance + ((slots // span) % radix) * stride
        stride = stride * radix
    return flat_index() ^ distance


def add_kernel(counts, radix, *refs):
    outs = refs[sum(counts) :]
    start = 0
    row = 0
    for count in counts:
        parts = refs[start : start + count]
        start = start + count
        total = parts[0][...].astype(F32)
        for part in parts[1:]:
            total = total + part[...].astype(F32)
        total = total.astype(BF16)
        span, share = total.shape[0] // radix, total.shape[1]
        for place, out in enumerate(outs):
            out[:, row : row + share] = total[place * span : (place + 1) * span]
        row = row + share


class SlotSum:
    def __init__(self, keep, send):
        self.others = []
        radices = stage_radices(device_count())
        strides = [1]
        for radix in radices[:-1]:
            strides.append(strides[-1] * radix)
        self.stages = list(zip(radices, strides))
        self.next = 1
        self.parts = self.scatter(0, [keep, send])
        self.mark = keep

    def join(self, other):
        self.others.append(other.parts)

    def scatter(self, stage, pieces):
        radix, stride = self.stages[stage]
        return [pieces[0]] + [
            swap_flat(pieces[step], step * stride) for step in range(radix - 1, 0, -1)
        ]

    def spread(self, stage, piece):
        radix, stride = self.stages[stage]
        return [piece] + [swap_flat(piece, step * stride) for step in range(1, radix)]

    def step(self, *earlier):
        count = len(self.stages)
        parts = self.parts
        if self.next >= 2 * count:
            return self.mark
        if earlier:
            parts = [after(parts[0], *earlier)] + parts[1:]
        if self.next <= count:
            radix = self.stages[self.next][0] if self.next < count else 1
            groups = [parts] + self.others
            self.others = []
            slots = parts[0].shape[0]
            if radix == 1:
                total = parts[0].astype(F32)
                for part in parts[1:]:
                    total = total + part.astype(F32)
                self.mark = total.astype(BF16)
                self.parts = self.spread(count - 1, self.mark)
                self.next = self.next + 1
                return self.mark
            share = sum(group[0].shape[1] for group in groups)
            pieces = call(
                functools.partial(add_kernel, [len(group) for group in groups], radix),
                [struct((slots // radix, share, LANES), BF16)] * radix,
                [part for group in groups for part in group],
                micros=2.0,
            )
            self.mark = pieces[0]
            self.parts = self.scatter(self.next, pieces)
        else:
            self.mark = jnp.concatenate(parts, axis=0)
            self.parts = self.spread(2 * count - 1 - self.next, self.mark)
        self.next = self.next + 1
        return self.mark

    def finish(self):
        while self.next < 2 * len(self.stages):
            self.step()
        return self.parts


def exchange_small(spread):
    return lax.all_to_all(spread, MODEL_AXES, 0, 0)


def after(value, *earlier):
    return lax.optimization_barrier((value,) + earlier)[0]


def arrival_order():
    count = lax.axis_size("seq")
    return [0, 1] + list(range(2, count, 2)), list(range(3, count, 2))


def gather_frames(shard, meanwhile):
    count = lax.axis_size("seq")
    across = [shard] + [swap_seq(shard, 2 * step) for step in range(1, count // 2)]
    made = meanwhile()
    blocks = []
    for step, block in enumerate(across):
        blocks.append(block)
        passed = block if step < count // 2 - 1 else after(block, made[0])
        blocks.append(swap_seq(passed, 1))
    return blocks, made


class FrameSum:
    def __init__(self, kept, passed):
        self.kept = kept
        self.passed = [swap_seq(pair, 1) for pair in passed]

    def step(self, *earlier):
        count = len(self.kept)
        self.arrived, self.joined = [], []
        for step in range(count - 1, 0, -1):
            came = self.passed[(count - 1 - step) // 2][(count - 1 - step) % 2]
            joined = self.kept[step].astype(F32) + came.astype(F32)
            if earlier:
                joined = after(joined, *earlier)
            self.joined.append(joined.astype(BF16))
            self.arrived.append(swap_seq(self.joined[-1], 2 * step))

    def finish(self, own):
        total = own + self.kept[0].astype(F32) + self.passed[-1][1].astype(F32)
        for block in self.arrived:
            total = total + block.astype(F32)
        return total


def cost(micros):
    return pl.CostEstimate(flops=int(micros * 0.460e9), bytes_accessed=0, transcendentals=0)


def call(body, outs, args, scratch=(), micros=2.0, smem=0):
    specs = [
        pl.BlockSpec(memory_space=pltpu.SMEM if place < smem else pltpu.VMEM)
        for place in range(len(args))
    ]
    return pl.pallas_call(
        body,
        out_shape=tuple(outs),
        in_specs=specs,
        out_specs=tuple(pl.BlockSpec(memory_space=pltpu.VMEM) for _ in outs),
        scratch_shapes=list(scratch),
        compiler_params=pltpu.CompilerParams(vmem_limit_bytes=VMEM_BYTES),
        cost_estimate=cost(micros),
    )(*args)


def struct(shape, dtype):
    return jax.ShapeDtypeStruct(tuple(shape), dtype)


def nn(left, right):
    return lax.dot_general(left, right, (((1,), (0,)), ((), ())), preferred_element_type=F32)


def nt(left, right):
    return lax.dot_general(left, right, (((1,), (1,)), ((), ())), preferred_element_type=F32)


def tn(left, right):
    return lax.dot_general(left, right, (((0,), (0,)), ((), ())), preferred_element_type=F32)


def norm_parts(summed):
    average = jnp.mean(summed, axis=-1, keepdims=True)
    centered = summed - average
    variance = jnp.mean(centered * centered, axis=-1, keepdims=True)
    inverse = lax.rsqrt(variance + EPS)
    return centered * inverse, inverse


def norm_back(unit, inverse, gain, incoming):
    scaled = incoming * gain
    first = jnp.mean(scaled, axis=-1, keepdims=True)
    second = jnp.mean(scaled * unit, axis=-1, keepdims=True)
    grad = inverse * (scaled - first - unit * second)
    return (
        grad,
        jnp.sum(incoming * unit, axis=0, keepdims=True),
        jnp.sum(incoming, axis=0, keepdims=True),
    )


def sigmoid(value):
    return 1.0 / (1.0 + jnp.exp(-value))


def silu_back(value):
    gate = sigmoid(value)
    return gate * (1.0 + value * (1.0 - gate))


def store_tile(ref, rows, copies):
    tile = jnp.zeros((8, LANES), F32)
    parts = []
    for row in rows:
        width = row.shape[1]
        blocks = -(-width // LANES)
        wide = row
        if blocks * LANES > width:
            wide = jnp.concatenate([row, jnp.zeros((1, blocks * LANES - width), F32)], axis=1)
        for block in range(blocks):
            parts.append(wide[:, block * LANES : (block + 1) * LANES])
    for place, part in enumerate(parts):
        tile = jnp.where(
            lax.broadcasted_iota(jnp.int32, (8, LANES), 0) == place,
            jnp.broadcast_to(part, (8, LANES)),
            tile,
        )
    ref[...] = jnp.broadcast_to(tile[None], (copies, 8, LANES))


def tile_row(tile, place, width):
    blocks = -(-width // LANES)
    parts = [tile[place * blocks + block : place * blocks + block + 1] for block in range(blocks)]
    return jnp.concatenate(parts, axis=1)[:, :width]


def plan_blocks(columns):
    runs = []
    block = 0
    for count in columns:
        full = count // LANES
        runs.append([(block + place, 0, place * LANES, LANES) for place in range(full)])
        block = block + full
    open_block, lane = None, LANES
    for place, count in enumerate(columns):
        rest = count % LANES
        if rest:
            if lane + rest > LANES:
                open_block, lane = block, 0
                block = block + 1
            runs[place].append((open_block, lane, count - rest, rest))
            lane = lane + rest
    return runs, block


def block_rows(rows):
    return -(-rows // 8) * 8


def store_matrix(packed, runs, value):
    rows = value.shape[0]
    low = value.astype(BF16)
    for block, lane, column, count in runs:
        start = block * block_rows(rows)
        packed[start : start + rows, lane : lane + count] = low[:, column : column + count]


def load_matrix(packed, runs, out, rows, row=0):
    for block, lane, column, count in runs:
        start = block * block_rows(rows)
        out[row : row + rows, column : column + count] = packed[
            start : start + rows, lane : lane + count
        ].astype(F32)


def load_layer(packed, runs, out, layer):
    rows = out.shape[0]
    for block, lane, column, count in runs:
        start = block * block_rows(rows)
        out[:, layer, column : column + count] = packed[
            start : start + rows, lane : lane + count
        ].astype(F32)


def spread_pieces(slots_ref, packed, keep_ref, send_ref):
    half, share = keep_ref.shape[:2]

    def one(slot, nothing):
        low = pl.multiple_of(slots_ref[slot] * share, HALO)
        keep_ref[slot] = packed[pl.ds(low, share), :]
        high = pl.multiple_of(slots_ref[slot + half] * share, HALO)
        send_ref[slot] = packed[pl.ds(high, share), :]
        return nothing

    lax.fori_loop(0, half, one, 0)


def collect_pieces(slots_ref, keep_ref, send_ref, packed, row=0):
    half = keep_ref.shape[0]
    share = packed.shape[0] // (2 * half)

    def one(slot, nothing):
        low = pl.multiple_of(slots_ref[slot] * share, HALO)
        packed[pl.ds(low, share), :] = keep_ref[slot, row : row + share]
        high = pl.multiple_of(slots_ref[slot + half] * share, HALO)
        packed[pl.ds(high, share), :] = send_ref[slot, row : row + share]
        return nothing

    lax.fori_loop(0, half, one, 0)


def share_rows(rows, devices):
    return -(-rows // (HALO * devices)) * HALO


def half_slots(rows, devices):
    share = share_rows(rows, devices)
    return [struct((devices // 2, share, LANES), BF16)] * 2, pltpu.VMEM((devices * share, LANES), BF16)


def wave_tables(rows, blocks, width):
    half = width // 2
    frequency = np.exp(np.arange(half) * (-2.0 * math.log(10000.0) / width))
    tail = np.zeros(LANES // 2)
    tail[: half - LANES] = frequency[LANES:]
    lanes = np.concatenate([frequency[:LANES], frequency[:LANES], tail, tail])[None]
    row_angles = np.arange(rows)[:, None] * lanes
    block_angles = (np.arange(blocks) * rows)[:, None] * lanes
    return [
        jnp.asarray(table.astype(np.float32))
        for table in (
            np.cos(row_angles),
            np.sin(row_angles),
            np.cos(block_angles),
            np.sin(block_angles),
        )
    ]


def half_pieces(width):
    half = width // 2
    rest = half - LANES
    return (
        (0, 0, LANES),
        (half, LANES, LANES),
        (LANES, 2 * LANES, rest),
        (half + LANES, 2 * LANES + LANES // 2, rest),
    )


def half_sign():
    lane = lax.broadcasted_iota(jnp.int32, (1, LANES), 1)
    return jnp.where(lane < LANES // 2, 1.0, -1.0)


def prepare_kernel(orders, where, lengths, turned, w_qkv, w_pos, w_out, bias, depth, base_cos, base_sin, block_cos, block_sin, block, query, shift, w_query, w_pair, w_pos_wide, w_out_wide, depth_wide, own_cos, own_sin, clip_rows, clip_wide, valid_wide, *by_order):
    place = where[0]
    width, rows = turned.shape
    size = width // HEADS
    blocks = block_cos.shape[0]
    w_query[...] = jnp.zeros_like(w_query)
    w_pair[...] = jnp.zeros_like(w_pair)
    w_pos_wide[...] = jnp.zeros_like(w_pos_wide)
    w_out_wide[...] = jnp.zeros_like(w_out_wide)
    depth_wide[...] = jnp.zeros_like(depth_wide)
    depth_wide[:, :width] = depth[...]
    for head in range(HEADS):
        natural = slice(head * size, (head + 1) * size)
        low = head * LANES
        w_query[:, low : low + size] = w_qkv[:, head * size : (head + 1) * size]
        w_pair[head, :, :size] = w_qkv[:, width + head * size : width + (head + 1) * size]
        w_pair[head, :, LANES : LANES + size] = w_qkv[
            :, 2 * width + head * size : 2 * width + (head + 1) * size
        ]
        w_out_wide[low : low + size] = w_out[natural]
        for source, target, length in half_pieces(width):
            w_pos_wide[target : target + length, low : low + size] = w_pos[
                source : source + length, natural
            ]
    lane = lax.broadcasted_iota(jnp.int32, (1, WIDE), 1)
    on_cosine = (lane < LANES) | ((lane >= 2 * LANES) & (lane < 2 * LANES + LANES // 2))
    row_cos, row_sin = base_cos[...], base_sin[...]
    ends = [lengths[0, 0]]
    for clip in range(1, lengths.shape[1]):
        ends.append(ends[-1] + lengths[0, clip])

    def clip_at(frames):
        clip = jnp.zeros_like(frames)
        for end in ends:
            clip = clip + (frames >= end).astype(jnp.int32)
        return clip

    for order, table, clip_columns in zip(orders, by_order[0::2], by_order[1::2]):
        for step, distance in enumerate(order):
            here = place ^ distance
            cosine = block_cos[pl.ds(here, 1), :]
            sine = block_sin[pl.ds(here, 1), :]
            one = jnp.where(on_cosine, cosine, sine)
            two = jnp.where(on_cosine, -sine, cosine)
            lanes = slice(step * rows, (step + 1) * rows)
            table[:, lanes] = (one * row_cos + two * row_sin).astype(BF16).T
            clip_columns[:, lanes] = clip_at(
                here * rows + lax.broadcasted_iota(jnp.int32, (1, rows), 1)
            )
    reached = place * rows - HALO + lax.broadcasted_iota(jnp.int32, (rows + 2 * HALO, LANES), 0)
    inside = (reached >= 0) & (reached < blocks * rows)
    reached_clip = jnp.where(inside, clip_at(reached), -1)
    clip_wide[...] = reached_clip
    clip_rows[...] = reached_clip[HALO : HALO + rows, 0:1]
    valid_wide[...] = (inside & (reached < ends[-1])).astype(F32)[:, 0:1]
    block_cosine = block_cos[pl.ds(place, 1), :]
    block_sine = block_sin[pl.ds(place, 1), :]
    cosines = block_cosine * row_cos - block_sine * row_sin
    sines = block_sine * row_cos + block_cosine * row_sin
    own_cos[...] = cosines
    own_sin[...] = sines
    frames = turned[...].T
    block[...] = frames
    projected = nn(frames, w_query[...])
    sign = half_sign()
    for head in range(HEADS):
        lanes = slice(head * LANES, (head + 1) * LANES)
        natural = slice(head * size, (head + 1) * size)
        wide = jnp.zeros((2, LANES - size), F32)
        added = jnp.concatenate([bias[:, natural], wide], axis=1)
        unit = (projected[:, lanes] + added[0:1]).astype(BF16)
        moved = (projected[:, lanes] + added[1:2]).astype(BF16)
        shift[:, lanes] = moved
        shifted = nt(moved, w_pos_wide[:, lanes])
        first, second = shifted[:, :LANES], shifted[:, LANES : 2 * LANES]
        tail = shifted[:, 2 * LANES :]
        sine, cosine = sines[:, :LANES], cosines[:, :LANES]
        query[head, :, :LANES] = unit
        query[head, :, LANES : 2 * LANES] = (first * sine + second * cosine).astype(BF16)
        query[head, :, 2 * LANES : 3 * LANES] = (second * sine - first * cosine).astype(BF16)
        query[head, :, 3 * LANES :] = (
            tail * sines[:, 2 * LANES :]
            + pltpu.roll(tail, LANES // 2, 1) * cosines[:, 2 * LANES :] * sign
        ).astype(BF16)


def masked_scores(query, upper, table, clip_rows, clip_columns, scale):
    raw = nn(query[:, : 2 * LANES], upper) + nn(query[:, 2 * LANES :], table[LANES:])
    return jnp.where(clip_rows == clip_columns, raw * (scale / math.log(2.0)), -1e30)


def attend_kernel(scale, count, last, *refs):
    blocks = refs[:count]
    query, w_pair, table, clip_rows, clip_columns = refs[count : count + 5]
    carried = refs[count + 5 : count + 8] if last else None
    outs = refs[count + (8 if last else 5) :]
    rows = blocks[0].shape[1]
    frames_all, pair = outs[-2:]

    @pl.when(pl.program_id(0) == 0)
    def _():
        for step in range(count):
            frames_all[:, step * rows : (step + 1) * rows] = blocks[step][...]

    both = tn(w_pair[0], frames_all[...]).astype(BF16)
    pair[0] = both
    upper = jnp.concatenate([both[:LANES], table[:LANES]], axis=0)
    scores = masked_scores(
        query[0], upper, table[...], clip_rows[...], clip_columns[...], scale
    )
    highest = jnp.max(scores, axis=1, keepdims=True)
    if last:
        highest = jnp.maximum(highest, carried[0][0])
    weights = jnp.exp2(scores - highest)
    total = jnp.sum(weights, axis=1, keepdims=True)
    summed = nt(weights.astype(BF16), both[LANES:])
    if last:
        fade = jnp.exp2(carried[0][0] - highest)
        total = total + carried[1][0] * fade
        summed = summed + carried[2][...] * fade
        attended, log_total = outs[:2]
        attended[...] = summed / total
        log_total[0] = highest + jnp.log2(total)
    else:
        outs[0][0] = highest
        outs[1][0] = total
        outs[2][...] = summed


def attend(blocks, query, w_pair, table, clip_rows, clip_columns, head_width, carried=()):
    rows = query.shape[1]
    frames = table.shape[1]
    width = w_pair.shape[1]
    stat = pl.BlockSpec((1, rows, 1), lambda h: (h, 0, 0))
    head = pl.BlockSpec((rows, LANES), lambda h: (0, h))
    stat_shape = struct((HEADS, rows, 1), F32)
    head_shape = struct((rows, HEADS * LANES), F32)
    last = len(carried) > 0
    return pl.pallas_call(
        functools.partial(attend_kernel, 1.0 / math.sqrt(head_width), len(blocks), last),
        grid=(HEADS,),
        in_specs=[pl.BlockSpec((width, rows), lambda h: (0, 0)) for _ in blocks]
        + [
            pl.BlockSpec((1, rows, 4 * LANES), lambda h: (h, 0, 0)),
            pl.BlockSpec((1, width, 2 * LANES), lambda h: (h, 0, 0)),
            pl.BlockSpec((WIDE, frames), lambda h: (0, 0)),
            pl.BlockSpec((rows, 1), lambda h: (0, 0)),
            pl.BlockSpec((1, frames), lambda h: (0, 0)),
        ]
        + ([stat, stat, head] if last else []),
        out_specs=((head, stat) if last else (stat, stat, head))
        + (
            pl.BlockSpec((width, frames), lambda h: (0, 0)),
            pl.BlockSpec((1, 2 * LANES, frames), lambda h: (h, 0, 0)),
        ),
        out_shape=((head_shape, stat_shape) if last else (stat_shape, stat_shape, head_shape))
        + (struct((width, frames), BF16), struct((HEADS, 2 * LANES, frames), BF16)),
        compiler_params=pltpu.CompilerParams(vmem_limit_bytes=VMEM_BYTES),
        cost_estimate=cost(5.0 if last else 8.0),
    )(*blocks, query, w_pair, table, clip_rows, clip_columns, *carried)


def early_kernel(block, attended, w_out, gains, biases, ffn_in, ffn_out, gates, first_sum, second_sum, second_norm, left, right, gated, attended_low):
    low = attended[...].astype(BF16)
    attended_low[...] = low
    summed = block[...].astype(F32) + nn(low, w_out[...])
    first_sum[...] = summed
    unit, _ = norm_parts(summed)
    first = unit * gains[0:1] + biases[0:1]
    inner = nn(first.astype(BF16), ffn_in[...])
    act = (inner * sigmoid(inner)).astype(BF16)
    summed = first + nt(act, ffn_out[...])
    second_sum[...] = summed
    unit, _ = norm_parts(summed)
    second = unit * gains[1:2] + biases[1:2]
    second_norm[...] = second
    second_low = second.astype(BF16)
    half = gates.shape[0] // 2
    one = nt(second_low, gates[:half])
    two = nt(second_low, gates[half:])
    left[...] = one
    right[...] = two
    gated[...] = jnp.zeros_like(gated)
    gated[:, : one.shape[1]] = (one * sigmoid(two)).astype(BF16)


def again_kernel(first_sum, second_sum, gains, biases, ffn_in, first_low_out, second_low_out, act_out, slope_out):
    unit, _ = norm_parts(second_sum[...])
    second_low_out[...] = (unit * gains[1:2] + biases[1:2]).astype(BF16)
    unit, _ = norm_parts(first_sum[...])
    first_low = (unit * gains[0:1] + biases[0:1]).astype(BF16)
    first_low_out[...] = first_low
    inner = nn(first_low, ffn_in[...])
    gate = sigmoid(inner)
    act_out[...] = (inner * gate).astype(BF16)
    slope_out[...] = (gate * (1.0 + inner * (1.0 - gate))).astype(BF16)


def lane_blocks(width):
    return [(lane, min(LANES, width - lane)) for lane in range(0, width, LANES)]


def extend(extended, low, middle, high):
    rows, width = middle.shape
    for block, (lane, count) in enumerate(lane_blocks(width)):
        if count < LANES:
            extended[block] = jnp.zeros((rows + 2 * HALO, LANES), F32)
        extended[block, 0:HALO, :count] = low[:, lane : lane + count].astype(F32)
        extended[block, HALO : HALO + rows, :count] = middle[:, lane : lane + count].astype(F32)
        extended[block, HALO + rows :, :count] = high[:, lane : lane + count].astype(F32)


def convolve(extended, clip, depth, mirrored, store):
    taps = depth.shape[0]
    blocks, rows, _ = extended.shape
    rows = rows - 2 * HALO
    step = 64
    for start in range(0, rows, step):
        own = clip[HALO + start : HALO + start + step]
        sums = [jnp.zeros((step, LANES), F32) for _ in range(blocks)]
        for tap in range(taps):
            place = HALO - taps // 2 + tap + start
            same = clip[place : place + step] == own
            row = taps - 1 - tap if mirrored else tap
            for block in range(blocks):
                lanes = slice(block * LANES, (block + 1) * LANES)
                sums[block] = sums[block] + depth[row : row + 1, lanes] * jnp.where(
                    same, extended[block, place : place + step], 0.0
                )
        store(start, step, jnp.concatenate(sums, axis=1))


def conv_kernel(copies, low, middle, high, clip, depth, valid, convolved, tile, extended):
    rows, width = convolved.shape
    extend(extended, low[...], middle[...], high[...])

    def store(start, step, value):
        convolved[start : start + step] = value[:, :width]

    convolve(extended, clip, depth, False, store)
    value = convolved[...]
    kept = value * valid[...]
    count = jnp.zeros((1, width), F32) + jnp.sum(valid[...], axis=0, keepdims=True)
    store_tile(
        tile,
        [
            jnp.sum(kept, axis=0, keepdims=True),
            jnp.sum(kept * value, axis=0, keepdims=True),
            count[:, :LANES],
        ],
        copies,
    )


def taps_kernel(taps, count, low, middle, high, clip, *refs):
    factor, *valid = refs[: 1 if count == 1 else 2]
    outs, extended = refs[len(valid) + 1 : -1], refs[-1]
    rows, width = factor.shape
    extend(extended, low[...], middle[...], high[...])
    step = 64
    sums = [[[None] * 3 for _ in range(taps)] for _ in range(count)]
    for start in range(0, rows, step):
        own = clip[HALO + start : HALO + start + step]
        for block, (lane, lanes) in enumerate(lane_blocks(width)):
            part = factor[start : start + step, lane : lane + lanes]
            if lanes < LANES:
                part = jnp.concatenate([part, jnp.zeros((step, LANES - lanes), F32)], axis=1)
            here = [part]
            if valid:
                kept = valid[0][start : start + step]
                here = [jnp.broadcast_to(kept, (step, LANES)), part * kept]
            for tap in range(taps):
                place = HALO - taps // 2 + tap + start
                same = clip[place : place + step] == own
                there = jnp.where(same, extended[block, place : place + step], 0.0)
                for which in range(count):
                    part = jnp.sum((there * here[which]).reshape(step // 8, 8, LANES), axis=0)
                    old = sums[which][tap][block]
                    sums[which][tap][block] = part if old is None else old + part
    for which in range(count):
        for tap in range(taps):
            outs[which][tap : tap + 1] = jnp.concatenate(
                [jnp.sum(part, axis=0, keepdims=True) for part in sums[which][tap]], axis=1
            )[:, :width]


def late_kernel(copies, arrived, convolved, second_norm, bn_gain, bn_bias, conv_out, gains, biases, ffn_in, ffn_out, cotangent, result, act_out, d_inner_out, third_low_out, fourth_grad_out, swished_out, third_grad_out, third_grad, d_normed_out, unit_out, tile, norm_grads, statistics, edge_low, edge_high):
    width = convolved.shape[1]
    rows = convolved.shape[0]
    sums = jnp.sum(arrived[...], axis=0)
    frames = sums[6:7, 0:1]
    mean = tile_row(sums, 0, width) / frames
    variance = tile_row(sums, 1, width) / frames - mean * mean
    inverse = lax.rsqrt(variance + EPS)
    unit = (convolved[...] - mean) * inverse
    unit_out[...] = unit
    statistics[...] = jnp.zeros_like(statistics)
    statistics[0:1, :width] = inverse
    statistics[1:2, :width] = jnp.broadcast_to(frames, (1, width))
    statistics[2:3, :width] = mean
    normed = unit * bn_gain[...] + bn_bias[...]
    swished = (normed * sigmoid(normed)).astype(BF16)
    swished_out[...] = swished
    third_unit, third_inverse = norm_parts(second_norm[...] + nn(swished, conv_out[...]))
    third = third_unit * gains[2:3] + biases[2:3]
    third_low = third.astype(BF16)
    third_low_out[...] = third_low
    inner = nn(third_low, ffn_in[...])
    gate = sigmoid(inner)
    act = (inner * gate).astype(BF16)
    act_out[...] = act
    fourth_unit, fourth_inverse = norm_parts(third + nt(act, ffn_out[...]))
    result[...] = (fourth_unit * gains[3:4] + biases[3:4]).T
    fourth_grad, gain_three, bias_three = norm_back(
        fourth_unit, fourth_inverse, gains[3:4], cotangent[...].T
    )
    fourth_low = fourth_grad.astype(BF16)
    fourth_grad_out[...] = fourth_low
    d_act = nn(fourth_low, ffn_out[...])
    d_inner = (d_act * (gate * (1.0 + inner * (1.0 - gate)))).astype(BF16)
    d_inner_out[...] = d_inner
    grad, gain_two, bias_two = norm_back(
        third_unit, third_inverse, gains[2:3], fourth_grad + nt(d_inner, ffn_in[...])
    )
    third_grad[...] = grad
    grad_low = grad.astype(BF16)
    third_grad_out[...] = grad_low
    d_normed = nt(grad_low, conv_out[...]) * silu_back(normed)
    d_normed_out[...] = d_normed
    store_tile(
        tile,
        [
            jnp.sum(d_normed * unit, axis=0, keepdims=True),
            jnp.sum(d_normed, axis=0, keepdims=True),
        ],
        copies,
    )
    norm_grads[0:1] = gain_two
    norm_grads[1:2] = gain_three
    norm_grads[2:3] = bias_two
    norm_grads[3:4] = bias_three
    edge_low[0] = d_normed[:HALO]
    edge_low[1] = unit[:HALO]
    edge_high[0] = d_normed[rows - HALO :]
    edge_high[1] = unit[rows - HALO :]


def late_columns(width, inner):
    return (inner, inner, width)


def early_columns(width, inner):
    return (inner, inner, width, width, width)


def last_columns(width):
    return (3 * width, width)


def packed_rows(columns, width, small=0):
    _, blocks = plan_blocks(columns)
    return blocks * block_rows(width) + small


def late_grads_kernel(slots, third_low, d_inner, act, fourth_grad, swished, third_grad, keep, send, packed):
    width = third_low.shape[1]
    runs, _ = plan_blocks(late_columns(width, act.shape[1]))
    store_matrix(packed, runs[0], tn(third_low[...], d_inner[...]))
    store_matrix(packed, runs[1], tn(fourth_grad[...], act[...]))
    store_matrix(packed, runs[2], tn(swished[...], third_grad[...]))
    spread_pieces(slots, packed, keep, send)


def middle_kernel(slots, arrived, statistics, bn_gain, d_normed, unit, from_low, from_high, clip, valid, depth, left, right, gates, third_grad, second_sum, gains, slope, first_sum, ffn_in, ffn_out, w_out, attended, first_low, second_low, act, attended_low, first_grad, d_attended, delta, norm_grads, bn_grads, keep, send, extended, d_gated, packed):
    rows, width = left.shape
    sums = jnp.sum(arrived[...], axis=0)
    gain_sum = tile_row(sums, 0, width)
    bias_sum = tile_row(sums, 1, width)
    bn_grads[0:1] = gain_sum
    bn_grads[1:2] = bias_sum
    gain = bn_gain[...]
    inverse = statistics[0:1, :width]
    frames = statistics[1:2, :width]

    def conv_grad(d_rows, unit_rows, valid_rows):
        return (
            inverse * gain * (d_rows - valid_rows * (bias_sum + unit_rows * gain_sum) / frames)
        ).astype(BF16)

    extend(
        extended,
        conv_grad(from_low[0], from_low[1], valid[0:HALO]),
        conv_grad(d_normed[...], unit[...], valid[HALO : HALO + rows]),
        conv_grad(from_high[0], from_high[1], valid[HALO + rows :]),
    )

    def store(start, step, value):
        d_gated[start : start + step] = value[:, :width]

    convolve(extended, clip, depth, True, store)
    gate = sigmoid(right[...])
    d_left = (d_gated[...] * gate).astype(BF16)
    d_right = (d_gated[...] * left[...] * gate * (1.0 - gate)).astype(BF16)
    second_unit, second_inverse = norm_parts(second_sum[...])
    half = gates.shape[0] // 2
    incoming = third_grad[...] + nn(d_left, gates[:half]) + nn(d_right, gates[half:])
    second_grad, gain_one, bias_one = norm_back(
        second_unit, second_inverse, gains[1:2], incoming
    )
    second_grad_low = second_grad.astype(BF16)
    d_act = nn(second_grad_low, ffn_out[...])
    d_inner = (d_act * slope[...].astype(F32)).astype(BF16)
    first_unit, first_inverse = norm_parts(first_sum[...])
    grad, gain_zero, bias_zero = norm_back(
        first_unit, first_inverse, gains[0:1], second_grad + nt(d_inner, ffn_in[...])
    )
    first_grad[...] = grad
    grad_low = grad.astype(BF16)
    for place, part in enumerate((gain_zero, gain_one, bias_zero, bias_one)):
        norm_grads[place : place + 1] = part
    back = nt(grad_low, w_out[...]).astype(BF16)
    d_attended[...] = back
    product = back.astype(F32) * attended[...]
    for head in range(HEADS):
        delta[head] = jnp.sum(
            product[:, head * LANES : (head + 1) * LANES], axis=1, keepdims=True
        )
    size = width // HEADS
    runs, _ = plan_blocks(early_columns(width, act.shape[1]))
    store_matrix(packed, runs[0], tn(first_low[...], d_inner))
    store_matrix(packed, runs[1], tn(second_grad_low, act[...]))
    store_matrix(packed, runs[2], tn(d_left, second_low[...]))
    store_matrix(packed, runs[3], tn(d_right, second_low[...]))
    d_out = tn(attended_low[...], grad_low)
    store_matrix(
        packed,
        runs[4],
        jnp.concatenate([d_out[head * LANES : head * LANES + size] for head in range(HEADS)], axis=0),
    )
    spread_pieces(slots, packed, keep, send)


def attend_back_kernel(scale, counts, query, pair_one, pair_two, table_one, table_two, clip_rows, clip_one, clip_two, frames_one, frames_two, log_total, delta, d_attended, shift, w_pos, w_query, w_pair, own_cos, own_sin, turned, first_grad, *refs):
    blocks = sum(counts)
    kept, passed = refs[: blocks // 2], refs[blocks // 2 : blocks // 2 + blocks // 4]
    d_pair_weight, d_query_weight, d_pos_weight, d_bias, own_grad, d_frames, d_pair, own_sum = refs[
        blocks // 2 + blocks // 4 :
    ]
    head = pl.program_id(0)
    rows = clip_rows.shape[0]
    d_head = d_attended[...]
    query_turned = query[0, :, :LANES].T
    d_head_turned = d_head.T
    unit_sum = jnp.zeros((rows, 2 * LANES), F32)
    rest_sum = jnp.zeros((rows, 2 * LANES), F32)
    runs = (
        (pair_one, table_one, clip_one, frames_one),
        (pair_two, table_two, clip_two, frames_two),
    )
    start = 0
    weight_sum = None
    pieces = []
    for run in runs:
        for low in range(0, run[3].shape[1], 5 * rows):
            pieces.append((run, low, min(5 * rows, run[3].shape[1] - low)))
    for (pair, table, clip_columns, frames), low, length in pieces:
        here = slice(low, low + length)
        span = slice(start, start + length)
        start = start + length
        upper = jnp.concatenate([pair[0, :LANES, here], table[:LANES, here]], axis=0)
        scores = masked_scores(
            query[0], upper, table[:, here], clip_rows[...], clip_columns[:, here], scale
        )
        probs = jnp.exp2(scores - log_total[0])
        slope = nn(d_head, pair[0, LANES:, here])
        d_raw = (probs * (slope * scale - delta[0] * scale)).astype(BF16)
        d_pair[:LANES, span] = nn(query_turned, d_raw).astype(BF16)
        d_pair[LANES:, span] = nn(d_head_turned, probs.astype(BF16)).astype(BF16)
        unit_sum = unit_sum + nt(d_raw, upper)
        rest_sum = rest_sum + nt(d_raw, table[LANES:, here])
        part = nt(frames[:, here], d_pair[:, span])
        weight_sum = part if weight_sum is None else weight_sum + part
        by_frame = nn(w_pair[0], d_pair[:, span])

        @pl.when(head == 0)
        def _():
            d_frames[:, span] = by_frame

        @pl.when(head > 0)
        def _():
            d_frames[:, span] += by_frame

    d_pair_weight[0] = weight_sum.astype(BF16)
    d_unit = unit_sum[:, :LANES]
    first, second = unit_sum[:, LANES:], rest_sum[:, :LANES]
    tail = rest_sum[:, LANES:]
    cosines, sines = own_cos[...], own_sin[...]
    sine, cosine = sines[:, :LANES], cosines[:, :LANES]
    d_shifted = jnp.concatenate(
        [
            first * sine - second * cosine,
            first * cosine + second * sine,
            tail * sines[:, 2 * LANES :]
            - pltpu.roll(tail, LANES // 2, 1) * cosines[:, 2 * LANES :] * half_sign(),
        ],
        axis=1,
    ).astype(BF16)
    d_from_pos = nn(d_shifted, w_pos[...])
    d_query = (d_unit + d_from_pos).astype(BF16)
    d_query_weight[...] = nn(turned[...], d_query).astype(BF16)
    d_pos_weight[...] = tn(d_shifted, shift[...]).astype(BF16)
    d_bias[0:1] = jnp.sum(d_unit, axis=0, keepdims=True)
    d_bias[1:2] = jnp.sum(d_from_pos, axis=0, keepdims=True)
    own = nt(d_query, w_query[...])

    @pl.when(head == 0)
    def _():
        own_sum[...] = first_grad[...] + own

    @pl.when(head > 0)
    def _():
        own_sum[...] += own

    @pl.when(head == HEADS - 1)
    def _():
        own_grad[...] = own_sum[...].T
        orders = [0, 1] + list(range(2, blocks, 2)) + list(range(3, blocks, 2))
        for step in range(blocks // 2):
            lanes = orders.index(2 * step) * rows
            kept[step][...] = d_frames[:, lanes : lanes + rows].astype(BF16)
            lanes = orders.index(2 * step + 1) * rows
            place = blocks // 2 - 1 - step
            passed[place // 2][place % 2] = d_frames[:, lanes : lanes + rows].astype(BF16)


def attend_back(counts, query, pairs, tables, clip_rows, clips, frames, log_total, delta, d_attended, shift, w_pos, w_query, w_pair, own_cos, own_sin, turned, first_grad, head_width):
    rows = query.shape[1]
    width = turned.shape[0]
    wide = HEADS * LANES
    blocks = sum(counts)
    total = blocks * rows

    def whole(array):
        return pl.BlockSpec(
            array.shape, lambda h: (0,) * len(array.shape), pipeline_mode=pl.Buffered(1)
        )

    def by_head(array):
        return pl.BlockSpec((1,) + array.shape[1:], lambda h: (h, 0, 0))

    def head_lanes(array):
        return pl.BlockSpec((array.shape[0], LANES), lambda h: (0, h))

    kept = [struct((width, rows), BF16)] * (blocks // 2)
    passed = [struct((2, width, rows), BF16)] * (blocks // 4)
    by_head_shapes = [struct((HEADS, width, 2 * LANES), BF16)]
    by_lane_shapes = [struct((width, wide), BF16), struct((WIDE, wide), BF16), struct((2, wide), F32)]
    own = struct((width, rows), F32)
    return pl.pallas_call(
        functools.partial(attend_back_kernel, 1.0 / math.sqrt(head_width), counts),
        grid=(HEADS,),
        in_specs=[by_head(query)]
        + [by_head(pair) for pair in pairs]
        + [whole(table) for table in tables]
        + [whole(clip_rows)]
        + [whole(clip) for clip in clips]
        + [whole(part) for part in frames]
        + [by_head(log_total), by_head(delta), head_lanes(d_attended), head_lanes(shift)]
        + [head_lanes(w_pos), head_lanes(w_query), by_head(w_pair), whole(own_cos)]
        + [whole(own_sin), whole(turned), whole(first_grad)],
        out_specs=tuple(whole(shape) for shape in kept + passed)
        + tuple(by_head(shape) for shape in by_head_shapes)
        + tuple(head_lanes(shape) for shape in by_lane_shapes)
        + (whole(own),),
        out_shape=tuple(kept + passed + by_head_shapes + by_lane_shapes + [own]),
        scratch_shapes=[
            pltpu.VMEM((width, total), F32),
            pltpu.VMEM((2 * LANES, total), BF16),
            pltpu.VMEM((rows, width), F32),
        ],
        compiler_params=pltpu.CompilerParams(vmem_limit_bytes=VMEM_BYTES),
        cost_estimate=cost(20.0),
    )(query, *pairs, *tables, clip_rows, *clips, *frames, log_total, delta, d_attended, shift, w_pos, w_query, w_pair, own_cos, own_sin, turned, first_grad)


def last_pack_kernel(slots, d_query_weight, d_pair_weight, d_pos, d_bias, depth_valid, depth_conv, depth_grad, statistics, bn_grads, bn_gain, late_norms, early_norms, keep, send, packed, natural):
    width = d_query_weight.shape[0]
    size = width // HEADS
    runs, total = plan_blocks(last_columns(width))
    for head in range(HEADS):
        lanes = slice(head * size, (head + 1) * size)
        low = head * LANES
        natural[:width, lanes] = d_query_weight[:, low : low + size].astype(F32)
        natural[:width, width + head * size : width + (head + 1) * size] = d_pair_weight[
            head, :, :size
        ].astype(F32)
        natural[:width, 2 * width + head * size : 2 * width + (head + 1) * size] = d_pair_weight[
            head, :, LANES : LANES + size
        ].astype(F32)
        for start, spread, length in half_pieces(width):
            natural[start : start + length, 3 * width + head * size : 3 * width + (head + 1) * size] = (
                d_pos[spread : spread + length, low : low + size].astype(F32)
            )
        natural[width : width + 2, lanes] = d_bias[:, low : low + size]
    taps = depth_valid.shape[0]
    inverse, frames, mean = (statistics[row : row + 1, :width] for row in range(3))
    gain_sum, bias_sum = bn_grads[0:1], bn_grads[1:2]
    by_unit = (depth_conv[...] - mean * depth_valid[...]) * inverse
    d_depth = (
        inverse
        * bn_gain[...]
        * (depth_grad[...] - (bias_sum * depth_valid[...] + gain_sum * by_unit) / frames)
    )
    natural[width + 2 : width + 6, :width] = early_norms[...]
    natural[width + 6 : width + 10, :width] = late_norms[...]
    natural[width + 10 : width + 10 + taps, :width] = d_depth
    store_matrix(packed, runs[0], natural[:width, : 3 * width])
    store_matrix(packed, runs[1], natural[:width, 3 * width :])
    start = total * block_rows(width)
    for lane in range(0, width, LANES):
        count = min(LANES, width - lane)
        packed[start : start + 10 + taps, :count] = natural[
            width : width + 10 + taps, lane : lane + count
        ].astype(BF16)
        start = start + SMALL
    spread_pieces(slots, packed, keep, send)


def finish_two_kernel(slots, keep, send, ffn_in, ffn_out, conv_in, conv_out, w_out, late, early):
    width, _, inner = ffn_in.shape
    share = late.shape[0] // (2 * keep.shape[0])
    collect_pieces(slots, keep, send, late)
    collect_pieces(slots, keep, send, early, share)
    late_runs, _ = plan_blocks(late_columns(width, inner))
    early_runs, _ = plan_blocks(early_columns(width, inner))
    for place, out in enumerate((ffn_in, ffn_out)):
        load_layer(early, early_runs[place], out, 0)
        load_layer(late, late_runs[place], out, 1)
    load_matrix(late, late_runs[2], conv_out, width)
    load_matrix(early, early_runs[2], conv_in, width)
    load_matrix(early, early_runs[3], conv_in, width, width)
    load_matrix(early, early_runs[4], w_out, width)


def finish_last_kernel(slots, keep, send, w_qkv, w_pos, d_bias, gains, biases, d_depth, packed):
    width = w_pos.shape[1]
    collect_pieces(slots, keep, send, packed)
    runs, total = plan_blocks(last_columns(width))
    load_matrix(packed, runs[0], w_qkv, width)
    load_matrix(packed, runs[1], w_pos, width)
    taps = d_depth.shape[0]
    start = total * block_rows(width)
    for lane in range(0, width, LANES):
        count = min(LANES, width - lane)
        lanes = slice(lane, lane + count)
        small = packed[start : start + SMALL, :count].astype(F32)
        d_bias[:, lanes] = small[0:2]
        gains[0:2, lanes] = small[2:4]
        biases[0:2, lanes] = small[4:6]
        gains[2:4, lanes] = small[6:8]
        biases[2:4, lanes] = small[8:10]
        d_depth[:, lanes] = small[10 : 10 + taps]
        start = start + SMALL


def local(inputs, w_qkv, w_pos, w_out, rel_bias, ffn_in, ffn_out, conv_in, conv_depth, conv_out, bn_gain, bn_bias, norm_gain, norm_bias, lengths, cotangent):
    _, rows, width = inputs.shape
    inner = ffn_in.shape[2]
    taps = conv_depth.shape[0]
    head_width = width // HEADS
    seq_count = lax.axis_size("seq")
    devices = device_count()
    slots = slot_pieces(devices)
    place = lax.axis_index("seq").astype(jnp.int32).reshape(1)
    orders = arrival_order()

    turned = inputs[0].T
    in_both = ffn_in.transpose(1, 0, 2)
    in_early, in_late = in_both[:, 0], in_both[:, 1]
    out_both = ffn_out.transpose(2, 0, 1)
    out_early, out_late = out_both[:, 0], out_both[:, 1]
    gates = conv_in.T
    cotangent_turned = cotangent[0].T
    bn_gain_row, bn_bias_row = bn_gain[None], bn_bias[None]

    model = struct((rows, width), F32)
    model_low = struct((rows, width), BF16)
    inner_low = struct((rows, inner), BF16)
    head_low = struct((rows, HEADS * LANES), BF16)
    tile = struct((devices, 8, LANES), F32)
    reached = rows + 2 * HALO
    blocks, (
        block,
        query,
        shift,
        w_query,
        w_pair,
        w_pos_wide,
        w_out_wide,
        depth_wide,
        own_cos,
        own_sin,
        clip_rows,
        clip_wide,
        valid_wide,
        *by_order,
    ) = gather_frames(turned, lambda: call(
        functools.partial(prepare_kernel, orders),
        [
            model_low,
            struct((HEADS, rows, 4 * LANES), BF16),
            head_low,
            struct((width, HEADS * LANES), BF16),
            struct((HEADS, width, 2 * LANES), BF16),
            struct((WIDE, HEADS * LANES), BF16),
            struct((HEADS * LANES, width), BF16),
            struct((taps, WIDE), F32),
            struct((rows, WIDE), F32),
            struct((rows, WIDE), F32),
            struct((rows, 1), jnp.int32),
            struct((reached, LANES), jnp.int32),
            struct((reached, 1), F32),
        ]
        + [
            struct((high, len(order) * rows), dtype)
            for order in orders
            for high, dtype in ((WIDE, BF16), (1, jnp.int32))
        ],
        [place, lengths, turned, w_qkv, w_pos, w_out, rel_bias, conv_depth]
        + wave_tables(rows, seq_count, width),
        micros=5.5,
        smem=2,
    ))
    valid_rows = valid_wide[HALO : HALO + rows]
    tables, clips = by_order[0::2], by_order[1::2]
    first_blocks, last_blocks = ([blocks[step] for step in order] for order in orders)
    blocks = first_blocks + last_blocks
    early_count = len(first_blocks)
    *carried, frames_one, pair_one = attend(
        first_blocks, query, w_pair, tables[0], clip_rows, clips[0], head_width
    )
    last_blocks = [after(last_blocks[0], pair_one)] + last_blocks[1:]
    attended, log_total, frames_two, pair_two = attend(
        last_blocks, query, w_pair, tables[1], clip_rows, clips[1], head_width, carried
    )
    pairs = (pair_one, pair_two)
    first_sum, second_sum, second_norm, left, right, gated, attended_low = call(
        early_kernel,
        [model, model, model, model, model, struct((rows, WIDE), BF16), head_low],
        [block, attended, w_out_wide, norm_gain, norm_bias, in_early, out_early, gates],
        micros=5.0,
    )
    gated_low = shift_seq(gated[rows - HALO :], 1)
    gated_high = shift_seq(gated[:HALO], -1)
    convolved, spread = call(
        functools.partial(conv_kernel, devices),
        [model, tile],
        [gated_low, gated, gated_high, clip_wide, depth_wide, valid_rows],
        scratch=[pltpu.VMEM((3, reached, LANES), F32)],
        micros=3.5,
    )
    arrived = exchange_small(spread)
    first_low, second_low, act_early, slope_early = call(
        again_kernel,
        [model_low, model_low, inner_low, inner_low],
        [first_sum, second_sum, norm_gain, norm_bias, in_early],
        micros=3.0,
    )

    def tap_sums(first, count, *factors):
        return call(
            functools.partial(taps_kernel, taps, count),
            [struct((taps, width), F32)] * count,
            [first, gated, gated_high, clip_wide] + list(factors),
            scratch=[pltpu.VMEM((3, reached, LANES), F32)],
            micros=2.5 + 1.0 * count,
        )

    depth_valid, depth_conv = tap_sums(gated_low, 2, convolved, valid_rows)
    arrived = after(arrived, first_low, depth_valid)
    edge = struct((2, HALO, width), F32)
    (
        result,
        act_late,
        d_inner_late,
        third_low,
        fourth_grad,
        swished,
        third_grad_low,
        third_grad,
        d_normed,
        unit,
        spread,
        late_norms,
        statistics,
        edge_low,
        edge_high,
    ) = call(
        functools.partial(late_kernel, devices),
        [struct((width, rows), F32), inner_low, inner_low, model_low, model_low, model_low]
        + [model_low, model, model, model]
        + [tile, struct((4, width), F32), struct((8, WIDE), F32), edge, edge],
        [arrived, convolved, second_norm, bn_gain_row, bn_bias_row, conv_out, norm_gain, norm_bias]
        + [in_late, out_late, cotangent_turned],
        micros=6.4,
    )
    from_low = shift_seq(edge_high, 1)
    from_high = shift_seq(edge_low, -1)
    arrived = exchange_small(spread)
    late_rows = packed_rows(late_columns(width, inner), width)
    outs, late_scratch = half_slots(late_rows, devices)
    late_keep, late_send = call(
        late_grads_kernel,
        outs,
        [slots, third_low, d_inner_late, act_late, fourth_grad, swished, third_grad_low],
        scratch=[late_scratch],
        micros=4.3,
        smem=1,
    )
    late_sum = SlotSum(late_keep, late_send)
    stat = struct((HEADS, rows, 1), F32)
    early_rows = packed_rows(early_columns(width, inner), width)
    outs, early_scratch = half_slots(early_rows, devices)
    mark = depth_valid
    mark = late_sum.step(mark)
    first_grad, d_attended, delta, early_norms, bn_grads, early_keep, early_send = call(
        middle_kernel,
        [model, head_low, stat, struct((4, width), F32), struct((2, width), F32)] + outs,
        [slots, after(arrived, late_keep, mark), statistics, bn_gain_row, d_normed, unit]
        + [from_low, from_high, clip_wide, valid_wide, depth_wide, left, right, gates, third_grad]
        + [second_sum, norm_gain, slope_early, first_sum, in_early, out_early, w_out_wide, attended]
        + [first_low, second_low, act_early, attended_low],
        scratch=[
            pltpu.VMEM((3, reached, LANES), F32),
            pltpu.VMEM((rows, width), F32),
            early_scratch,
        ],
        micros=12.0,
        smem=1,
    )
    early_sum = SlotSum(early_keep, early_send)
    mark = first_grad
    (depth_grad,) = tap_sums(after(gated_low, mark), 1, d_normed)
    mark = depth_grad
    mark = early_sum.step(mark)
    *d_frames, d_pair_weight, d_query_weight, d_pos_weight, d_bias, own_grad = attend_back(
        [len(order) for order in orders], after(query, mark), pairs, tables, clip_rows, clips,
        (frames_one, frames_two), log_total, delta, d_attended, shift, w_pos_wide, w_query, w_pair,
        own_cos, own_sin, turned, first_grad, head_width,
    )
    mark = own_grad
    late_sum.join(early_sum)
    both_sum = late_sum
    mark = both_sum.step(mark)
    last_rows = packed_rows(last_columns(width), width, 3 * SMALL)
    outs, packed = half_slots(last_rows, devices)
    last_keep, last_send = call(
        last_pack_kernel,
        outs,
        [slots, after(d_query_weight, mark), d_pair_weight, d_pos_weight, d_bias]
        + [depth_valid, depth_conv, depth_grad, statistics, bn_grads, bn_gain_row]
        + [late_norms, early_norms],
        scratch=[packed, pltpu.VMEM((block_rows(width + SMALL), 4 * width), F32)],
        micros=3.0,
        smem=1,
    )
    last_sum = SlotSum(last_keep, last_send)
    mark = last_keep
    frame_sum = FrameSum(d_frames[: seq_count // 2], [after(part, mark) for part in d_frames[seq_count // 2 :]])
    mark = both_sum.step(mark)
    mark = last_sum.step(mark)
    mark = both_sum.step(mark)
    frame_sum.step(mark)
    mark = frame_sum.joined[-1]
    mark = last_sum.step(mark)
    mark = last_sum.step(mark)
    mark = last_sum.step(mark, *frame_sum.arrived)
    input_grad = frame_sum.finish(own_grad)
    mark = both_sum.step(mark, input_grad)
    mark = last_sum.step(mark)
    both_keep, both_send = both_sum.finish()
    last_keep, last_send = last_sum.finish()
    last_share = share_rows(last_rows, devices) * devices
    square = struct((width, width), F32)
    sum_in, sum_out, sum_conv_in, sum_conv_out, sum_w_out = call(
        finish_two_kernel,
        [struct((width, 2, inner), F32)] * 2 + [struct((2 * width, width), F32), square, square],
        [slots, both_keep, both_send],
        scratch=[late_scratch, early_scratch],
        micros=10.0,
        smem=1,
    )
    sum_qkv, sum_pos, sum_rel, sum_gain, sum_bias, sum_depth = call(
        finish_last_kernel,
        [struct(w_qkv.shape, F32), struct(w_pos.shape, F32), struct(rel_bias.shape, F32)]
        + [struct(norm_gain.shape, F32), struct(norm_bias.shape, F32)]
        + [struct(conv_depth.shape, F32)],
        [slots, last_keep, last_send],
        scratch=[pltpu.VMEM((last_share, LANES), BF16)],
        micros=3.0,
        smem=1,
    )
    return (
        result.T[None],
        input_grad.T[None],
        sum_qkv,
        sum_pos,
        sum_w_out,
        sum_rel,
        sum_in.transpose(1, 0, 2),
        sum_out.transpose(1, 2, 0),
        sum_conv_in.T,
        sum_depth,
        sum_conv_out,
        bn_grads[0],
        bn_grads[1],
        sum_gain,
        sum_bias,
    )


def solution(mesh):
    whole = P()
    split = P("dp", "seq", None)
    return jax.shard_map(
        local,
        mesh=mesh,
        in_specs=(split,) + (whole,) * 13 + (P("dp", None), split),
        out_specs=(split, split) + (whole,) * 13,
        check_vma=False,
    )
```

```python
import functools
import math

import jax
import jax.numpy as jnp
from jax import lax
from jax.experimental import pallas as pl
from jax.experimental.pallas import tpu as pltpu
from jax.sharding import PartitionSpec as P
import numpy as np

HEADS = 4
LANES = 128
WIDE = 3 * LANES
HALO = 16
SMALL = 48
EPS = 1e-05
MODEL_AXES = ("seq", "dp")
VMEM_BYTES = 60 * 1024 * 1024
BF16 = jnp.bfloat16
F32 = jnp.float32


def device_count():
    return lax.axis_size("seq") * lax.axis_size("dp")


def flat_index():
    return lax.axis_index("seq") * lax.axis_size("dp") + lax.axis_index("dp")


def swap_flat(block, distance):
    pairs = [(i, i ^ distance) for i in range(device_count())]
    return lax.ppermute(block, MODEL_AXES, pairs)


def swap_seq(block, distance):
    pairs = [(i, i ^ distance) for i in range(lax.axis_size("seq"))]
    return lax.ppermute(block, "seq", pairs)


def shift_seq(block, step):
    count = lax.axis_size("seq")
    pairs = [(i, i + step) for i in range(count) if 0 <= i + step < count]
    return lax.ppermute(block, "seq", pairs)


def stage_radices(devices):
    radices = [2]
    left = devices // 2
    while left > 1:
        radix = 4 if left % 4 == 0 else 2
        radices.append(radix)
        left = left // radix
    return radices


def slot_pieces(devices, earlier):
    slots = jnp.arange(devices, dtype=jnp.int32)
    distance = jnp.zeros((devices,), jnp.int32)
    span = devices
    stride = 1
    for radix in stage_radices(devices):
        span = span // radix
        distance = distance + ((slots // span) % radix) * stride
        stride = stride * radix
    place = after(flat_index().astype(jnp.int32), earlier)
    return place ^ distance


def add_kernel(counts, radix, *refs):
    outs = refs[sum(counts) :]
    start = 0
    row = 0
    for count in counts:
        parts = refs[start : start + count]
        start = start + count
        total = parts[0][...].astype(F32)
        for part in parts[1:]:
            total = total + part[...].astype(F32)
        total = total.astype(BF16)
        span, share = total.shape[0] // radix, total.shape[1]
        for place, out in enumerate(outs):
            out[:, row : row + share] = total[place * span : (place + 1) * span]
        row = row + share


class SlotSum:
    def __init__(self, keep, send):
        self.others = []
        radices = stage_radices(device_count())
        strides = [1]
        for radix in radices[:-1]:
            strides.append(strides[-1] * radix)
        self.stages = list(zip(radices, strides))
        self.next = 1
        self.parts = self.scatter(0, [keep, send])
        self.mark = keep

    def join(self, other):
        self.others.append(other.parts)

    def scatter(self, stage, pieces):
        radix, stride = self.stages[stage]
        return [pieces[0]] + [
            swap_flat(pieces[step], step * stride) for step in range(radix - 1, 0, -1)
        ]

    def spread(self, stage, piece):
        radix, stride = self.stages[stage]
        return [piece] + [swap_flat(piece, step * stride) for step in range(1, radix)]

    def step(self, *earlier):
        count = len(self.stages)
        parts = self.parts
        if self.next >= 2 * count:
            return self.mark
        if earlier:
            parts = [after(parts[0], *earlier)] + parts[1:]
        if self.next <= count:
            radix = self.stages[self.next][0] if self.next < count else 1
            groups = [parts] + self.others
            self.others = []
            slots = parts[0].shape[0]
            if radix == 1:
                total = parts[0].astype(F32)
                for part in parts[1:]:
                    total = total + part.astype(F32)
                self.mark = total.astype(BF16)
                self.parts = self.spread(count - 1, self.mark)
                self.next = self.next + 1
                return self.mark
            share = sum(group[0].shape[1] for group in groups)
            pieces = call(
                functools.partial(add_kernel, [len(group) for group in groups], radix),
                [struct((slots // radix, share, LANES), BF16)] * radix,
                [part for group in groups for part in group],
                micros=2.0,
            )
            self.mark = pieces[0]
            self.parts = self.scatter(self.next, pieces)
        else:
            self.mark = jnp.concatenate(parts, axis=0)
            self.parts = self.spread(2 * count - 1 - self.next, self.mark)
        self.next = self.next + 1
        return self.mark

    def finish(self):
        while self.next < 2 * len(self.stages):
            self.step()
        return self.parts


def exchange_small(spread):
    return lax.all_to_all(spread, MODEL_AXES, 0, 0)


def after(value, *earlier):
    return lax.optimization_barrier((value,) + earlier)[0]


def arrival_order():
    count = lax.axis_size("seq")
    return [0, 1] + list(range(2, count, 2)), list(range(3, count, 2))


def gather_frames(shard, meanwhile):
    count = lax.axis_size("seq")
    across = [shard] + [swap_seq(shard, 2 * step) for step in range(1, count // 2)]
    made = meanwhile()
    blocks = []
    for step, block in enumerate(across):
        blocks.append(block)
        passed = block if step < count // 2 - 1 else after(block, made[0])
        blocks.append(swap_seq(passed, 1))
    return blocks, made


class FrameSum:
    def __init__(self, kept, passed):
        self.kept = kept
        self.passed = [swap_seq(pair, 1) for pair in passed]

    def step(self, *earlier):
        count = len(self.kept)
        self.arrived, self.joined = [], []
        for step in range(count - 1, 0, -1):
            came = self.passed[(count - 1 - step) // 2][(count - 1 - step) % 2]
            joined = self.kept[step].astype(F32) + came.astype(F32)
            if earlier:
                joined = after(joined, *earlier)
            self.joined.append(joined.astype(BF16))
            self.arrived.append(swap_seq(self.joined[-1], 2 * step))

    def finish(self, own):
        total = own + self.kept[0].astype(F32) + self.passed[-1][1].astype(F32)
        for block in self.arrived:
            total = total + block.astype(F32)
        return total


def cost(micros):
    return pl.CostEstimate(flops=int(micros * 0.460e9), bytes_accessed=0, transcendentals=0)


def call(body, outs, args, scratch=(), micros=2.0, smem=0):
    specs = [
        pl.BlockSpec(memory_space=pltpu.SMEM if place < smem else pltpu.VMEM)
        for place in range(len(args))
    ]
    return pl.pallas_call(
        body,
        out_shape=tuple(outs),
        in_specs=specs,
        out_specs=tuple(pl.BlockSpec(memory_space=pltpu.VMEM) for _ in outs),
        scratch_shapes=list(scratch),
        compiler_params=pltpu.CompilerParams(vmem_limit_bytes=VMEM_BYTES),
        cost_estimate=cost(micros),
    )(*args)


def struct(shape, dtype):
    return jax.ShapeDtypeStruct(tuple(shape), dtype)


def nn(left, right):
    return lax.dot_general(left, right, (((1,), (0,)), ((), ())), preferred_element_type=F32)


def nt(left, right):
    return lax.dot_general(left, right, (((1,), (1,)), ((), ())), preferred_element_type=F32)


def tn(left, right):
    return lax.dot_general(left, right, (((0,), (0,)), ((), ())), preferred_element_type=F32)


def norm_parts(summed):
    average = jnp.mean(summed, axis=-1, keepdims=True)
    centered = summed - average
    variance = jnp.mean(centered * centered, axis=-1, keepdims=True)
    inverse = lax.rsqrt(variance + EPS)
    return centered * inverse, inverse


def norm_back(unit, inverse, gain, incoming):
    scaled = incoming * gain
    first = jnp.mean(scaled, axis=-1, keepdims=True)
    second = jnp.mean(scaled * unit, axis=-1, keepdims=True)
    grad = inverse * (scaled - first - unit * second)
    return (
        grad,
        jnp.sum(incoming * unit, axis=0, keepdims=True),
        jnp.sum(incoming, axis=0, keepdims=True),
    )


def sigmoid(value):
    return 0.5 * jnp.tanh(0.5 * value) + 0.5


def silu_back(value):
    gate = sigmoid(value)
    return gate * (1.0 + value * (1.0 - gate))


def store_tile(ref, rows, copies):
    tile = jnp.zeros((8, LANES), F32)
    parts = []
    for row in rows:
        width = row.shape[1]
        blocks = -(-width // LANES)
        wide = row
        if blocks * LANES > width:
            wide = jnp.concatenate([row, jnp.zeros((1, blocks * LANES - width), F32)], axis=1)
        for block in range(blocks):
            parts.append(wide[:, block * LANES : (block + 1) * LANES])
    for place, part in enumerate(parts):
        tile = jnp.where(
            lax.broadcasted_iota(jnp.int32, (8, LANES), 0) == place,
            jnp.broadcast_to(part, (8, LANES)),
            tile,
        )
    ref[...] = jnp.broadcast_to(tile[None], (copies, 8, LANES))


def tile_row(tile, place, width):
    blocks = -(-width // LANES)
    parts = [tile[place * blocks + block : place * blocks + block + 1] for block in range(blocks)]
    return jnp.concatenate(parts, axis=1)[:, :width]


def plan_blocks(columns):
    runs = []
    block = 0
    for count in columns:
        full = count // LANES
        runs.append([(block + place, 0, place * LANES, LANES) for place in range(full)])
        block = block + full
    open_block, lane = None, LANES
    for place, count in enumerate(columns):
        rest = count % LANES
        if rest:
            if lane + rest > LANES:
                open_block, lane = block, 0
                block = block + 1
            runs[place].append((open_block, lane, count - rest, rest))
            lane = lane + rest
    return runs, block


def block_rows(rows):
    return -(-rows // 8) * 8


def store_matrix(packed, runs, value):
    rows = value.shape[0]
    low = value.astype(BF16)
    for block, lane, column, count in runs:
        start = block * block_rows(rows)
        packed[start : start + rows, lane : lane + count] = low[:, column : column + count]


def load_matrix(packed, runs, out, rows, row=0):
    for block, lane, column, count in runs:
        start = block * block_rows(rows)
        out[row : row + rows, column : column + count] = packed[
            start : start + rows, lane : lane + count
        ].astype(F32)


def load_layer(packed, runs, out, layer):
    rows = out.shape[0]
    for block, lane, column, count in runs:
        start = block * block_rows(rows)
        out[:, layer, column : column + count] = packed[
            start : start + rows, lane : lane + count
        ].astype(F32)


def spread_pieces(slots_ref, packed, keep_ref, send_ref):
    half, share = keep_ref.shape[:2]

    def one(slot, nothing):
        low = pl.multiple_of(slots_ref[slot] * share, HALO)
        keep_ref[slot] = packed[pl.ds(low, share), :]
        high = pl.multiple_of(slots_ref[slot + half] * share, HALO)
        send_ref[slot] = packed[pl.ds(high, share), :]
        return nothing

    lax.fori_loop(0, half, one, 0)


def collect_pieces(slots_ref, keep_ref, send_ref, packed, row=0):
    half = keep_ref.shape[0]
    share = packed.shape[0] // (2 * half)

    def one(slot, nothing):
        low = pl.multiple_of(slots_ref[slot] * share, HALO)
        packed[pl.ds(low, share), :] = keep_ref[slot, row : row + share]
        high = pl.multiple_of(slots_ref[slot + half] * share, HALO)
        packed[pl.ds(high, share), :] = send_ref[slot, row : row + share]
        return nothing

    lax.fori_loop(0, half, one, 0)


def share_rows(rows, devices):
    return -(-rows // (HALO * devices)) * HALO


def half_slots(rows, devices):
    share = share_rows(rows, devices)
    return [struct((devices // 2, share, LANES), BF16)] * 2, pltpu.VMEM((devices * share, LANES), BF16)


def wave_tables(rows, blocks, width):
    half = width // 2
    frequency = np.exp(np.arange(half) * (-2.0 * math.log(10000.0) / width))
    tail = np.zeros(LANES // 2)
    tail[: half - LANES] = frequency[LANES:]
    lanes = np.concatenate([frequency[:LANES], frequency[:LANES], tail, tail])[None]
    row_angles = np.arange(rows)[:, None] * lanes
    block_angles = (np.arange(blocks) * rows)[:, None] * lanes
    return [
        jnp.asarray(table.astype(np.float32))
        for table in (
            np.cos(row_angles),
            np.sin(row_angles),
            np.cos(block_angles),
            np.sin(block_angles),
        )
    ]


def half_pieces(width):
    half = width // 2
    rest = half - LANES
    return (
        (0, 0, LANES),
        (half, LANES, LANES),
        (LANES, 2 * LANES, rest),
        (half + LANES, 2 * LANES + LANES // 2, rest),
    )


def half_sign():
    lane = lax.broadcasted_iota(jnp.int32, (1, LANES), 1)
    return jnp.where(lane < LANES // 2, 1.0, -1.0)


def prepare_kernel(orders, where, lengths, turned, w_qkv, w_pos, w_out, bias, depth, base_cos, base_sin, block_cos, block_sin, block, query, shift, w_query, w_pair, w_pos_wide, w_out_wide, depth_wide, own_cos, own_sin, clip_rows, clip_wide, valid_wide, valid_rows, *by_order):
    place = where[0]
    width, rows = turned.shape
    size = width // HEADS
    blocks = block_cos.shape[0]
    w_query[...] = jnp.zeros_like(w_query)
    w_pair[...] = jnp.zeros_like(w_pair)
    w_pos_wide[...] = jnp.zeros_like(w_pos_wide)
    w_out_wide[...] = jnp.zeros_like(w_out_wide)
    depth_wide[...] = jnp.zeros_like(depth_wide)
    depth_wide[:, :width] = depth[...]
    for head in range(HEADS):
        natural = slice(head * size, (head + 1) * size)
        low = head * LANES
        w_query[:, low : low + size] = w_qkv[:, head * size : (head + 1) * size]
        w_pair[head, :, :size] = w_qkv[:, width + head * size : width + (head + 1) * size]
        w_pair[head, :, LANES : LANES + size] = w_qkv[
            :, 2 * width + head * size : 2 * width + (head + 1) * size
        ]
        w_out_wide[low : low + size] = w_out[natural]
        for source, target, length in half_pieces(width):
            w_pos_wide[target : target + length, low : low + size] = w_pos[
                source : source + length, natural
            ]
    lane = lax.broadcasted_iota(jnp.int32, (1, WIDE), 1)
    on_cosine = (lane < LANES) | ((lane >= 2 * LANES) & (lane < 2 * LANES + LANES // 2))
    row_cos, row_sin = base_cos[...], base_sin[...]
    ends = [lengths[0, 0]]
    for clip in range(1, lengths.shape[1]):
        ends.append(ends[-1] + lengths[0, clip])

    def clip_at(frames):
        clip = jnp.zeros_like(frames)
        for end in ends:
            clip = clip + (frames >= end).astype(jnp.int32)
        return clip

    for order, table, clip_columns in zip(orders, by_order[0::2], by_order[1::2]):
        for step, distance in enumerate(order):
            here = place ^ distance
            cosine = block_cos[pl.ds(here, 1), :]
            sine = block_sin[pl.ds(here, 1), :]
            one = jnp.where(on_cosine, cosine, sine)
            two = jnp.where(on_cosine, -sine, cosine)
            lanes = slice(step * rows, (step + 1) * rows)
            table[:, lanes] = (one * row_cos + two * row_sin).astype(BF16).T
            clip_columns[:, lanes] = clip_at(
                here * rows + lax.broadcasted_iota(jnp.int32, (1, rows), 1)
            )
    reached = place * rows - HALO + lax.broadcasted_iota(jnp.int32, (rows + 2 * HALO, LANES), 0)
    inside = (reached >= 0) & (reached < blocks * rows)
    reached_clip = jnp.where(inside, clip_at(reached), -1)
    clip_wide[...] = reached_clip
    clip_rows[...] = reached_clip[HALO : HALO + rows, 0:1]
    valid = (inside & (reached < ends[-1])).astype(F32)[:, 0:1]
    valid_wide[...] = valid
    valid_rows[...] = valid[HALO : HALO + rows]
    block_cosine = block_cos[pl.ds(place, 1), :]
    block_sine = block_sin[pl.ds(place, 1), :]
    cosines = block_cosine * row_cos - block_sine * row_sin
    sines = block_sine * row_cos + block_cosine * row_sin
    own_cos[...] = cosines
    own_sin[...] = sines
    frames = turned[...].T
    block[...] = frames
    projected = nn(frames, w_query[...])
    sign = half_sign()
    for head in range(HEADS):
        lanes = slice(head * LANES, (head + 1) * LANES)
        natural = slice(head * size, (head + 1) * size)
        wide = jnp.zeros((2, LANES - size), F32)
        added = jnp.concatenate([bias[:, natural], wide], axis=1)
        unit = (projected[:, lanes] + added[0:1]).astype(BF16)
        moved = (projected[:, lanes] + added[1:2]).astype(BF16)
        shift[:, lanes] = moved
        shifted = nt(moved, w_pos_wide[:, lanes])
        first, second = shifted[:, :LANES], shifted[:, LANES : 2 * LANES]
        tail = shifted[:, 2 * LANES :]
        sine, cosine = sines[:, :LANES], cosines[:, :LANES]
        query[head, :, :LANES] = unit
        query[head, :, LANES : 2 * LANES] = (first * sine + second * cosine).astype(BF16)
        query[head, :, 2 * LANES : 3 * LANES] = (second * sine - first * cosine).astype(BF16)
        query[head, :, 3 * LANES :] = (
            tail * sines[:, 2 * LANES :]
            + pltpu.roll(tail, LANES // 2, 1) * cosines[:, 2 * LANES :] * sign
        ).astype(BF16)


def masked_scores(query, upper, table, clip_rows, clip_columns, scale):
    raw = nn(query[:, : 2 * LANES], upper) + nn(query[:, 2 * LANES :], table[LANES:])
    return jnp.where(clip_rows == clip_columns, raw * (scale / math.log(2.0)), -1e30)


def attend_kernel(scale, count, last, *refs):
    blocks = refs[:count]
    query, w_pair, table, clip_rows, clip_columns = refs[count : count + 5]
    carried = refs[count + 5 : count + 8] if last else None
    outs = refs[count + (8 if last else 5) :]
    rows = blocks[0].shape[1]
    heads = query.shape[0]
    frames_all, pair = outs[-2:]

    @pl.when(pl.program_id(0) == 0)
    def _():
        for step in range(count):
            frames_all[:, step * rows : (step + 1) * rows] = blocks[step][...]

    def scored(head):
        both = tn(w_pair[head], frames_all[...]).astype(BF16)
        pair[head] = both
        upper = jnp.concatenate([both[:LANES], table[:LANES]], axis=0)
        return both[LANES:], masked_scores(
            query[head], upper, table[...], clip_rows[...], clip_columns[...], scale
        )

    following = scored(0)
    for head in range(heads):
        values, scores = following
        if head + 1 < heads:
            following = scored(head + 1)
        lanes = slice(head * LANES, (head + 1) * LANES)
        highest = jnp.max(scores, axis=1, keepdims=True)
        if last:
            highest = jnp.maximum(highest, carried[0][head])
        weights = jnp.exp2(scores - highest)
        total = jnp.sum(weights, axis=1, keepdims=True)
        summed = nt(weights.astype(BF16), values)
        if last:
            fade = jnp.exp2(carried[0][head] - highest)
            total = total + carried[1][head] * fade
            summed = summed + carried[2][:, lanes] * fade
            attended, log_total = outs[:2]
            attended[:, lanes] = summed / total
            log_total[head] = highest + jnp.log2(total)
        else:
            outs[0][head] = highest
            outs[1][head] = total
            outs[2][:, lanes] = summed


def heads_at_once(frames):
    return 2 if frames <= 2048 else 1


def attend(blocks, query, w_pair, table, clip_rows, clip_columns, head_width, carried=()):
    rows = query.shape[1]
    frames = table.shape[1]
    width = w_pair.shape[1]
    per = heads_at_once(frames)
    stat = pl.BlockSpec((per, rows, 1), lambda h: (h, 0, 0))
    head = pl.BlockSpec((rows, per * LANES), lambda h: (0, h))
    stat_shape = struct((HEADS, rows, 1), F32)
    head_shape = struct((rows, HEADS * LANES), F32)
    last = len(carried) > 0
    return pl.pallas_call(
        functools.partial(attend_kernel, 1.0 / math.sqrt(head_width), len(blocks), last),
        grid=(HEADS // per,),
        in_specs=[pl.BlockSpec((width, rows), lambda h: (0, 0)) for _ in blocks]
        + [
            pl.BlockSpec((per, rows, 4 * LANES), lambda h: (h, 0, 0)),
            pl.BlockSpec((per, width, 2 * LANES), lambda h: (h, 0, 0)),
            pl.BlockSpec((WIDE, frames), lambda h: (0, 0)),
            pl.BlockSpec((rows, 1), lambda h: (0, 0)),
            pl.BlockSpec((1, frames), lambda h: (0, 0)),
        ]
        + ([stat, stat, head] if last else []),
        out_specs=((head, stat) if last else (stat, stat, head))
        + (
            pl.BlockSpec((width, frames), lambda h: (0, 0)),
            pl.BlockSpec((per, 2 * LANES, frames), lambda h: (h, 0, 0)),
        ),
        out_shape=((head_shape, stat_shape) if last else (stat_shape, stat_shape, head_shape))
        + (struct((width, frames), BF16), struct((HEADS, 2 * LANES, frames), BF16)),
        compiler_params=pltpu.CompilerParams(vmem_limit_bytes=VMEM_BYTES),
        cost_estimate=cost(5.0 if last else 8.0),
    )(*blocks, query, w_pair, table, clip_rows, clip_columns, *carried)


def early_kernel(block, attended, w_out, gains, biases, ffn_in, ffn_out, gates, first_sum, second_sum, second_norm, left, right, gated, attended_low):
    low = attended[...].astype(BF16)
    attended_low[...] = low
    summed = block[...].astype(F32) + nn(low, w_out[...])
    first_sum[...] = summed
    unit, _ = norm_parts(summed)
    first = unit * gains[0:1] + biases[0:1]
    inner = nn(first.astype(BF16), ffn_in[...])
    act = (inner * sigmoid(inner)).astype(BF16)
    summed = first + nt(act, ffn_out[...])
    second_sum[...] = summed
    unit, _ = norm_parts(summed)
    second = unit * gains[1:2] + biases[1:2]
    second_norm[...] = second
    second_low = second.astype(BF16)
    half = gates.shape[0] // 2
    one = nt(second_low, gates[:half])
    two = nt(second_low, gates[half:])
    left[...] = one
    right[...] = two
    gated[...] = jnp.zeros_like(gated)
    gated[:, : one.shape[1]] = (one * sigmoid(two)).astype(BF16)


def again_kernel(first_sum, second_sum, gains, biases, ffn_in, first_low_out, second_low_out, act_out, slope_out):
    unit, _ = norm_parts(second_sum[...])
    second_low_out[...] = (unit * gains[1:2] + biases[1:2]).astype(BF16)
    unit, _ = norm_parts(first_sum[...])
    first_low = (unit * gains[0:1] + biases[0:1]).astype(BF16)
    first_low_out[...] = first_low
    inner = nn(first_low, ffn_in[...])
    gate = sigmoid(inner)
    act_out[...] = (inner * gate).astype(BF16)
    slope_out[...] = (gate * (1.0 + inner * (1.0 - gate))).astype(BF16)


def lane_blocks(width):
    return [(lane, min(LANES, width - lane)) for lane in range(0, width, LANES)]


def extend(extended, low, middle, high):
    rows, width = middle.shape
    for block, (lane, count) in enumerate(lane_blocks(width)):
        if count < LANES:
            extended[block] = jnp.zeros((rows + 2 * HALO, LANES), F32)
        extended[block, 0:HALO, :count] = low[:, lane : lane + count].astype(F32)
        extended[block, HALO : HALO + rows, :count] = middle[:, lane : lane + count].astype(F32)
        extended[block, HALO + rows :, :count] = high[:, lane : lane + count].astype(F32)


def convolve(extended, clip, depth, mirrored, store):
    taps = depth.shape[0]
    blocks, rows, _ = extended.shape
    rows = rows - 2 * HALO
    step = 64
    for start in range(0, rows, step):
        own = clip[HALO + start : HALO + start + step]
        sums = [jnp.zeros((step, LANES), F32) for _ in range(blocks)]
        for tap in range(taps):
            place = HALO - taps // 2 + tap + start
            same = clip[place : place + step] == own
            row = taps - 1 - tap if mirrored else tap
            for block in range(blocks):
                lanes = slice(block * LANES, (block + 1) * LANES)
                sums[block] = sums[block] + depth[row : row + 1, lanes] * jnp.where(
                    same, extended[block, place : place + step], 0.0
                )
        store(start, step, jnp.concatenate(sums, axis=1))


def conv_kernel(copies, low, middle, high, clip, depth, valid, convolved, tile, extended):
    rows, width = convolved.shape
    extend(extended, low[...], middle[...], high[...])

    def store(start, step, value):
        convolved[start : start + step] = value[:, :width]

    convolve(extended, clip, depth, False, store)
    value = convolved[...]
    kept = value * valid[...]
    count = jnp.zeros((1, width), F32) + jnp.sum(valid[...], axis=0, keepdims=True)
    store_tile(
        tile,
        [
            jnp.sum(kept, axis=0, keepdims=True),
            jnp.sum(kept * value, axis=0, keepdims=True),
            count[:, :LANES],
        ],
        copies,
    )


def taps_kernel(taps, count, low, middle, high, clip, *refs):
    factor, *valid = refs[: 1 if count == 1 else 2]
    outs, extended = refs[len(valid) + 1 : -1], refs[-1]
    rows, width = factor.shape
    extend(extended, low[...], middle[...], high[...])
    step = 64
    sums = [[[None] * 3 for _ in range(taps)] for _ in range(count)]
    for start in range(0, rows, step):
        own = clip[HALO + start : HALO + start + step]
        for block, (lane, lanes) in enumerate(lane_blocks(width)):
            part = factor[start : start + step, lane : lane + lanes]
            if lanes < LANES:
                part = jnp.concatenate([part, jnp.zeros((step, LANES - lanes), F32)], axis=1)
            here = [part]
            if valid:
                kept = valid[0][start : start + step]
                here = [jnp.broadcast_to(kept, (step, LANES)), part * kept]
            for tap in range(taps):
                place = HALO - taps // 2 + tap + start
                same = clip[place : place + step] == own
                there = jnp.where(same, extended[block, place : place + step], 0.0)
                for which in range(count):
                    part = jnp.sum((there * here[which]).reshape(step // 8, 8, LANES), axis=0)
                    old = sums[which][tap][block]
                    sums[which][tap][block] = part if old is None else old + part
    for which in range(count):
        for tap in range(taps):
            outs[which][tap : tap + 1] = jnp.concatenate(
                [jnp.sum(part, axis=0, keepdims=True) for part in sums[which][tap]], axis=1
            )[:, :width]


def late_kernel(copies, arrived, convolved, second_norm, bn_gain, bn_bias, conv_out, gains, biases, ffn_in, ffn_out, cotangent, result, act_out, d_inner_out, third_low_out, fourth_grad_out, swished_out, third_grad_out, third_grad, d_normed_out, unit_out, tile, norm_grads, statistics, edge_low, edge_high):
    width = convolved.shape[1]
    rows = convolved.shape[0]
    sums = jnp.sum(arrived[...], axis=0)
    frames = sums[6:7, 0:1]
    mean = tile_row(sums, 0, width) / frames
    variance = tile_row(sums, 1, width) / frames - mean * mean
    inverse = lax.rsqrt(variance + EPS)
    unit = (convolved[...] - mean) * inverse
    unit_out[...] = unit
    statistics[...] = jnp.zeros_like(statistics)
    statistics[0:1, :width] = inverse
    statistics[1:2, :width] = jnp.broadcast_to(frames, (1, width))
    statistics[2:3, :width] = mean
    normed = unit * bn_gain[...] + bn_bias[...]
    swished = (normed * sigmoid(normed)).astype(BF16)
    swished_out[...] = swished
    third_unit, third_inverse = norm_parts(second_norm[...] + nn(swished, conv_out[...]))
    third = third_unit * gains[2:3] + biases[2:3]
    third_low = third.astype(BF16)
    third_low_out[...] = third_low
    inner = nn(third_low, ffn_in[...])
    gate = sigmoid(inner)
    act = (inner * gate).astype(BF16)
    act_out[...] = act
    fourth_unit, fourth_inverse = norm_parts(third + nt(act, ffn_out[...]))
    result[...] = (fourth_unit * gains[3:4] + biases[3:4]).T
    fourth_grad, gain_three, bias_three = norm_back(
        fourth_unit, fourth_inverse, gains[3:4], cotangent[...].T
    )
    fourth_low = fourth_grad.astype(BF16)
    fourth_grad_out[...] = fourth_low
    d_act = nn(fourth_low, ffn_out[...])
    d_inner = (d_act * (gate * (1.0 + inner * (1.0 - gate)))).astype(BF16)
    d_inner_out[...] = d_inner
    grad, gain_two, bias_two = norm_back(
        third_unit, third_inverse, gains[2:3], fourth_grad + nt(d_inner, ffn_in[...])
    )
    third_grad[...] = grad
    grad_low = grad.astype(BF16)
    third_grad_out[...] = grad_low
    d_normed = nt(grad_low, conv_out[...]) * silu_back(normed)
    d_normed_out[...] = d_normed
    store_tile(
        tile,
        [
            jnp.sum(d_normed * unit, axis=0, keepdims=True),
            jnp.sum(d_normed, axis=0, keepdims=True),
        ],
        copies,
    )
    norm_grads[0:1] = gain_two
    norm_grads[1:2] = gain_three
    norm_grads[2:3] = bias_two
    norm_grads[3:4] = bias_three
    edge_low[0] = d_normed[:HALO]
    edge_low[1] = unit[:HALO]
    edge_high[0] = d_normed[rows - HALO :]
    edge_high[1] = unit[rows - HALO :]


def late_columns(width, inner):
    return (inner, inner, width)


def early_columns(width, inner):
    return (inner, inner, width, width, width)


def last_columns(width):
    return (3 * width, width)


def packed_rows(columns, width, small=0):
    _, blocks = plan_blocks(columns)
    return blocks * block_rows(width) + small


def late_grads_kernel(slots, third_low, d_inner, act, fourth_grad, swished, third_grad, keep, send, packed):
    width = third_low.shape[1]
    runs, _ = plan_blocks(late_columns(width, act.shape[1]))
    store_matrix(packed, runs[0], tn(third_low[...], d_inner[...]))
    store_matrix(packed, runs[1], tn(fourth_grad[...], act[...]))
    store_matrix(packed, runs[2], tn(swished[...], third_grad[...]))
    spread_pieces(slots, packed, keep, send)


def middle_kernel(slots, arrived, statistics, bn_gain, d_normed, unit, from_low, from_high, clip, valid, depth, left, right, gates, third_grad, second_sum, gains, slope, first_sum, ffn_in, ffn_out, w_out, attended, first_low, second_low, act, attended_low, first_grad, d_attended, delta, norm_grads, bn_grads, keep, send, extended, d_gated, packed):
    rows, width = left.shape
    sums = jnp.sum(arrived[...], axis=0)
    gain_sum = tile_row(sums, 0, width)
    bias_sum = tile_row(sums, 1, width)
    bn_grads[0:1] = gain_sum
    bn_grads[1:2] = bias_sum
    gain = bn_gain[...]
    inverse = statistics[0:1, :width]
    frames = statistics[1:2, :width]

    def conv_grad(d_rows, unit_rows, valid_rows):
        return (
            inverse * gain * (d_rows - valid_rows * (bias_sum + unit_rows * gain_sum) / frames)
        ).astype(BF16)

    extend(
        extended,
        conv_grad(from_low[0], from_low[1], valid[0:HALO]),
        conv_grad(d_normed[...], unit[...], valid[HALO : HALO + rows]),
        conv_grad(from_high[0], from_high[1], valid[HALO + rows :]),
    )

    def store(start, step, value):
        d_gated[start : start + step] = value[:, :width]

    convolve(extended, clip, depth, True, store)
    gate = sigmoid(right[...])
    d_left = (d_gated[...] * gate).astype(BF16)
    d_right = (d_gated[...] * left[...] * gate * (1.0 - gate)).astype(BF16)
    second_unit, second_inverse = norm_parts(second_sum[...])
    half = gates.shape[0] // 2
    incoming = third_grad[...] + nn(d_left, gates[:half]) + nn(d_right, gates[half:])
    second_grad, gain_one, bias_one = norm_back(
        second_unit, second_inverse, gains[1:2], incoming
    )
    second_grad_low = second_grad.astype(BF16)
    d_act = nn(second_grad_low, ffn_out[...])
    d_inner = (d_act * slope[...].astype(F32)).astype(BF16)
    first_unit, first_inverse = norm_parts(first_sum[...])
    grad, gain_zero, bias_zero = norm_back(
        first_unit, first_inverse, gains[0:1], second_grad + nt(d_inner, ffn_in[...])
    )
    first_grad[...] = grad
    grad_low = grad.astype(BF16)
    for place, part in enumerate((gain_zero, gain_one, bias_zero, bias_one)):
        norm_grads[place : place + 1] = part
    back = nt(grad_low, w_out[...]).astype(BF16)
    d_attended[...] = back
    product = back.astype(F32) * attended[...]
    for head in range(HEADS):
        delta[head] = jnp.sum(
            product[:, head * LANES : (head + 1) * LANES], axis=1, keepdims=True
        )
    size = width // HEADS
    runs, _ = plan_blocks(early_columns(width, act.shape[1]))
    store_matrix(packed, runs[0], tn(first_low[...], d_inner))
    store_matrix(packed, runs[1], tn(second_grad_low, act[...]))
    store_matrix(packed, runs[2], tn(d_left, second_low[...]))
    store_matrix(packed, runs[3], tn(d_right, second_low[...]))
    d_out = tn(attended_low[...], grad_low)
    store_matrix(
        packed,
        runs[4],
        jnp.concatenate([d_out[head * LANES : head * LANES + size] for head in range(HEADS)], axis=0),
    )
    spread_pieces(slots, packed, keep, send)


def attend_back_kernel(scale, counts, query, pair_one, pair_two, table_one, table_two, clip_rows, clip_one, clip_two, frames_one, frames_two, log_total, delta, d_attended, shift, w_pos, w_query, w_pair, own_cos, own_sin, turned, first_grad, *refs):
    blocks = sum(counts)
    kept, passed = refs[: blocks // 2], refs[blocks // 2 : blocks // 2 + blocks // 4]
    d_pair_weight, d_query_weight, d_pos_weight, d_bias, own_grad, d_frames, d_pair, own_sum = refs[
        blocks // 2 + blocks // 4 :
    ]
    group = pl.program_id(0)
    rows = clip_rows.shape[0]
    heads = query.shape[0]
    cosines, sines = own_cos[...], own_sin[...]
    runs = (
        (pair_one, table_one, clip_one, frames_one),
        (pair_two, table_two, clip_two, frames_two),
    )
    pieces = []
    start = 0
    for run in runs:
        for low in range(0, run[3].shape[1], 5 * rows):
            length = min(5 * rows, run[3].shape[1] - low)
            pieces.append(run + (slice(low, low + length), slice(start, start + length)))
            start = start + length
    work = [(head, piece) for head in range(heads) for piece in pieces]

    def scored(head, piece):
        pair, table, clip_columns, _, here, _ = piece
        lanes = slice(head * LANES, (head + 1) * LANES)
        upper = jnp.concatenate([pair[head, :LANES, here], table[:LANES, here]], axis=0)
        scores = masked_scores(
            query[head], upper, table[:, here], clip_rows[...], clip_columns[:, here], scale
        )
        return upper, scores, nn(d_attended[:, lanes], pair[head, LANES:, here])

    following = scored(*work[0])
    for place, (head, piece) in enumerate(work):
        _, table, _, frames, here, span = piece
        lanes = slice(head * LANES, (head + 1) * LANES)
        upper, scores, slope = following
        if place + 1 < len(work):
            following = scored(*work[place + 1])
        probs = jnp.exp2(scores - log_total[head])
        d_raw = (probs * (slope * scale - delta[head] * scale)).astype(BF16)
        d_pair[:LANES, span] = nn(query[head, :, :LANES].T, d_raw).astype(BF16)
        d_pair[LANES:, span] = nn(d_attended[:, lanes].T, probs.astype(BF16)).astype(BF16)
        first_piece = place % len(pieces) == 0
        unit_part = nt(d_raw, upper)
        rest_part = nt(d_raw, table[LANES:, here])
        weight_part = nt(frames[:, here], d_pair[:, span])
        unit_sum = unit_part if first_piece else unit_sum + unit_part
        rest_sum = rest_part if first_piece else rest_sum + rest_part
        weight_sum = weight_part if first_piece else weight_sum + weight_part
        by_frame = nn(w_pair[head], d_pair[:, span])
        if head > 0:
            d_frames[:, span] += by_frame
        else:

            @pl.when(group == 0)
            def _():
                d_frames[:, span] = by_frame

            @pl.when(group > 0)
            def _():
                d_frames[:, span] += by_frame

        if place % len(pieces) < len(pieces) - 1:
            continue
        d_pair_weight[head] = weight_sum.astype(BF16)
        d_unit = unit_sum[:, :LANES]
        first, second = unit_sum[:, LANES:], rest_sum[:, :LANES]
        tail = rest_sum[:, LANES:]
        sine, cosine = sines[:, :LANES], cosines[:, :LANES]
        d_shifted = jnp.concatenate(
            [
                first * sine - second * cosine,
                first * cosine + second * sine,
                tail * sines[:, 2 * LANES :]
                - pltpu.roll(tail, LANES // 2, 1) * cosines[:, 2 * LANES :] * half_sign(),
            ],
            axis=1,
        ).astype(BF16)
        d_from_pos = nn(d_shifted, w_pos[:, lanes])
        d_query = (d_unit + d_from_pos).astype(BF16)
        d_query_weight[:, lanes] = nn(turned[...], d_query).astype(BF16)
        d_pos_weight[:, lanes] = tn(d_shifted, shift[:, lanes]).astype(BF16)
        d_bias[0:1, lanes] = jnp.sum(d_unit, axis=0, keepdims=True)
        d_bias[1:2, lanes] = jnp.sum(d_from_pos, axis=0, keepdims=True)
        own = nt(d_query, w_query[:, lanes])
        if head > 0:
            own_sum[...] += own
        else:

            @pl.when(group == 0)
            def _():
                own_sum[...] = first_grad[...] + own

            @pl.when(group > 0)
            def _():
                own_sum[...] += own

    @pl.when(group == HEADS // heads - 1)
    def _():
        own_grad[...] = own_sum[...].T
        orders = [0, 1] + list(range(2, blocks, 2)) + list(range(3, blocks, 2))
        for step in range(blocks // 2):
            lanes = orders.index(2 * step) * rows
            kept[step][...] = d_frames[:, lanes : lanes + rows].astype(BF16)
            lanes = orders.index(2 * step + 1) * rows
            place = blocks // 2 - 1 - step
            passed[place // 2][place % 2] = d_frames[:, lanes : lanes + rows].astype(BF16)


def attend_back(counts, query, pairs, tables, clip_rows, clips, frames, log_total, delta, d_attended, shift, w_pos, w_query, w_pair, own_cos, own_sin, turned, first_grad, head_width):
    rows = query.shape[1]
    width = turned.shape[0]
    wide = HEADS * LANES
    blocks = sum(counts)
    total = blocks * rows
    per = heads_at_once(total)

    def whole(array):
        return pl.BlockSpec(
            array.shape, lambda h: (0,) * len(array.shape), pipeline_mode=pl.Buffered(1)
        )

    def by_head(array):
        return pl.BlockSpec((per,) + array.shape[1:], lambda h: (h, 0, 0))

    def head_lanes(array):
        return pl.BlockSpec((array.shape[0], per * LANES), lambda h: (0, h))

    kept = [struct((width, rows), BF16)] * (blocks // 2)
    passed = [struct((2, width, rows), BF16)] * (blocks // 4)
    by_head_shapes = [struct((HEADS, width, 2 * LANES), BF16)]
    by_lane_shapes = [struct((width, wide), BF16), struct((WIDE, wide), BF16), struct((2, wide), F32)]
    own = struct((width, rows), F32)
    return pl.pallas_call(
        functools.partial(attend_back_kernel, 1.0 / math.sqrt(head_width), counts),
        grid=(HEADS // per,),
        in_specs=[by_head(query)]
        + [by_head(pair) for pair in pairs]
        + [whole(table) for table in tables]
        + [whole(clip_rows)]
        + [whole(clip) for clip in clips]
        + [whole(part) for part in frames]
        + [by_head(log_total), by_head(delta), head_lanes(d_attended), head_lanes(shift)]
        + [head_lanes(w_pos), head_lanes(w_query), by_head(w_pair), whole(own_cos)]
        + [whole(own_sin), whole(turned), whole(first_grad)],
        out_specs=tuple(whole(shape) for shape in kept + passed)
        + tuple(by_head(shape) for shape in by_head_shapes)
        + tuple(head_lanes(shape) for shape in by_lane_shapes)
        + (whole(own),),
        out_shape=tuple(kept + passed + by_head_shapes + by_lane_shapes + [own]),
        scratch_shapes=[
            pltpu.VMEM((width, total), F32),
            pltpu.VMEM((2 * LANES, total), BF16),
            pltpu.VMEM((rows, width), F32),
        ],
        compiler_params=pltpu.CompilerParams(vmem_limit_bytes=VMEM_BYTES),
        cost_estimate=cost(20.0),
    )(query, *pairs, *tables, clip_rows, *clips, *frames, log_total, delta, d_attended, shift, w_pos, w_query, w_pair, own_cos, own_sin, turned, first_grad)


def last_pack_kernel(slots, d_query_weight, d_pair_weight, d_pos, d_bias, depth_valid, depth_conv, depth_grad, statistics, bn_grads, bn_gain, late_norms, early_norms, keep, send, packed, natural):
    width = d_query_weight.shape[0]
    size = width // HEADS
    runs, total = plan_blocks(last_columns(width))
    for head in range(HEADS):
        lanes = slice(head * size, (head + 1) * size)
        low = head * LANES
        natural[:width, lanes] = d_query_weight[:, low : low + size].astype(F32)
        natural[:width, width + head * size : width + (head + 1) * size] = d_pair_weight[
            head, :, :size
        ].astype(F32)
        natural[:width, 2 * width + head * size : 2 * width + (head + 1) * size] = d_pair_weight[
            head, :, LANES : LANES + size
        ].astype(F32)
        for start, spread, length in half_pieces(width):
            natural[start : start + length, 3 * width + head * size : 3 * width + (head + 1) * size] = (
                d_pos[spread : spread + length, low : low + size].astype(F32)
            )
        natural[width : width + 2, lanes] = d_bias[:, low : low + size]
    taps = depth_valid.shape[0]
    inverse, frames, mean = (statistics[row : row + 1, :width] for row in range(3))
    gain_sum, bias_sum = bn_grads[0:1], bn_grads[1:2]
    by_unit = (depth_conv[...] - mean * depth_valid[...]) * inverse
    d_depth = (
        inverse
        * bn_gain[...]
        * (depth_grad[...] - (bias_sum * depth_valid[...] + gain_sum * by_unit) / frames)
    )
    natural[width + 2 : width + 6, :width] = early_norms[...]
    natural[width + 6 : width + 10, :width] = late_norms[...]
    natural[width + 10 : width + 10 + taps, :width] = d_depth
    store_matrix(packed, runs[0], natural[:width, : 3 * width])
    store_matrix(packed, runs[1], natural[:width, 3 * width :])
    start = total * block_rows(width)
    for lane in range(0, width, LANES):
        count = min(LANES, width - lane)
        packed[start : start + 10 + taps, :count] = natural[
            width : width + 10 + taps, lane : lane + count
        ].astype(BF16)
        start = start + SMALL
    spread_pieces(slots, packed, keep, send)


def finish_two_kernel(slots, keep, send, ffn_in, ffn_out, conv_in, conv_out, w_out, late, early):
    width, _, inner = ffn_in.shape
    share = late.shape[0] // (2 * keep.shape[0])
    collect_pieces(slots, keep, send, late)
    collect_pieces(slots, keep, send, early, share)
    late_runs, _ = plan_blocks(late_columns(width, inner))
    early_runs, _ = plan_blocks(early_columns(width, inner))
    for place, out in enumerate((ffn_in, ffn_out)):
        load_layer(early, early_runs[place], out, 0)
        load_layer(late, late_runs[place], out, 1)
    load_matrix(late, late_runs[2], conv_out, width)
    load_matrix(early, early_runs[2], conv_in, width)
    load_matrix(early, early_runs[3], conv_in, width, width)
    load_matrix(early, early_runs[4], w_out, width)


def finish_last_kernel(slots, keep, send, w_qkv, w_pos, d_bias, gains, biases, d_depth, packed):
    width = w_pos.shape[1]
    collect_pieces(slots, keep, send, packed)
    runs, total = plan_blocks(last_columns(width))
    load_matrix(packed, runs[0], w_qkv, width)
    load_matrix(packed, runs[1], w_pos, width)
    taps = d_depth.shape[0]
    start = total * block_rows(width)
    for lane in range(0, width, LANES):
        count = min(LANES, width - lane)
        lanes = slice(lane, lane + count)
        small = packed[start : start + SMALL, :count].astype(F32)
        d_bias[:, lanes] = small[0:2]
        gains[0:2, lanes] = small[2:4]
        biases[0:2, lanes] = small[4:6]
        gains[2:4, lanes] = small[6:8]
        biases[2:4, lanes] = small[8:10]
        d_depth[:, lanes] = small[10 : 10 + taps]
        start = start + SMALL


def local(inputs, w_qkv, w_pos, w_out, rel_bias, ffn_in, ffn_out, conv_in, conv_depth, conv_out, bn_gain, bn_bias, norm_gain, norm_bias, lengths, cotangent):
    _, rows, width = inputs.shape
    inner = ffn_in.shape[2]
    taps = conv_depth.shape[0]
    head_width = width // HEADS
    seq_count = lax.axis_size("seq")
    devices = device_count()
    place = lax.axis_index("seq").astype(jnp.int32).reshape(1)
    orders = arrival_order()

    turned = inputs[0].T
    in_both = ffn_in.transpose(1, 0, 2)
    in_early, in_late = in_both[:, 0], in_both[:, 1]
    out_both = ffn_out.transpose(2, 0, 1)
    out_early, out_late = out_both[:, 0], out_both[:, 1]
    gates = conv_in.T

    model = struct((rows, width), F32)
    model_low = struct((rows, width), BF16)
    inner_low = struct((rows, inner), BF16)
    head_low = struct((rows, HEADS * LANES), BF16)
    tile = struct((devices, 8, LANES), F32)
    reached = rows + 2 * HALO
    blocks, (
        block,
        query,
        shift,
        w_query,
        w_pair,
        w_pos_wide,
        w_out_wide,
        depth_wide,
        own_cos,
        own_sin,
        clip_rows,
        clip_wide,
        valid_wide,
        valid_rows,
        *by_order,
    ) = gather_frames(turned, lambda: call(
        functools.partial(prepare_kernel, orders),
        [
            model_low,
            struct((HEADS, rows, 4 * LANES), BF16),
            head_low,
            struct((width, HEADS * LANES), BF16),
            struct((HEADS, width, 2 * LANES), BF16),
            struct((WIDE, HEADS * LANES), BF16),
            struct((HEADS * LANES, width), BF16),
            struct((taps, WIDE), F32),
            struct((rows, WIDE), F32),
            struct((rows, WIDE), F32),
            struct((rows, 1), jnp.int32),
            struct((reached, LANES), jnp.int32),
            struct((reached, 1), F32),
            struct((rows, 1), F32),
        ]
        + [
            struct((high, len(order) * rows), dtype)
            for order in orders
            for high, dtype in ((WIDE, BF16), (1, jnp.int32))
        ],
        [place, lengths, turned, w_qkv, w_pos, w_out, rel_bias, conv_depth]
        + wave_tables(rows, seq_count, width),
        micros=5.5,
        smem=2,
    ))
    tables, clips = by_order[0::2], by_order[1::2]
    first_blocks, last_blocks = ([blocks[step] for step in order] for order in orders)
    blocks = first_blocks + last_blocks
    early_count = len(first_blocks)
    *carried, frames_one, pair_one = attend(
        first_blocks, query, w_pair, tables[0], clip_rows, clips[0], head_width
    )
    last_blocks = [after(last_blocks[0], pair_one)] + last_blocks[1:]
    attended, log_total, frames_two, pair_two = attend(
        last_blocks, query, w_pair, tables[1], clip_rows, clips[1], head_width, carried
    )
    pairs = (pair_one, pair_two)
    first_sum, second_sum, second_norm, left, right, gated, attended_low = call(
        early_kernel,
        [model, model, model, model, model, struct((rows, WIDE), BF16), head_low],
        [block, attended, w_out_wide, norm_gain, norm_bias, in_early, out_early, gates],
        micros=5.0,
    )
    gated_low = shift_seq(gated[rows - HALO :], 1)
    gated_high = shift_seq(gated[:HALO], -1)
    convolved, spread = call(
        functools.partial(conv_kernel, devices),
        [model, tile],
        [gated_low, gated, gated_high, clip_wide, depth_wide, valid_rows],
        scratch=[pltpu.VMEM((3, reached, LANES), F32)],
        micros=3.5,
    )
    arrived = exchange_small(spread)
    bn_gain_row, bn_bias_row = after(bn_gain, convolved)[None], after(bn_bias, convolved)[None]
    cotangent_turned = after(cotangent, convolved)[0].T
    slots = slot_pieces(devices, convolved)
    first_low, second_low, act_early, slope_early = call(
        again_kernel,
        [model_low, model_low, inner_low, inner_low],
        [first_sum, second_sum, norm_gain, norm_bias, in_early],
        micros=3.0,
    )

    def tap_sums(first, count, *factors):
        return call(
            functools.partial(taps_kernel, taps, count),
            [struct((taps, width), F32)] * count,
            [first, gated, gated_high, clip_wide] + list(factors),
            scratch=[pltpu.VMEM((3, reached, LANES), F32)],
            micros=2.5 + 1.0 * count,
        )

    depth_valid, depth_conv = tap_sums(gated_low, 2, convolved, valid_rows)
    arrived = after(arrived, first_low, depth_valid)
    edge = struct((2, HALO, width), F32)
    (
        result,
        act_late,
        d_inner_late,
        third_low,
        fourth_grad,
        swished,
        third_grad_low,
        third_grad,
        d_normed,
        unit,
        spread,
        late_norms,
        statistics,
        edge_low,
        edge_high,
    ) = call(
        functools.partial(late_kernel, devices),
        [struct((width, rows), F32), inner_low, inner_low, model_low, model_low, model_low]
        + [model_low, model, model, model]
        + [tile, struct((4, width), F32), struct((8, WIDE), F32), edge, edge],
        [arrived, convolved, second_norm, bn_gain_row, bn_bias_row, conv_out, norm_gain, norm_bias]
        + [in_late, out_late, cotangent_turned],
        micros=6.4,
    )
    from_low = shift_seq(edge_high, 1)
    from_high = shift_seq(edge_low, -1)
    arrived = exchange_small(spread)
    late_rows = packed_rows(late_columns(width, inner), width)
    outs, late_scratch = half_slots(late_rows, devices)
    late_keep, late_send = call(
        late_grads_kernel,
        outs,
        [slots, third_low, d_inner_late, act_late, fourth_grad, swished, third_grad_low],
        scratch=[late_scratch],
        micros=4.3,
        smem=1,
    )
    late_sum = SlotSum(late_keep, late_send)
    stat = struct((HEADS, rows, 1), F32)
    early_rows = packed_rows(early_columns(width, inner), width)
    outs, early_scratch = half_slots(early_rows, devices)
    result_out = result.T[None]
    arrived = after(arrived, result_out)
    mark = depth_valid
    mark = late_sum.step(mark)
    first_grad, d_attended, delta, early_norms, bn_grads, early_keep, early_send = call(
        middle_kernel,
        [model, head_low, stat, struct((4, width), F32), struct((2, width), F32)] + outs,
        [slots, after(arrived, late_keep, mark), statistics, bn_gain_row, d_normed, unit]
        + [from_low, from_high, clip_wide, valid_wide, depth_wide, left, right, gates, third_grad]
        + [second_sum, norm_gain, slope_early, first_sum, in_early, out_early, w_out_wide, attended]
        + [first_low, second_low, act_early, attended_low],
        scratch=[
            pltpu.VMEM((3, reached, LANES), F32),
            pltpu.VMEM((rows, width), F32),
            early_scratch,
        ],
        micros=12.0,
        smem=1,
    )
    early_sum = SlotSum(early_keep, early_send)
    mark = first_grad
    (depth_grad,) = tap_sums(after(gated_low, mark), 1, d_normed)
    mark = depth_grad
    mark = early_sum.step(mark)
    *d_frames, d_pair_weight, d_query_weight, d_pos_weight, d_bias, own_grad = attend_back(
        [len(order) for order in orders], after(query, mark), pairs, tables, clip_rows, clips,
        (frames_one, frames_two), log_total, delta, d_attended, shift, w_pos_wide, w_query, w_pair,
        own_cos, own_sin, turned, first_grad, head_width,
    )
    mark = own_grad
    late_sum.join(early_sum)
    both_sum = late_sum
    mark = both_sum.step(mark)
    last_rows = packed_rows(last_columns(width), width, 3 * SMALL)
    outs, packed = half_slots(last_rows, devices)
    last_keep, last_send = call(
        last_pack_kernel,
        outs,
        [slots, after(d_query_weight, mark), d_pair_weight, d_pos_weight, d_bias]
        + [depth_valid, depth_conv, depth_grad, statistics, bn_grads, bn_gain_row]
        + [late_norms, early_norms],
        scratch=[packed, pltpu.VMEM((block_rows(width + SMALL), 4 * width), F32)],
        micros=3.0,
        smem=1,
    )
    last_sum = SlotSum(last_keep, last_send)
    mark = last_keep
    frame_sum = FrameSum(d_frames[: seq_count // 2], [after(part, mark) for part in d_frames[seq_count // 2 :]])
    mark = both_sum.step(mark)
    mark = last_sum.step(mark)
    mark = both_sum.step(mark)
    frame_sum.step(mark)
    mark = frame_sum.joined[-1]
    mark = last_sum.step(mark)
    mark = last_sum.step(mark)
    mark = last_sum.step(mark, *frame_sum.arrived)
    input_grad = frame_sum.finish(own_grad)
    mark = both_sum.step(mark, input_grad)
    mark = last_sum.step(mark)
    both_keep, both_send = both_sum.finish()
    last_keep, last_send = last_sum.finish()
    last_share = share_rows(last_rows, devices) * devices
    square = struct((width, width), F32)
    sum_in, sum_out, sum_conv_in, sum_conv_out, sum_w_out = call(
        finish_two_kernel,
        [struct((width, 2, inner), F32)] * 2 + [struct((2 * width, width), F32), square, square],
        [slots, both_keep, both_send],
        scratch=[late_scratch, early_scratch],
        micros=10.0,
        smem=1,
    )
    sum_qkv, sum_pos, sum_rel, sum_gain, sum_bias, sum_depth = call(
        finish_last_kernel,
        [struct(w_qkv.shape, F32), struct(w_pos.shape, F32), struct(rel_bias.shape, F32)]
        + [struct(norm_gain.shape, F32), struct(norm_bias.shape, F32)]
        + [struct(conv_depth.shape, F32)],
        [slots, last_keep, last_send],
        scratch=[pltpu.VMEM((last_share, LANES), BF16)],
        micros=3.0,
        smem=1,
    )
    return (
        result_out,
        input_grad.T[None],
        sum_qkv,
        sum_pos,
        sum_w_out,
        sum_rel,
        sum_in.transpose(1, 0, 2),
        sum_out.transpose(1, 2, 0),
        sum_conv_in.T,
        sum_depth,
        sum_conv_out,
        bn_grads[0],
        bn_grads[1],
        sum_gain,
        sum_bias,
    )


def solution(mesh):
    whole = P()
    split = P("dp", "seq", None)
    return jax.shard_map(
        local,
        mesh=mesh,
        in_specs=(split,) + (whole,) * 13 + (P("dp", None), split),
        out_specs=(split, split) + (whole,) * 13,
        check_vma=False,
    )
```

```python
import functools
import math

import jax
import jax.numpy as jnp
from jax import lax
from jax.experimental import pallas as pl
from jax.experimental.pallas import tpu as pltpu
from jax.sharding import PartitionSpec as P
import numpy as np

HEADS = 4
LANES = 128
WIDE = 3 * LANES
HALO = 16
SMALL = 48
EPS = 1e-05
MODEL_AXES = ("seq", "dp")
VMEM_BYTES = 60 * 1024 * 1024
BF16 = jnp.bfloat16
F32 = jnp.float32


def device_count():
    return lax.axis_size("seq") * lax.axis_size("dp")


def flat_index():
    return lax.axis_index("seq") * lax.axis_size("dp") + lax.axis_index("dp")


def swap_flat(block, distance):
    pairs = [(i, i ^ distance) for i in range(device_count())]
    return lax.ppermute(block, MODEL_AXES, pairs)


def swap_seq(block, distance):
    pairs = [(i, i ^ distance) for i in range(lax.axis_size("seq"))]
    return lax.ppermute(block, "seq", pairs)


def shift_seq(block, step):
    count = lax.axis_size("seq")
    pairs = [(i, i + step) for i in range(count) if 0 <= i + step < count]
    return lax.ppermute(block, "seq", pairs)


def stage_radices(devices):
    radices = [2]
    left = devices // 2
    while left > 1:
        radix = 4 if left % 4 == 0 else 2
        radices.append(radix)
        left = left // radix
    return radices


def slot_pieces(devices, earlier):
    slots = jnp.arange(devices, dtype=jnp.int32)
    distance = jnp.zeros((devices,), jnp.int32)
    span = devices
    stride = 1
    for radix in stage_radices(devices):
        span = span // radix
        distance = distance + ((slots // span) % radix) * stride
        stride = stride * radix
    place = after(flat_index().astype(jnp.int32), earlier)
    return place ^ distance


def add_kernel(counts, radix, *refs):
    outs = refs[sum(counts) :]
    start = 0
    row = 0
    for count in counts:
        parts = refs[start : start + count]
        start = start + count
        total = parts[0][...].astype(F32)
        for part in parts[1:]:
            total = total + part[...].astype(F32)
        total = total.astype(BF16)
        span, share = total.shape[0] // radix, total.shape[1]
        for place, out in enumerate(outs):
            out[:, row : row + share] = total[place * span : (place + 1) * span]
        row = row + share


class SlotSum:
    def __init__(self, keep, send):
        self.others = []
        radices = stage_radices(device_count())
        strides = [1]
        for radix in radices[:-1]:
            strides.append(strides[-1] * radix)
        self.stages = list(zip(radices, strides))
        self.next = 1
        self.parts = self.scatter(0, [keep, send])
        self.mark = keep

    def join(self, other):
        self.others.append(other.parts)

    def scatter(self, stage, pieces):
        radix, stride = self.stages[stage]
        return [pieces[0]] + [
            swap_flat(pieces[step], step * stride) for step in range(radix - 1, 0, -1)
        ]

    def spread(self, stage, piece):
        radix, stride = self.stages[stage]
        return [piece] + [swap_flat(piece, step * stride) for step in range(1, radix)]

    def step(self, *earlier):
        count = len(self.stages)
        parts = self.parts
        if self.next >= 2 * count:
            return self.mark
        if earlier:
            parts = [after(parts[0], *earlier)] + parts[1:]
        if self.next <= count:
            radix = self.stages[self.next][0] if self.next < count else 1
            groups = [parts] + self.others
            self.others = []
            slots = parts[0].shape[0]
            if radix == 1:
                total = parts[0].astype(F32)
                for part in parts[1:]:
                    total = total + part.astype(F32)
                self.mark = total.astype(BF16)
                self.parts = self.spread(count - 1, self.mark)
                self.next = self.next + 1
                return self.mark
            share = sum(group[0].shape[1] for group in groups)
            pieces = call(
                functools.partial(add_kernel, [len(group) for group in groups], radix),
                [struct((slots // radix, share, LANES), BF16)] * radix,
                [part for group in groups for part in group],
                micros=2.0,
            )
            self.mark = pieces[0]
            self.parts = self.scatter(self.next, pieces)
        else:
            self.mark = jnp.concatenate(parts, axis=0)
            self.parts = self.spread(2 * count - 1 - self.next, self.mark)
        self.next = self.next + 1
        return self.mark

    def finish(self):
        while self.next < 2 * len(self.stages):
            self.step()
        return self.parts


def exchange_small(spread):
    return lax.all_to_all(spread, MODEL_AXES, 0, 0)


def after(value, *earlier):
    return lax.optimization_barrier((value,) + earlier)[0]


def arrival_order():
    count = lax.axis_size("seq")
    return [0, 1] + list(range(2, count, 2)), list(range(3, count, 2))


def gather_frames(shard, meanwhile):
    count = lax.axis_size("seq")
    across = [shard] + [swap_seq(shard, 2 * step) for step in range(1, count // 2)]
    made = meanwhile()
    blocks = []
    for step, block in enumerate(across):
        blocks.append(block)
        passed = block if step < count // 2 - 1 else after(block, made[0])
        blocks.append(swap_seq(passed, 1))
    return blocks, made


class FrameSum:
    def __init__(self, kept, passed):
        self.kept = kept
        self.passed = [swap_seq(pair, 1) for pair in passed]

    def step(self, *earlier):
        count = len(self.kept)
        self.arrived, self.joined = [], []
        for step in range(count - 1, 0, -1):
            came = self.passed[(count - 1 - step) // 2][(count - 1 - step) % 2]
            joined = self.kept[step].astype(F32) + came.astype(F32)
            if earlier:
                joined = after(joined, *earlier)
            self.joined.append(joined.astype(BF16))
            self.arrived.append(swap_seq(self.joined[-1], 2 * step))

    def finish(self, own):
        total = own + self.kept[0].astype(F32) + self.passed[-1][1].astype(F32)
        for block in self.arrived:
            total = total + block.astype(F32)
        return total


def cost(micros):
    return pl.CostEstimate(flops=int(micros * 0.460e9), bytes_accessed=0, transcendentals=0)


def call(body, outs, args, scratch=(), micros=2.0, smem=0):
    specs = [
        pl.BlockSpec(memory_space=pltpu.SMEM if place < smem else pltpu.VMEM)
        for place in range(len(args))
    ]
    return pl.pallas_call(
        body,
        out_shape=tuple(outs),
        in_specs=specs,
        out_specs=tuple(pl.BlockSpec(memory_space=pltpu.VMEM) for _ in outs),
        scratch_shapes=list(scratch),
        compiler_params=pltpu.CompilerParams(vmem_limit_bytes=VMEM_BYTES),
        cost_estimate=cost(micros),
    )(*args)


def struct(shape, dtype):
    return jax.ShapeDtypeStruct(tuple(shape), dtype)


def nn(left, right):
    return lax.dot_general(left, right, (((1,), (0,)), ((), ())), preferred_element_type=F32)


def nt(left, right):
    return lax.dot_general(left, right, (((1,), (1,)), ((), ())), preferred_element_type=F32)


def tn(left, right):
    return lax.dot_general(left, right, (((0,), (0,)), ((), ())), preferred_element_type=F32)


def norm_parts(summed):
    average = jnp.mean(summed, axis=-1, keepdims=True)
    centered = summed - average
    variance = jnp.mean(centered * centered, axis=-1, keepdims=True)
    inverse = lax.rsqrt(variance + EPS)
    return centered * inverse, inverse


def norm_back(unit, inverse, gain, incoming):
    scaled = incoming * gain
    first = jnp.mean(scaled, axis=-1, keepdims=True)
    second = jnp.mean(scaled * unit, axis=-1, keepdims=True)
    grad = inverse * (scaled - first - unit * second)
    return (
        grad,
        jnp.sum(incoming * unit, axis=0, keepdims=True),
        jnp.sum(incoming, axis=0, keepdims=True),
    )


def sigmoid(value):
    return 0.5 * jnp.tanh(0.5 * value) + 0.5


def silu_back(value):
    gate = sigmoid(value)
    return gate * (1.0 + value * (1.0 - gate))


def store_tile(ref, rows, copies):
    tile = jnp.zeros((8, LANES), F32)
    parts = []
    for row in rows:
        width = row.shape[1]
        blocks = -(-width // LANES)
        wide = row
        if blocks * LANES > width:
            wide = jnp.concatenate([row, jnp.zeros((1, blocks * LANES - width), F32)], axis=1)
        for block in range(blocks):
            parts.append(wide[:, block * LANES : (block + 1) * LANES])
    for place, part in enumerate(parts):
        tile = jnp.where(
            lax.broadcasted_iota(jnp.int32, (8, LANES), 0) == place,
            jnp.broadcast_to(part, (8, LANES)),
            tile,
        )
    ref[...] = jnp.broadcast_to(tile[None], (copies, 8, LANES))


def tile_row(tile, place, width):
    blocks = -(-width // LANES)
    parts = [tile[place * blocks + block : place * blocks + block + 1] for block in range(blocks)]
    return jnp.concatenate(parts, axis=1)[:, :width]


def plan_blocks(columns):
    runs = []
    block = 0
    for count in columns:
        full = count // LANES
        runs.append([(block + place, 0, place * LANES, LANES) for place in range(full)])
        block = block + full
    open_block, lane = None, LANES
    for place, count in enumerate(columns):
        rest = count % LANES
        if rest:
            if lane + rest > LANES:
                open_block, lane = block, 0
                block = block + 1
            runs[place].append((open_block, lane, count - rest, rest))
            lane = lane + rest
    return runs, block


def block_rows(rows):
    return -(-rows // 8) * 8


def store_matrix(packed, runs, value):
    rows = value.shape[0]
    low = value.astype(BF16)
    for block, lane, column, count in runs:
        start = block * block_rows(rows)
        packed[start : start + rows, lane : lane + count] = low[:, column : column + count]


def load_matrix(packed, runs, out, rows, row=0):
    for block, lane, column, count in runs:
        start = block * block_rows(rows)
        out[row : row + rows, column : column + count] = packed[
            start : start + rows, lane : lane + count
        ].astype(F32)


def load_layer(packed, runs, out, layer):
    rows = out.shape[0]
    for block, lane, column, count in runs:
        start = block * block_rows(rows)
        out[:, layer, column : column + count] = packed[
            start : start + rows, lane : lane + count
        ].astype(F32)


def spread_pieces(slots_ref, packed, keep_ref, send_ref):
    half, share = keep_ref.shape[:2]

    def one(slot, nothing):
        low = pl.multiple_of(slots_ref[slot] * share, HALO)
        keep_ref[slot] = packed[pl.ds(low, share), :]
        high = pl.multiple_of(slots_ref[slot + half] * share, HALO)
        send_ref[slot] = packed[pl.ds(high, share), :]
        return nothing

    lax.fori_loop(0, half, one, 0)


def collect_pieces(slots_ref, keep_ref, send_ref, packed, row=0):
    half = keep_ref.shape[0]
    share = packed.shape[0] // (2 * half)

    def one(slot, nothing):
        low = pl.multiple_of(slots_ref[slot] * share, HALO)
        packed[pl.ds(low, share), :] = keep_ref[slot, row : row + share]
        high = pl.multiple_of(slots_ref[slot + half] * share, HALO)
        packed[pl.ds(high, share), :] = send_ref[slot, row : row + share]
        return nothing

    lax.fori_loop(0, half, one, 0)


def share_rows(rows, devices):
    return -(-rows // (HALO * devices)) * HALO


def half_slots(rows, devices):
    share = share_rows(rows, devices)
    return [struct((devices // 2, share, LANES), BF16)] * 2, pltpu.VMEM((devices * share, LANES), BF16)


def wave_tables(rows, blocks, width):
    half = width // 2
    frequency = np.exp(np.arange(half) * (-2.0 * math.log(10000.0) / width))
    tail = np.zeros(LANES // 2)
    tail[: half - LANES] = frequency[LANES:]
    lanes = np.concatenate([frequency[:LANES], frequency[:LANES], tail, tail])[None]
    row_angles = np.arange(rows)[:, None] * lanes
    block_angles = (np.arange(blocks) * rows)[:, None] * lanes
    return [
        jnp.asarray(table.astype(np.float32))
        for table in (
            np.cos(row_angles),
            np.sin(row_angles),
            np.cos(block_angles),
            np.sin(block_angles),
        )
    ]


def half_pieces(width):
    half = width // 2
    rest = half - LANES
    return (
        (0, 0, LANES),
        (half, LANES, LANES),
        (LANES, 2 * LANES, rest),
        (half + LANES, 2 * LANES + LANES // 2, rest),
    )


def half_sign():
    lane = lax.broadcasted_iota(jnp.int32, (1, LANES), 1)
    return jnp.where(lane < LANES // 2, 1.0, -1.0)


def prepare_kernel(orders, where, lengths, turned, w_qkv, w_pos, w_out, bias, depth, base_cos, base_sin, block_cos, block_sin, block, query, shift, w_query, w_pair, w_pos_wide, w_out_wide, depth_wide, own_cos, own_sin, clip_rows, clip_wide, valid_wide, valid_rows, *by_order):
    place = where[0]
    width, rows = turned.shape
    size = width // HEADS
    blocks = block_cos.shape[0]
    w_query[...] = jnp.zeros_like(w_query)
    w_pair[...] = jnp.zeros_like(w_pair)
    w_pos_wide[...] = jnp.zeros_like(w_pos_wide)
    w_out_wide[...] = jnp.zeros_like(w_out_wide)
    depth_wide[...] = jnp.zeros_like(depth_wide)
    depth_wide[:, :width] = depth[...]
    for head in range(HEADS):
        natural = slice(head * size, (head + 1) * size)
        low = head * LANES
        w_query[:, low : low + size] = w_qkv[:, head * size : (head + 1) * size]
        w_pair[head, :, :size] = w_qkv[:, width + head * size : width + (head + 1) * size]
        w_pair[head, :, LANES : LANES + size] = w_qkv[
            :, 2 * width + head * size : 2 * width + (head + 1) * size
        ]
        w_out_wide[low : low + size] = w_out[natural]
        for source, target, length in half_pieces(width):
            w_pos_wide[target : target + length, low : low + size] = w_pos[
                source : source + length, natural
            ]
    lane = lax.broadcasted_iota(jnp.int32, (1, WIDE), 1)
    on_cosine = (lane < LANES) | ((lane >= 2 * LANES) & (lane < 2 * LANES + LANES // 2))
    row_cos, row_sin = base_cos[...], base_sin[...]
    ends = [lengths[0, 0]]
    for clip in range(1, lengths.shape[1]):
        ends.append(ends[-1] + lengths[0, clip])

    def clip_at(frames):
        clip = jnp.zeros_like(frames)
        for end in ends:
            clip = clip + (frames >= end).astype(jnp.int32)
        return clip

    for order, table, clip_columns in zip(orders, by_order[0::2], by_order[1::2]):
        for step, distance in enumerate(order):
            here = place ^ distance
            cosine = block_cos[pl.ds(here, 1), :]
            sine = block_sin[pl.ds(here, 1), :]
            one = jnp.where(on_cosine, cosine, sine)
            two = jnp.where(on_cosine, -sine, cosine)
            lanes = slice(step * rows, (step + 1) * rows)
            table[:, lanes] = (one * row_cos + two * row_sin).astype(BF16).T
            clip_columns[:, lanes] = clip_at(
                here * rows + lax.broadcasted_iota(jnp.int32, (1, rows), 1)
            )
    reached = place * rows - HALO + lax.broadcasted_iota(jnp.int32, (rows + 2 * HALO, LANES), 0)
    inside = (reached >= 0) & (reached < blocks * rows)
    reached_clip = jnp.where(inside, clip_at(reached), -1)
    clip_wide[...] = reached_clip
    clip_rows[...] = reached_clip[HALO : HALO + rows, 0:1]
    valid = (inside & (reached < ends[-1])).astype(F32)[:, 0:1]
    valid_wide[...] = valid
    valid_rows[...] = valid[HALO : HALO + rows]
    block_cosine = block_cos[pl.ds(place, 1), :]
    block_sine = block_sin[pl.ds(place, 1), :]
    cosines = block_cosine * row_cos - block_sine * row_sin
    sines = block_sine * row_cos + block_cosine * row_sin
    own_cos[...] = cosines
    own_sin[...] = sines
    frames = turned[...].T
    block[...] = frames
    projected = nn(frames, w_query[...])
    sign = half_sign()
    for head in range(HEADS):
        lanes = slice(head * LANES, (head + 1) * LANES)
        natural = slice(head * size, (head + 1) * size)
        wide = jnp.zeros((2, LANES - size), F32)
        added = jnp.concatenate([bias[:, natural], wide], axis=1)
        unit = (projected[:, lanes] + added[0:1]).astype(BF16)
        moved = (projected[:, lanes] + added[1:2]).astype(BF16)
        shift[:, lanes] = moved
        shifted = nt(moved, w_pos_wide[:, lanes])
        first, second = shifted[:, :LANES], shifted[:, LANES : 2 * LANES]
        tail = shifted[:, 2 * LANES :]
        sine, cosine = sines[:, :LANES], cosines[:, :LANES]
        query[head, :, :LANES] = unit
        query[head, :, LANES : 2 * LANES] = (first * sine + second * cosine).astype(BF16)
        query[head, :, 2 * LANES : 3 * LANES] = (second * sine - first * cosine).astype(BF16)
        query[head, :, 3 * LANES :] = (
            tail * sines[:, 2 * LANES :]
            + pltpu.roll(tail, LANES // 2, 1) * cosines[:, 2 * LANES :] * sign
        ).astype(BF16)


def masked_scores(query, upper, table, clip_rows, clip_columns, scale):
    raw = nn(query[:, : 2 * LANES], upper) + nn(query[:, 2 * LANES :], table[LANES:])
    return jnp.where(clip_rows == clip_columns, raw * (scale / math.log(2.0)), -1e30)


def attend_kernel(scale, count, last, *refs):
    blocks = refs[:count]
    query, w_pair, table, clip_rows, clip_columns = refs[count : count + 5]
    carried = refs[count + 5 : count + 8] if last else None
    outs = refs[count + (8 if last else 5) :]
    rows = blocks[0].shape[1]
    heads = query.shape[0]
    frames_all, pair = outs[-2:]

    @pl.when(pl.program_id(0) == 0)
    def _():
        for step in range(count):
            frames_all[:, step * rows : (step + 1) * rows] = blocks[step][...]

    def scored(head):
        both = tn(w_pair[head], frames_all[...]).astype(BF16)
        pair[head] = both
        upper = jnp.concatenate([both[:LANES], table[:LANES]], axis=0)
        return both[LANES:], masked_scores(
            query[head], upper, table[...], clip_rows[...], clip_columns[...], scale
        )

    following = scored(0)
    for head in range(heads):
        values, scores = following
        if head + 1 < heads:
            following = scored(head + 1)
        lanes = slice(head * LANES, (head + 1) * LANES)
        highest = jnp.max(scores, axis=1, keepdims=True)
        if last:
            highest = jnp.maximum(highest, carried[0][head])
        weights = jnp.exp2(scores - highest)
        total = jnp.sum(weights, axis=1, keepdims=True)
        summed = nt(weights.astype(BF16), values)
        if last:
            fade = jnp.exp2(carried[0][head] - highest)
            total = total + carried[1][head] * fade
            summed = summed + carried[2][:, lanes] * fade
            attended, log_total = outs[:2]
            attended[:, lanes] = summed / total
            log_total[head] = highest + jnp.log2(total)
        else:
            outs[0][head] = highest
            outs[1][head] = total
            outs[2][:, lanes] = summed


def heads_at_once(frames):
    return 2 if frames <= 2048 else 1


def attend(blocks, query, w_pair, table, clip_rows, clip_columns, head_width, carried=()):
    rows = query.shape[1]
    frames = table.shape[1]
    width = w_pair.shape[1]
    per = heads_at_once(frames)
    stat = pl.BlockSpec((per, rows, 1), lambda h: (h, 0, 0))
    head = pl.BlockSpec((rows, per * LANES), lambda h: (0, h))
    stat_shape = struct((HEADS, rows, 1), F32)
    head_shape = struct((rows, HEADS * LANES), F32)
    last = len(carried) > 0
    return pl.pallas_call(
        functools.partial(attend_kernel, 1.0 / math.sqrt(head_width), len(blocks), last),
        grid=(HEADS // per,),
        in_specs=[pl.BlockSpec((width, rows), lambda h: (0, 0)) for _ in blocks]
        + [
            pl.BlockSpec((per, rows, 4 * LANES), lambda h: (h, 0, 0)),
            pl.BlockSpec((per, width, 2 * LANES), lambda h: (h, 0, 0)),
            pl.BlockSpec((WIDE, frames), lambda h: (0, 0)),
            pl.BlockSpec((rows, 1), lambda h: (0, 0)),
            pl.BlockSpec((1, frames), lambda h: (0, 0)),
        ]
        + ([stat, stat, head] if last else []),
        out_specs=((head, stat) if last else (stat, stat, head))
        + (
            pl.BlockSpec((width, frames), lambda h: (0, 0)),
            pl.BlockSpec((per, 2 * LANES, frames), lambda h: (h, 0, 0)),
        ),
        out_shape=((head_shape, stat_shape) if last else (stat_shape, stat_shape, head_shape))
        + (struct((width, frames), BF16), struct((HEADS, 2 * LANES, frames), BF16)),
        compiler_params=pltpu.CompilerParams(vmem_limit_bytes=VMEM_BYTES),
        cost_estimate=cost(5.0 if last else 8.0),
    )(*blocks, query, w_pair, table, clip_rows, clip_columns, *carried)


def early_kernel(block, attended, w_out, gains, biases, ffn_in, ffn_out, gates, first_sum, second_sum, second_norm, left, right, gated, attended_low):
    low = attended[...].astype(BF16)
    attended_low[...] = low
    summed = block[...].astype(F32) + nn(low, w_out[...])
    first_sum[...] = summed
    unit, _ = norm_parts(summed)
    first = unit * gains[0:1] + biases[0:1]
    inner = nn(first.astype(BF16), ffn_in[...])
    act = (inner * sigmoid(inner)).astype(BF16)
    summed = first + nt(act, ffn_out[...])
    second_sum[...] = summed
    unit, _ = norm_parts(summed)
    second = unit * gains[1:2] + biases[1:2]
    second_norm[...] = second
    second_low = second.astype(BF16)
    half = gates.shape[0] // 2
    one = nt(second_low, gates[:half])
    two = nt(second_low, gates[half:])
    left[...] = one
    right[...] = two
    gated[...] = jnp.zeros_like(gated)
    gated[:, : one.shape[1]] = (one * sigmoid(two)).astype(BF16)


def again_kernel(first_sum, second_sum, gains, biases, ffn_in, first_low_out, second_low_out, act_out, slope_out):
    unit, _ = norm_parts(second_sum[...])
    second_low_out[...] = (unit * gains[1:2] + biases[1:2]).astype(BF16)
    unit, _ = norm_parts(first_sum[...])
    first_low = (unit * gains[0:1] + biases[0:1]).astype(BF16)
    first_low_out[...] = first_low
    inner = nn(first_low, ffn_in[...])
    gate = sigmoid(inner)
    act_out[...] = (inner * gate).astype(BF16)
    slope_out[...] = (gate * (1.0 + inner * (1.0 - gate))).astype(BF16)


def lane_blocks(width):
    return [(lane, min(LANES, width - lane)) for lane in range(0, width, LANES)]


def extend(extended, low, middle, high):
    rows, width = middle.shape
    for block, (lane, count) in enumerate(lane_blocks(width)):
        if count < LANES:
            extended[block] = jnp.zeros((rows + 2 * HALO, LANES), F32)
        extended[block, 0:HALO, :count] = low[:, lane : lane + count].astype(F32)
        extended[block, HALO : HALO + rows, :count] = middle[:, lane : lane + count].astype(F32)
        extended[block, HALO + rows :, :count] = high[:, lane : lane + count].astype(F32)


def convolve(extended, clip, depth, mirrored, store):
    taps = depth.shape[0]
    blocks, rows, _ = extended.shape
    rows = rows - 2 * HALO
    step = 64
    for start in range(0, rows, step):
        own = clip[HALO + start : HALO + start + step]
        sums = [jnp.zeros((step, LANES), F32) for _ in range(blocks)]
        for tap in range(taps):
            place = HALO - taps // 2 + tap + start
            same = clip[place : place + step] == own
            row = taps - 1 - tap if mirrored else tap
            for block in range(blocks):
                lanes = slice(block * LANES, (block + 1) * LANES)
                sums[block] = sums[block] + depth[row : row + 1, lanes] * jnp.where(
                    same, extended[block, place : place + step], 0.0
                )
        store(start, step, jnp.concatenate(sums, axis=1))


def conv_kernel(copies, low, middle, high, clip, depth, valid, convolved, tile, extended):
    rows, width = convolved.shape
    extend(extended, low[...], middle[...], high[...])

    def store(start, step, value):
        convolved[start : start + step] = value[:, :width]

    convolve(extended, clip, depth, False, store)
    value = convolved[...]
    kept = value * valid[...]
    count = jnp.zeros((1, width), F32) + jnp.sum(valid[...], axis=0, keepdims=True)
    store_tile(
        tile,
        [
            jnp.sum(kept, axis=0, keepdims=True),
            jnp.sum(kept * value, axis=0, keepdims=True),
            count[:, :LANES],
        ],
        copies,
    )


def taps_kernel(taps, count, low, middle, high, clip, *refs):
    factor, *valid = refs[: 1 if count == 1 else 2]
    outs, extended = refs[len(valid) + 1 : -1], refs[-1]
    rows, width = factor.shape
    extend(extended, low[...], middle[...], high[...])
    step = 64
    sums = [[[None] * 3 for _ in range(taps)] for _ in range(count)]
    for start in range(0, rows, step):
        own = clip[HALO + start : HALO + start + step]
        for block, (lane, lanes) in enumerate(lane_blocks(width)):
            part = factor[start : start + step, lane : lane + lanes]
            if lanes < LANES:
                part = jnp.concatenate([part, jnp.zeros((step, LANES - lanes), F32)], axis=1)
            here = [part]
            if valid:
                kept = valid[0][start : start + step]
                here = [jnp.broadcast_to(kept, (step, LANES)), part * kept]
            for tap in range(taps):
                place = HALO - taps // 2 + tap + start
                same = clip[place : place + step] == own
                there = jnp.where(same, extended[block, place : place + step], 0.0)
                for which in range(count):
                    part = jnp.sum((there * here[which]).reshape(step // 8, 8, LANES), axis=0)
                    old = sums[which][tap][block]
                    sums[which][tap][block] = part if old is None else old + part
    for which in range(count):
        for tap in range(taps):
            outs[which][tap : tap + 1] = jnp.concatenate(
                [jnp.sum(part, axis=0, keepdims=True) for part in sums[which][tap]], axis=1
            )[:, :width]


def late_kernel(copies, arrived, convolved, second_norm, bn_gain, bn_bias, conv_out, gains, biases, ffn_in, ffn_out, cotangent, result, act_out, d_inner_out, third_low_out, fourth_grad_out, swished_out, third_grad_out, third_grad, d_normed_out, unit_out, tile, norm_grads, statistics, edge_low, edge_high):
    width = convolved.shape[1]
    rows = convolved.shape[0]
    sums = jnp.sum(arrived[...], axis=0)
    frames = sums[6:7, 0:1]
    mean = tile_row(sums, 0, width) / frames
    variance = tile_row(sums, 1, width) / frames - mean * mean
    inverse = lax.rsqrt(variance + EPS)
    unit = (convolved[...] - mean) * inverse
    unit_out[...] = unit
    statistics[...] = jnp.zeros_like(statistics)
    statistics[0:1, :width] = inverse
    statistics[1:2, :width] = jnp.broadcast_to(frames, (1, width))
    statistics[2:3, :width] = mean
    normed = unit * bn_gain[...] + bn_bias[...]
    swished = (normed * sigmoid(normed)).astype(BF16)
    swished_out[...] = swished
    third_unit, third_inverse = norm_parts(second_norm[...] + nn(swished, conv_out[...]))
    third = third_unit * gains[2:3] + biases[2:3]
    third_low = third.astype(BF16)
    third_low_out[...] = third_low
    inner = nn(third_low, ffn_in[...])
    gate = sigmoid(inner)
    act = (inner * gate).astype(BF16)
    act_out[...] = act
    fourth_unit, fourth_inverse = norm_parts(third + nt(act, ffn_out[...]))
    result[...] = (fourth_unit * gains[3:4] + biases[3:4]).T
    fourth_grad, gain_three, bias_three = norm_back(
        fourth_unit, fourth_inverse, gains[3:4], cotangent[...].T
    )
    fourth_low = fourth_grad.astype(BF16)
    fourth_grad_out[...] = fourth_low
    d_act = nn(fourth_low, ffn_out[...])
    d_inner = (d_act * (gate * (1.0 + inner * (1.0 - gate)))).astype(BF16)
    d_inner_out[...] = d_inner
    grad, gain_two, bias_two = norm_back(
        third_unit, third_inverse, gains[2:3], fourth_grad + nt(d_inner, ffn_in[...])
    )
    third_grad[...] = grad
    grad_low = grad.astype(BF16)
    third_grad_out[...] = grad_low
    d_normed = nt(grad_low, conv_out[...]) * silu_back(normed)
    d_normed_out[...] = d_normed
    store_tile(
        tile,
        [
            jnp.sum(d_normed * unit, axis=0, keepdims=True),
            jnp.sum(d_normed, axis=0, keepdims=True),
        ],
        copies,
    )
    norm_grads[0:1] = gain_two
    norm_grads[1:2] = gain_three
    norm_grads[2:3] = bias_two
    norm_grads[3:4] = bias_three
    edge_low[0] = d_normed[:HALO]
    edge_low[1] = unit[:HALO]
    edge_high[0] = d_normed[rows - HALO :]
    edge_high[1] = unit[rows - HALO :]


def late_columns(width, inner):
    return (inner, inner, width)


def early_columns(width, inner):
    return (inner, inner, width, width, width)


def last_columns(width):
    return (3 * width, width)


def packed_rows(columns, width, small=0):
    _, blocks = plan_blocks(columns)
    return blocks * block_rows(width) + small


def late_grads_kernel(slots, third_low, d_inner, act, fourth_grad, swished, third_grad, keep, send, packed):
    width = third_low.shape[1]
    runs, _ = plan_blocks(late_columns(width, act.shape[1]))
    store_matrix(packed, runs[0], tn(third_low[...], d_inner[...]))
    store_matrix(packed, runs[1], tn(fourth_grad[...], act[...]))
    store_matrix(packed, runs[2], tn(swished[...], third_grad[...]))
    spread_pieces(slots, packed, keep, send)


def middle_kernel(slots, arrived, statistics, bn_gain, d_normed, unit, from_low, from_high, clip, valid, depth, left, right, gates, third_grad, second_sum, gains, slope, first_sum, ffn_in, ffn_out, w_out, attended, first_low, second_low, act, attended_low, first_grad, d_attended, delta, norm_grads, bn_grads, keep, send, extended, d_gated, packed):
    rows, width = left.shape
    sums = jnp.sum(arrived[...], axis=0)
    gain_sum = tile_row(sums, 0, width)
    bias_sum = tile_row(sums, 1, width)
    bn_grads[0:1] = gain_sum
    bn_grads[1:2] = bias_sum
    gain = bn_gain[...]
    inverse = statistics[0:1, :width]
    frames = statistics[1:2, :width]

    def conv_grad(d_rows, unit_rows, valid_rows):
        return (
            inverse * gain * (d_rows - valid_rows * (bias_sum + unit_rows * gain_sum) / frames)
        ).astype(BF16)

    extend(
        extended,
        conv_grad(from_low[0], from_low[1], valid[0:HALO]),
        conv_grad(d_normed[...], unit[...], valid[HALO : HALO + rows]),
        conv_grad(from_high[0], from_high[1], valid[HALO + rows :]),
    )

    def store(start, step, value):
        d_gated[start : start + step] = value[:, :width]

    convolve(extended, clip, depth, True, store)
    gate = sigmoid(right[...])
    d_left = (d_gated[...] * gate).astype(BF16)
    d_right = (d_gated[...] * left[...] * gate * (1.0 - gate)).astype(BF16)
    second_unit, second_inverse = norm_parts(second_sum[...])
    half = gates.shape[0] // 2
    incoming = third_grad[...] + nn(d_left, gates[:half]) + nn(d_right, gates[half:])
    second_grad, gain_one, bias_one = norm_back(
        second_unit, second_inverse, gains[1:2], incoming
    )
    second_grad_low = second_grad.astype(BF16)
    d_act = nn(second_grad_low, ffn_out[...])
    d_inner = (d_act * slope[...].astype(F32)).astype(BF16)
    first_unit, first_inverse = norm_parts(first_sum[...])
    grad, gain_zero, bias_zero = norm_back(
        first_unit, first_inverse, gains[0:1], second_grad + nt(d_inner, ffn_in[...])
    )
    first_grad[...] = grad
    grad_low = grad.astype(BF16)
    for place, part in enumerate((gain_zero, gain_one, bias_zero, bias_one)):
        norm_grads[place : place + 1] = part
    back = nt(grad_low, w_out[...]).astype(BF16)
    d_attended[...] = back
    product = back.astype(F32) * attended[...]
    for head in range(HEADS):
        delta[head] = jnp.sum(
            product[:, head * LANES : (head + 1) * LANES], axis=1, keepdims=True
        )
    size = width // HEADS
    runs, _ = plan_blocks(early_columns(width, act.shape[1]))
    store_matrix(packed, runs[0], tn(first_low[...], d_inner))
    store_matrix(packed, runs[1], tn(second_grad_low, act[...]))
    store_matrix(packed, runs[2], tn(d_left, second_low[...]))
    store_matrix(packed, runs[3], tn(d_right, second_low[...]))
    d_out = tn(attended_low[...], grad_low)
    store_matrix(
        packed,
        runs[4],
        jnp.concatenate([d_out[head * LANES : head * LANES + size] for head in range(HEADS)], axis=0),
    )
    spread_pieces(slots, packed, keep, send)


def attend_back_kernel(scale, counts, query, pair_one, pair_two, table_one, table_two, clip_rows, clip_one, clip_two, frames_one, frames_two, log_total, delta, d_attended, shift, w_pos, w_query, w_pair, own_cos, own_sin, turned, first_grad, *refs):
    blocks = sum(counts)
    kept, passed = refs[: blocks // 2], refs[blocks // 2 : blocks // 2 + blocks // 4]
    d_pair_weight, d_query_weight, d_pos_weight, d_bias, own_grad, d_frames, d_pair, own_sum = refs[
        blocks // 2 + blocks // 4 :
    ]
    group = pl.program_id(0)
    rows = clip_rows.shape[0]
    heads = query.shape[0]
    cosines, sines = own_cos[...], own_sin[...]
    runs = (
        (pair_one, table_one, clip_one, frames_one),
        (pair_two, table_two, clip_two, frames_two),
    )
    pieces = []
    start = 0
    for run in runs:
        for low in range(0, run[3].shape[1], 5 * rows):
            length = min(5 * rows, run[3].shape[1] - low)
            pieces.append(run + (slice(low, low + length), slice(start, start + length)))
            start = start + length
    work = [(head, piece) for head in range(heads) for piece in pieces]

    def scored(head, piece):
        pair, table, clip_columns, _, here, _ = piece
        lanes = slice(head * LANES, (head + 1) * LANES)
        upper = jnp.concatenate([pair[head, :LANES, here], table[:LANES, here]], axis=0)
        scores = masked_scores(
            query[head], upper, table[:, here], clip_rows[...], clip_columns[:, here], scale
        )
        return upper, scores, nn(d_attended[:, lanes], pair[head, LANES:, here])

    following = scored(*work[0])
    for place, (head, piece) in enumerate(work):
        _, table, _, frames, here, span = piece
        lanes = slice(head * LANES, (head + 1) * LANES)
        upper, scores, slope = following
        if place + 1 < len(work):
            following = scored(*work[place + 1])
        probs = jnp.exp2(scores - log_total[head])
        d_raw = (probs * (slope * scale - delta[head] * scale)).astype(BF16)
        d_pair[:LANES, span] = nn(query[head, :, :LANES].T, d_raw).astype(BF16)
        d_pair[LANES:, span] = nn(d_attended[:, lanes].T, probs.astype(BF16)).astype(BF16)
        first_piece = place % len(pieces) == 0
        unit_part = nt(d_raw, upper)
        rest_part = nt(d_raw, table[LANES:, here])
        weight_part = nt(frames[:, here], d_pair[:, span])
        unit_sum = unit_part if first_piece else unit_sum + unit_part
        rest_sum = rest_part if first_piece else rest_sum + rest_part
        weight_sum = weight_part if first_piece else weight_sum + weight_part
        by_frame = nn(w_pair[head], d_pair[:, span])
        if head > 0:
            d_frames[:, span] += by_frame
        else:

            @pl.when(group == 0)
            def _():
                d_frames[:, span] = by_frame

            @pl.when(group > 0)
            def _():
                d_frames[:, span] += by_frame

        if place % len(pieces) < len(pieces) - 1:
            continue
        d_pair_weight[head] = weight_sum.astype(BF16)
        d_unit = unit_sum[:, :LANES]
        first, second = unit_sum[:, LANES:], rest_sum[:, :LANES]
        tail = rest_sum[:, LANES:]
        sine, cosine = sines[:, :LANES], cosines[:, :LANES]
        d_shifted = jnp.concatenate(
            [
                first * sine - second * cosine,
                first * cosine + second * sine,
                tail * sines[:, 2 * LANES :]
                - pltpu.roll(tail, LANES // 2, 1) * cosines[:, 2 * LANES :] * half_sign(),
            ],
            axis=1,
        ).astype(BF16)
        d_from_pos = nn(d_shifted, w_pos[:, lanes])
        d_query = (d_unit + d_from_pos).astype(BF16)
        d_query_weight[:, lanes] = nn(turned[...], d_query).astype(BF16)
        d_pos_weight[:, lanes] = tn(d_shifted, shift[:, lanes]).astype(BF16)
        d_bias[0:1, lanes] = jnp.sum(d_unit, axis=0, keepdims=True)
        d_bias[1:2, lanes] = jnp.sum(d_from_pos, axis=0, keepdims=True)
        own = nt(d_query, w_query[:, lanes])
        if head > 0:
            own_sum[...] += own
        else:

            @pl.when(group == 0)
            def _():
                own_sum[...] = first_grad[...] + own

            @pl.when(group > 0)
            def _():
                own_sum[...] += own

    @pl.when(group == HEADS // heads - 1)
    def _():
        own_grad[...] = own_sum[...].T
        orders = [0, 1] + list(range(2, blocks, 2)) + list(range(3, blocks, 2))
        for step in range(blocks // 2):
            lanes = orders.index(2 * step) * rows
            kept[step][...] = d_frames[:, lanes : lanes + rows].astype(BF16)
            lanes = orders.index(2 * step + 1) * rows
            place = blocks // 2 - 1 - step
            passed[place // 2][place % 2] = d_frames[:, lanes : lanes + rows].astype(BF16)


def attend_back(counts, query, pairs, tables, clip_rows, clips, frames, log_total, delta, d_attended, shift, w_pos, w_query, w_pair, own_cos, own_sin, turned, first_grad, head_width):
    rows = query.shape[1]
    width = turned.shape[0]
    wide = HEADS * LANES
    blocks = sum(counts)
    total = blocks * rows
    per = heads_at_once(total)

    def whole(array):
        return pl.BlockSpec(
            array.shape, lambda h: (0,) * len(array.shape), pipeline_mode=pl.Buffered(1)
        )

    def by_head(array):
        return pl.BlockSpec((per,) + array.shape[1:], lambda h: (h, 0, 0))

    def head_lanes(array):
        return pl.BlockSpec((array.shape[0], per * LANES), lambda h: (0, h))

    kept = [struct((width, rows), BF16)] * (blocks // 2)
    passed = [struct((2, width, rows), BF16)] * (blocks // 4)
    by_head_shapes = [struct((HEADS, width, 2 * LANES), BF16)]
    by_lane_shapes = [struct((width, wide), BF16), struct((WIDE, wide), BF16), struct((2, wide), F32)]
    own = struct((width, rows), F32)
    return pl.pallas_call(
        functools.partial(attend_back_kernel, 1.0 / math.sqrt(head_width), counts),
        grid=(HEADS // per,),
        in_specs=[by_head(query)]
        + [by_head(pair) for pair in pairs]
        + [whole(table) for table in tables]
        + [whole(clip_rows)]
        + [whole(clip) for clip in clips]
        + [whole(part) for part in frames]
        + [by_head(log_total), by_head(delta), head_lanes(d_attended), head_lanes(shift)]
        + [head_lanes(w_pos), head_lanes(w_query), by_head(w_pair), whole(own_cos)]
        + [whole(own_sin), whole(turned), whole(first_grad)],
        out_specs=tuple(whole(shape) for shape in kept + passed)
        + tuple(by_head(shape) for shape in by_head_shapes)
        + tuple(head_lanes(shape) for shape in by_lane_shapes)
        + (whole(own),),
        out_shape=tuple(kept + passed + by_head_shapes + by_lane_shapes + [own]),
        scratch_shapes=[
            pltpu.VMEM((width, total), F32),
            pltpu.VMEM((2 * LANES, total), BF16),
            pltpu.VMEM((rows, width), F32),
        ],
        compiler_params=pltpu.CompilerParams(vmem_limit_bytes=VMEM_BYTES),
        cost_estimate=cost(20.0),
    )(query, *pairs, *tables, clip_rows, *clips, *frames, log_total, delta, d_attended, shift, w_pos, w_query, w_pair, own_cos, own_sin, turned, first_grad)


def last_pack_kernel(slots, d_query_weight, d_pair_weight, d_pos, d_bias, depth_valid, depth_conv, depth_grad, statistics, bn_grads, bn_gain, late_norms, early_norms, keep, send, packed, natural):
    width = d_query_weight.shape[0]
    size = width // HEADS
    runs, total = plan_blocks(last_columns(width))
    for head in range(HEADS):
        lanes = slice(head * size, (head + 1) * size)
        low = head * LANES
        natural[:width, lanes] = d_query_weight[:, low : low + size].astype(F32)
        natural[:width, width + head * size : width + (head + 1) * size] = d_pair_weight[
            head, :, :size
        ].astype(F32)
        natural[:width, 2 * width + head * size : 2 * width + (head + 1) * size] = d_pair_weight[
            head, :, LANES : LANES + size
        ].astype(F32)
        for start, spread, length in half_pieces(width):
            natural[start : start + length, 3 * width + head * size : 3 * width + (head + 1) * size] = (
                d_pos[spread : spread + length, low : low + size].astype(F32)
            )
        natural[width : width + 2, lanes] = d_bias[:, low : low + size]
    taps = depth_valid.shape[0]
    inverse, frames, mean = (statistics[row : row + 1, :width] for row in range(3))
    gain_sum, bias_sum = bn_grads[0:1], bn_grads[1:2]
    by_unit = (depth_conv[...] - mean * depth_valid[...]) * inverse
    d_depth = (
        inverse
        * bn_gain[...]
        * (depth_grad[...] - (bias_sum * depth_valid[...] + gain_sum * by_unit) / frames)
    )
    natural[width + 2 : width + 6, :width] = early_norms[...]
    natural[width + 6 : width + 10, :width] = late_norms[...]
    natural[width + 10 : width + 10 + taps, :width] = d_depth
    store_matrix(packed, runs[0], natural[:width, : 3 * width])
    store_matrix(packed, runs[1], natural[:width, 3 * width :])
    start = total * block_rows(width)
    for lane in range(0, width, LANES):
        count = min(LANES, width - lane)
        packed[start : start + 10 + taps, :count] = natural[
            width : width + 10 + taps, lane : lane + count
        ].astype(BF16)
        start = start + SMALL
    spread_pieces(slots, packed, keep, send)


def finish_two_kernel(slots, keep, send, ffn_in, ffn_out, conv_in, conv_out, w_out, late, early):
    width, _, inner = ffn_in.shape
    share = late.shape[0] // (2 * keep.shape[0])
    collect_pieces(slots, keep, send, late)
    collect_pieces(slots, keep, send, early, share)
    late_runs, _ = plan_blocks(late_columns(width, inner))
    early_runs, _ = plan_blocks(early_columns(width, inner))
    for place, out in enumerate((ffn_in, ffn_out)):
        load_layer(early, early_runs[place], out, 0)
        load_layer(late, late_runs[place], out, 1)
    load_matrix(late, late_runs[2], conv_out, width)
    load_matrix(early, early_runs[2], conv_in, width)
    load_matrix(early, early_runs[3], conv_in, width, width)
    load_matrix(early, early_runs[4], w_out, width)


def finish_last_kernel(slots, keep, send, w_qkv, w_pos, d_bias, gains, biases, d_depth, packed):
    width = w_pos.shape[1]
    collect_pieces(slots, keep, send, packed)
    runs, total = plan_blocks(last_columns(width))
    load_matrix(packed, runs[0], w_qkv, width)
    load_matrix(packed, runs[1], w_pos, width)
    taps = d_depth.shape[0]
    start = total * block_rows(width)
    for lane in range(0, width, LANES):
        count = min(LANES, width - lane)
        lanes = slice(lane, lane + count)
        small = packed[start : start + SMALL, :count].astype(F32)
        d_bias[:, lanes] = small[0:2]
        gains[0:2, lanes] = small[2:4]
        biases[0:2, lanes] = small[4:6]
        gains[2:4, lanes] = small[6:8]
        biases[2:4, lanes] = small[8:10]
        d_depth[:, lanes] = small[10 : 10 + taps]
        start = start + SMALL


def local(inputs, w_qkv, w_pos, w_out, rel_bias, ffn_in, ffn_out, conv_in, conv_depth, conv_out, bn_gain, bn_bias, norm_gain, norm_bias, lengths, cotangent):
    _, rows, width = inputs.shape
    inner = ffn_in.shape[2]
    taps = conv_depth.shape[0]
    head_width = width // HEADS
    seq_count = lax.axis_size("seq")
    devices = device_count()
    place = lax.axis_index("seq").astype(jnp.int32).reshape(1)
    orders = arrival_order()

    turned = inputs[0].T
    in_both = ffn_in.transpose(1, 0, 2)
    in_early, in_late = in_both[:, 0], in_both[:, 1]
    out_both = ffn_out.transpose(2, 0, 1)
    out_early, out_late = out_both[:, 0], out_both[:, 1]
    gates = conv_in.T

    model = struct((rows, width), F32)
    model_low = struct((rows, width), BF16)
    inner_low = struct((rows, inner), BF16)
    head_low = struct((rows, HEADS * LANES), BF16)
    tile = struct((devices, 8, LANES), F32)
    reached = rows + 2 * HALO
    blocks, (
        block,
        query,
        shift,
        w_query,
        w_pair,
        w_pos_wide,
        w_out_wide,
        depth_wide,
        own_cos,
        own_sin,
        clip_rows,
        clip_wide,
        valid_wide,
        valid_rows,
        *by_order,
    ) = gather_frames(turned, lambda: call(
        functools.partial(prepare_kernel, orders),
        [
            model_low,
            struct((HEADS, rows, 4 * LANES), BF16),
            head_low,
            struct((width, HEADS * LANES), BF16),
            struct((HEADS, width, 2 * LANES), BF16),
            struct((WIDE, HEADS * LANES), BF16),
            struct((HEADS * LANES, width), BF16),
            struct((taps, WIDE), F32),
            struct((rows, WIDE), F32),
            struct((rows, WIDE), F32),
            struct((rows, 1), jnp.int32),
            struct((reached, LANES), jnp.int32),
            struct((reached, 1), F32),
            struct((rows, 1), F32),
        ]
        + [
            struct((high, len(order) * rows), dtype)
            for order in orders
            for high, dtype in ((WIDE, BF16), (1, jnp.int32))
        ],
        [place, lengths, turned, w_qkv, w_pos, w_out, rel_bias, conv_depth]
        + wave_tables(rows, seq_count, width),
        micros=5.5,
        smem=2,
    ))
    tables, clips = by_order[0::2], by_order[1::2]
    first_blocks, last_blocks = ([blocks[step] for step in order] for order in orders)
    blocks = first_blocks + last_blocks
    early_count = len(first_blocks)
    *carried, frames_one, pair_one = attend(
        first_blocks, query, w_pair, tables[0], clip_rows, clips[0], head_width
    )
    last_blocks = [after(last_blocks[0], pair_one)] + last_blocks[1:]
    attended, log_total, frames_two, pair_two = attend(
        last_blocks, query, w_pair, tables[1], clip_rows, clips[1], head_width, carried
    )
    pairs = (pair_one, pair_two)
    first_sum, second_sum, second_norm, left, right, gated, attended_low = call(
        early_kernel,
        [model, model, model, model, model, struct((rows, WIDE), BF16), head_low],
        [block, attended, w_out_wide, norm_gain, norm_bias, in_early, out_early, gates],
        micros=5.0,
    )
    gated_low = shift_seq(gated[rows - HALO :], 1)
    gated_high = shift_seq(gated[:HALO], -1)
    convolved, spread = call(
        functools.partial(conv_kernel, devices),
        [model, tile],
        [gated_low, gated, gated_high, clip_wide, depth_wide, valid_rows],
        scratch=[pltpu.VMEM((3, reached, LANES), F32)],
        micros=3.5,
    )
    arrived = exchange_small(spread)
    bn_gain_row, bn_bias_row = after(bn_gain, convolved)[None], after(bn_bias, convolved)[None]
    cotangent_turned = after(cotangent, convolved)[0].T
    slots = slot_pieces(devices, convolved)
    first_low, second_low, act_early, slope_early = call(
        again_kernel,
        [model_low, model_low, inner_low, inner_low],
        [first_sum, second_sum, norm_gain, norm_bias, in_early],
        micros=3.0,
    )

    def tap_sums(first, count, *factors):
        return call(
            functools.partial(taps_kernel, taps, count),
            [struct((taps, width), F32)] * count,
            [first, gated, gated_high, clip_wide] + list(factors),
            scratch=[pltpu.VMEM((3, reached, LANES), F32)],
            micros=2.5 + 1.0 * count,
        )

    depth_valid, depth_conv = tap_sums(gated_low, 2, convolved, valid_rows)
    arrived = after(arrived, first_low, depth_valid)
    edge = struct((2, HALO, width), F32)
    (
        result,
        act_late,
        d_inner_late,
        third_low,
        fourth_grad,
        swished,
        third_grad_low,
        third_grad,
        d_normed,
        unit,
        spread,
        late_norms,
        statistics,
        edge_low,
        edge_high,
    ) = call(
        functools.partial(late_kernel, devices),
        [struct((width, rows), F32), inner_low, inner_low, model_low, model_low, model_low]
        + [model_low, model, model, model]
        + [tile, struct((4, width), F32), struct((8, WIDE), F32), edge, edge],
        [arrived, convolved, second_norm, bn_gain_row, bn_bias_row, conv_out, norm_gain, norm_bias]
        + [in_late, out_late, cotangent_turned],
        micros=6.4,
    )
    from_low = shift_seq(edge_high, 1)
    from_high = shift_seq(edge_low, -1)
    arrived = exchange_small(spread)
    late_rows = packed_rows(late_columns(width, inner), width)
    outs, late_scratch = half_slots(late_rows, devices)
    late_keep, late_send = call(
        late_grads_kernel,
        outs,
        [slots, third_low, d_inner_late, act_late, fourth_grad, swished, third_grad_low],
        scratch=[late_scratch],
        micros=4.3,
        smem=1,
    )
    late_sum = SlotSum(late_keep, late_send)
    stat = struct((HEADS, rows, 1), F32)
    early_rows = packed_rows(early_columns(width, inner), width)
    outs, early_scratch = half_slots(early_rows, devices)
    result_out = result.T[None]
    arrived = after(arrived, result_out)
    mark = depth_valid
    mark = late_sum.step(mark)
    first_grad, d_attended, delta, early_norms, bn_grads, early_keep, early_send = call(
        middle_kernel,
        [model, head_low, stat, struct((4, width), F32), struct((2, width), F32)] + outs,
        [slots, after(arrived, late_keep, mark), statistics, bn_gain_row, d_normed, unit]
        + [from_low, from_high, clip_wide, valid_wide, depth_wide, left, right, gates, third_grad]
        + [second_sum, norm_gain, slope_early, first_sum, in_early, out_early, w_out_wide, attended]
        + [first_low, second_low, act_early, attended_low],
        scratch=[
            pltpu.VMEM((3, reached, LANES), F32),
            pltpu.VMEM((rows, width), F32),
            early_scratch,
        ],
        micros=12.0,
        smem=1,
    )
    early_sum = SlotSum(early_keep, early_send)
    mark = first_grad
    (depth_grad,) = tap_sums(after(gated_low, mark), 1, d_normed)
    mark = depth_grad
    mark = early_sum.step(mark)
    *d_frames, d_pair_weight, d_query_weight, d_pos_weight, d_bias, own_grad = attend_back(
        [len(order) for order in orders], after(query, mark), pairs, tables, clip_rows, clips,
        (frames_one, frames_two), log_total, delta, d_attended, shift, w_pos_wide, w_query, w_pair,
        own_cos, own_sin, turned, first_grad, head_width,
    )
    mark = own_grad
    late_sum.join(early_sum)
    both_sum = late_sum
    mark = both_sum.step(mark)
    last_rows = packed_rows(last_columns(width), width, 3 * SMALL)
    outs, packed = half_slots(last_rows, devices)
    last_keep, last_send = call(
        last_pack_kernel,
        outs,
        [slots, after(d_query_weight, mark), d_pair_weight, d_pos_weight, d_bias]
        + [depth_valid, depth_conv, depth_grad, statistics, bn_grads, bn_gain_row]
        + [late_norms, early_norms],
        scratch=[packed, pltpu.VMEM((block_rows(width + SMALL), 4 * width), F32)],
        micros=3.0,
        smem=1,
    )
    last_sum = SlotSum(last_keep, last_send)
    mark = last_keep
    frame_sum = FrameSum(d_frames[: seq_count // 2], [after(part, mark) for part in d_frames[seq_count // 2 :]])
    mark = both_sum.step(mark)
    mark = last_sum.step(mark)
    mark = both_sum.step(mark)
    frame_sum.step(mark)
    mark = frame_sum.joined[-1]
    mark = last_sum.step(mark)
    mark = last_sum.step(mark)
    mark = last_sum.step(mark, *frame_sum.arrived)
    input_grad = frame_sum.finish(own_grad)
    mark = both_sum.step(mark, input_grad)
    both_keep, both_send = both_sum.finish()
    square = struct((width, width), F32)
    sum_in, sum_out, sum_conv_in, sum_conv_out, sum_w_out = call(
        finish_two_kernel,
        [struct((width, 2, inner), F32)] * 2 + [struct((2 * width, width), F32), square, square],
        [slots, both_keep, both_send],
        scratch=[late_scratch, early_scratch],
        micros=10.0,
        smem=1,
    )
    mark = last_sum.step(sum_w_out)
    last_keep, last_send = last_sum.finish()
    last_share = share_rows(last_rows, devices) * devices
    sum_qkv, sum_pos, sum_rel, sum_gain, sum_bias, sum_depth = call(
        finish_last_kernel,
        [struct(w_qkv.shape, F32), struct(w_pos.shape, F32), struct(rel_bias.shape, F32)]
        + [struct(norm_gain.shape, F32), struct(norm_bias.shape, F32)]
        + [struct(conv_depth.shape, F32)],
        [slots, last_keep, last_send],
        scratch=[pltpu.VMEM((last_share, LANES), BF16)],
        micros=3.0,
        smem=1,
    )
    return (
        result_out,
        input_grad.T[None],
        sum_qkv,
        sum_pos,
        sum_w_out,
        sum_rel,
        sum_in.transpose(1, 0, 2),
        sum_out.transpose(1, 2, 0),
        sum_conv_in.T,
        sum_depth,
        sum_conv_out,
        bn_grads[0],
        bn_grads[1],
        sum_gain,
        sum_bias,
    )


def solution(mesh):
    whole = P()
    split = P("dp", "seq", None)
    return jax.shard_map(
        local,
        mesh=mesh,
        in_specs=(split,) + (whole,) * 13 + (P("dp", None), split),
        out_specs=(split, split) + (whole,) * 13,
        check_vma=False,
    )
```

```python
import functools
import math

import jax
import jax.numpy as jnp
from jax import lax
from jax.experimental import pallas as pl
from jax.experimental.pallas import tpu as pltpu
from jax.sharding import PartitionSpec as P
import numpy as np

HEADS = 4
LANES = 128
WIDE = 3 * LANES
HALO = 16
SMALL = 48
EPS = 1e-05
MODEL_AXES = ("seq", "dp")
VMEM_BYTES = 60 * 1024 * 1024
BF16 = jnp.bfloat16
F32 = jnp.float32


def device_count():
    return lax.axis_size("seq") * lax.axis_size("dp")


def flat_index():
    return lax.axis_index("seq") * lax.axis_size("dp") + lax.axis_index("dp")


def swap_flat(block, distance):
    pairs = [(i, i ^ distance) for i in range(device_count())]
    return lax.ppermute(block, MODEL_AXES, pairs)


def swap_seq(block, distance):
    pairs = [(i, i ^ distance) for i in range(lax.axis_size("seq"))]
    return lax.ppermute(block, "seq", pairs)


def shift_seq(block, step):
    count = lax.axis_size("seq")
    pairs = [(i, i + step) for i in range(count) if 0 <= i + step < count]
    return lax.ppermute(block, "seq", pairs)


def stage_radices(devices):
    radices = [2]
    left = devices // 2
    while left > 1:
        radix = 4 if left % 4 == 0 else 2
        radices.append(radix)
        left = left // radix
    return radices


def slot_pieces(devices, earlier):
    slots = jnp.arange(devices, dtype=jnp.int32)
    distance = jnp.zeros((devices,), jnp.int32)
    span = devices
    stride = 1
    for radix in stage_radices(devices):
        span = span // radix
        distance = distance + ((slots // span) % radix) * stride
        stride = stride * radix
    place = after(flat_index().astype(jnp.int32), earlier)
    return place ^ distance


def add_kernel(counts, radix, *refs):
    outs = refs[sum(counts) :]
    start = 0
    row = 0
    for count in counts:
        parts = refs[start : start + count]
        start = start + count
        total = parts[0][...].astype(F32)
        for part in parts[1:]:
            total = total + part[...].astype(F32)
        total = total.astype(BF16)
        span, share = total.shape[0] // radix, total.shape[1]
        for place, out in enumerate(outs):
            out[:, row : row + share] = total[place * span : (place + 1) * span]
        row = row + share


class SlotSum:
    def __init__(self, keep, send):
        self.others = []
        radices = stage_radices(device_count())
        strides = [1]
        for radix in radices[:-1]:
            strides.append(strides[-1] * radix)
        self.stages = list(zip(radices, strides))
        self.next = 1
        self.parts = self.scatter(0, [keep, send])
        self.mark = keep

    def join(self, other):
        self.others.append(other.parts)

    def scatter(self, stage, pieces):
        radix, stride = self.stages[stage]
        return [pieces[0]] + [
            swap_flat(pieces[step], step * stride) for step in range(radix - 1, 0, -1)
        ]

    def spread(self, stage, piece):
        radix, stride = self.stages[stage]
        return [piece] + [swap_flat(piece, step * stride) for step in range(1, radix)]

    def step(self, *earlier):
        count = len(self.stages)
        parts = self.parts
        if self.next >= 2 * count:
            return self.mark
        if earlier:
            parts = [after(parts[0], *earlier)] + parts[1:]
        if self.next <= count:
            radix = self.stages[self.next][0] if self.next < count else 1
            groups = [parts] + self.others
            self.others = []
            slots = parts[0].shape[0]
            if radix == 1:
                total = parts[0].astype(F32)
                for part in parts[1:]:
                    total = total + part.astype(F32)
                self.mark = total.astype(BF16)
                self.parts = self.spread(count - 1, self.mark)
                self.next = self.next + 1
                return self.mark
            share = sum(group[0].shape[1] for group in groups)
            pieces = call(
                functools.partial(add_kernel, [len(group) for group in groups], radix),
                [struct((slots // radix, share, LANES), BF16)] * radix,
                [part for group in groups for part in group],
                micros=2.0,
            )
            self.mark = pieces[0]
            self.parts = self.scatter(self.next, pieces)
        else:
            self.mark = jnp.concatenate(parts, axis=0)
            self.parts = self.spread(2 * count - 1 - self.next, self.mark)
        self.next = self.next + 1
        return self.mark

    def finish(self):
        while self.next < 2 * len(self.stages):
            self.step()
        return self.parts


def exchange_small(spread):
    return lax.all_to_all(spread, MODEL_AXES, 0, 0)


def after(value, *earlier):
    return lax.optimization_barrier((value,) + earlier)[0]


def arrival_order():
    count = lax.axis_size("seq")
    return [0, 1] + list(range(2, count, 2)), list(range(3, count, 2))


def gather_frames(shard, meanwhile):
    count = lax.axis_size("seq")
    across = [shard] + [swap_seq(shard, 2 * step) for step in range(1, count // 2)]
    made = meanwhile()
    blocks = []
    for step, block in enumerate(across):
        blocks.append(block)
        passed = block if step < count // 2 - 1 else after(block, made[0])
        blocks.append(swap_seq(passed, 1))
    return blocks, made


class FrameSum:
    def __init__(self, kept, passed):
        self.kept = kept
        self.passed = [swap_seq(pair, 1) for pair in passed]

    def step(self, *earlier):
        count = len(self.kept)
        self.arrived, self.joined = [], []
        for step in range(count - 1, 0, -1):
            came = self.passed[(count - 1 - step) // 2][(count - 1 - step) % 2]
            joined = self.kept[step].astype(F32) + came.astype(F32)
            if earlier:
                joined = after(joined, *earlier)
            self.joined.append(joined.astype(BF16))
            self.arrived.append(swap_seq(self.joined[-1], 2 * step))

    def finish(self, own):
        total = own + self.kept[0].astype(F32) + self.passed[-1][1].astype(F32)
        for block in self.arrived:
            total = total + block.astype(F32)
        return total


def cost(micros):
    return pl.CostEstimate(flops=int(micros * 0.460e9), bytes_accessed=0, transcendentals=0)


def call(body, outs, args, scratch=(), micros=2.0, smem=0):
    specs = [
        pl.BlockSpec(memory_space=pltpu.SMEM if place < smem else pltpu.VMEM)
        for place in range(len(args))
    ]
    return pl.pallas_call(
        body,
        out_shape=tuple(outs),
        in_specs=specs,
        out_specs=tuple(pl.BlockSpec(memory_space=pltpu.VMEM) for _ in outs),
        scratch_shapes=list(scratch),
        compiler_params=pltpu.CompilerParams(vmem_limit_bytes=VMEM_BYTES),
        cost_estimate=cost(micros),
    )(*args)


def struct(shape, dtype):
    return jax.ShapeDtypeStruct(tuple(shape), dtype)


def nn(left, right):
    return lax.dot_general(left, right, (((1,), (0,)), ((), ())), preferred_element_type=F32)


def nt(left, right):
    return lax.dot_general(left, right, (((1,), (1,)), ((), ())), preferred_element_type=F32)


def tn(left, right):
    return lax.dot_general(left, right, (((0,), (0,)), ((), ())), preferred_element_type=F32)


def norm_parts(summed):
    average = jnp.mean(summed, axis=-1, keepdims=True)
    centered = summed - average
    variance = jnp.mean(centered * centered, axis=-1, keepdims=True)
    inverse = lax.rsqrt(variance + EPS)
    return centered * inverse, inverse


def norm_back(unit, inverse, gain, incoming):
    scaled = incoming * gain
    first = jnp.mean(scaled, axis=-1, keepdims=True)
    second = jnp.mean(scaled * unit, axis=-1, keepdims=True)
    grad = inverse * (scaled - first - unit * second)
    return (
        grad,
        jnp.sum(incoming * unit, axis=0, keepdims=True),
        jnp.sum(incoming, axis=0, keepdims=True),
    )


def sigmoid(value):
    return 0.5 * jnp.tanh(0.5 * value) + 0.5


def silu_back(value):
    gate = sigmoid(value)
    return gate * (1.0 + value * (1.0 - gate))


def store_tile(ref, rows, copies):
    tile = jnp.zeros((8, LANES), F32)
    parts = []
    for row in rows:
        width = row.shape[1]
        blocks = -(-width // LANES)
        wide = row
        if blocks * LANES > width:
            wide = jnp.concatenate([row, jnp.zeros((1, blocks * LANES - width), F32)], axis=1)
        for block in range(blocks):
            parts.append(wide[:, block * LANES : (block + 1) * LANES])
    for place, part in enumerate(parts):
        tile = jnp.where(
            lax.broadcasted_iota(jnp.int32, (8, LANES), 0) == place,
            jnp.broadcast_to(part, (8, LANES)),
            tile,
        )
    ref[...] = jnp.broadcast_to(tile[None], (copies, 8, LANES))


def tile_row(tile, place, width):
    blocks = -(-width // LANES)
    parts = [tile[place * blocks + block : place * blocks + block + 1] for block in range(blocks)]
    return jnp.concatenate(parts, axis=1)[:, :width]


def plan_blocks(columns):
    runs = []
    block = 0
    for count in columns:
        full = count // LANES
        runs.append([(block + place, 0, place * LANES, LANES) for place in range(full)])
        block = block + full
    open_block, lane = None, LANES
    for place, count in enumerate(columns):
        rest = count % LANES
        if rest:
            if lane + rest > LANES:
                open_block, lane = block, 0
                block = block + 1
            runs[place].append((open_block, lane, count - rest, rest))
            lane = lane + rest
    return runs, block


def block_rows(rows):
    return -(-rows // 8) * 8


def store_matrix(packed, runs, value):
    rows = value.shape[0]
    low = value.astype(BF16)
    for block, lane, column, count in runs:
        start = block * block_rows(rows)
        packed[start : start + rows, lane : lane + count] = low[:, column : column + count]


def load_matrix(packed, runs, out, rows, row=0):
    for block, lane, column, count in runs:
        start = block * block_rows(rows)
        out[row : row + rows, column : column + count] = packed[
            start : start + rows, lane : lane + count
        ].astype(F32)


def load_layer(packed, runs, out, layer):
    rows = out.shape[0]
    for block, lane, column, count in runs:
        start = block * block_rows(rows)
        out[:, layer, column : column + count] = packed[
            start : start + rows, lane : lane + count
        ].astype(F32)


def spread_pieces(slots_ref, packed, keep_ref, send_ref):
    half, share = keep_ref.shape[:2]

    def one(slot, nothing):
        low = pl.multiple_of(slots_ref[slot] * share, HALO)
        keep_ref[slot] = packed[pl.ds(low, share), :]
        high = pl.multiple_of(slots_ref[slot + half] * share, HALO)
        send_ref[slot] = packed[pl.ds(high, share), :]
        return nothing

    lax.fori_loop(0, half, one, 0)


def collect_pieces(slots_ref, keep_ref, send_ref, packed, row=0):
    half = keep_ref.shape[0]
    share = packed.shape[0] // (2 * half)

    def one(slot, nothing):
        low = pl.multiple_of(slots_ref[slot] * share, HALO)
        packed[pl.ds(low, share), :] = keep_ref[slot, row : row + share]
        high = pl.multiple_of(slots_ref[slot + half] * share, HALO)
        packed[pl.ds(high, share), :] = send_ref[slot, row : row + share]
        return nothing

    lax.fori_loop(0, half, one, 0)


def share_rows(rows, devices):
    return -(-rows // (HALO * devices)) * HALO


def half_slots(rows, devices):
    share = share_rows(rows, devices)
    return [struct((devices // 2, share, LANES), BF16)] * 2, pltpu.VMEM((devices * share, LANES), BF16)


def wave_tables(rows, blocks, width):
    half = width // 2
    frequency = np.exp(np.arange(half) * (-2.0 * math.log(10000.0) / width))
    tail = np.zeros(LANES // 2)
    tail[: half - LANES] = frequency[LANES:]
    lanes = np.concatenate([frequency[:LANES], frequency[:LANES], tail, tail])[None]
    row_angles = np.arange(rows)[:, None] * lanes
    block_angles = (np.arange(blocks) * rows)[:, None] * lanes
    return [
        jnp.asarray(table.astype(np.float32))
        for table in (
            np.cos(row_angles),
            np.sin(row_angles),
            np.cos(block_angles),
            np.sin(block_angles),
        )
    ]


def half_pieces(width):
    half = width // 2
    rest = half - LANES
    return (
        (0, 0, LANES),
        (half, LANES, LANES),
        (LANES, 2 * LANES, rest),
        (half + LANES, 2 * LANES + LANES // 2, rest),
    )


def half_sign():
    lane = lax.broadcasted_iota(jnp.int32, (1, LANES), 1)
    return jnp.where(lane < LANES // 2, 1.0, -1.0)


def prepare_kernel(orders, where, lengths, turned, w_qkv, w_pos, w_out, bias, depth, base_cos, base_sin, block_cos, block_sin, block, query, shift, w_query, w_pair, w_pos_wide, w_out_wide, depth_wide, own_cos, own_sin, clip_rows, clip_wide, valid_wide, valid_rows, *by_order):
    place = where[0]
    width, rows = turned.shape
    size = width // HEADS
    blocks = block_cos.shape[0]
    w_query[...] = jnp.zeros_like(w_query)
    w_pair[...] = jnp.zeros_like(w_pair)
    w_pos_wide[...] = jnp.zeros_like(w_pos_wide)
    w_out_wide[...] = jnp.zeros_like(w_out_wide)
    depth_wide[...] = jnp.zeros_like(depth_wide)
    depth_wide[:, :width] = depth[...]
    for head in range(HEADS):
        natural = slice(head * size, (head + 1) * size)
        low = head * LANES
        w_query[:, low : low + size] = w_qkv[:, head * size : (head + 1) * size]
        w_pair[head, :, :size] = w_qkv[:, width + head * size : width + (head + 1) * size]
        w_pair[head, :, LANES : LANES + size] = w_qkv[
            :, 2 * width + head * size : 2 * width + (head + 1) * size
        ]
        w_out_wide[low : low + size] = w_out[natural]
        for source, target, length in half_pieces(width):
            w_pos_wide[target : target + length, low : low + size] = w_pos[
                source : source + length, natural
            ]
    lane = lax.broadcasted_iota(jnp.int32, (1, WIDE), 1)
    on_cosine = (lane < LANES) | ((lane >= 2 * LANES) & (lane < 2 * LANES + LANES // 2))
    row_cos, row_sin = base_cos[...], base_sin[...]
    ends = [lengths[0, 0]]
    for clip in range(1, lengths.shape[1]):
        ends.append(ends[-1] + lengths[0, clip])

    def clip_at(frames):
        clip = jnp.zeros_like(frames)
        for end in ends:
            clip = clip + (frames >= end).astype(jnp.int32)
        return clip

    for order, table, clip_columns in zip(orders, by_order[0::2], by_order[1::2]):
        for step, distance in enumerate(order):
            here = place ^ distance
            cosine = block_cos[pl.ds(here, 1), :]
            sine = block_sin[pl.ds(here, 1), :]
            one = jnp.where(on_cosine, cosine, sine)
            two = jnp.where(on_cosine, -sine, cosine)
            lanes = slice(step * rows, (step + 1) * rows)
            table[:, lanes] = (one * row_cos + two * row_sin).astype(BF16).T
            clip_columns[:, lanes] = clip_at(
                here * rows + lax.broadcasted_iota(jnp.int32, (1, rows), 1)
            )
    reached = place * rows - HALO + lax.broadcasted_iota(jnp.int32, (rows + 2 * HALO, LANES), 0)
    inside = (reached >= 0) & (reached < blocks * rows)
    reached_clip = jnp.where(inside, clip_at(reached), -1)
    clip_wide[...] = reached_clip
    clip_rows[...] = reached_clip[HALO : HALO + rows, 0:1]
    valid = (inside & (reached < ends[-1])).astype(F32)[:, 0:1]
    valid_wide[...] = valid
    valid_rows[...] = valid[HALO : HALO + rows]
    block_cosine = block_cos[pl.ds(place, 1), :]
    block_sine = block_sin[pl.ds(place, 1), :]
    cosines = block_cosine * row_cos - block_sine * row_sin
    sines = block_sine * row_cos + block_cosine * row_sin
    own_cos[...] = cosines
    own_sin[...] = sines
    frames = turned[...].T
    block[...] = frames
    projected = nn(frames, w_query[...])
    sign = half_sign()
    for head in range(HEADS):
        lanes = slice(head * LANES, (head + 1) * LANES)
        natural = slice(head * size, (head + 1) * size)
        wide = jnp.zeros((2, LANES - size), F32)
        added = jnp.concatenate([bias[:, natural], wide], axis=1)
        unit = (projected[:, lanes] + added[0:1]).astype(BF16)
        moved = (projected[:, lanes] + added[1:2]).astype(BF16)
        shift[:, lanes] = moved
        shifted = nt(moved, w_pos_wide[:, lanes])
        first, second = shifted[:, :LANES], shifted[:, LANES : 2 * LANES]
        tail = shifted[:, 2 * LANES :]
        sine, cosine = sines[:, :LANES], cosines[:, :LANES]
        query[head, :, :LANES] = unit
        query[head, :, LANES : 2 * LANES] = (first * sine + second * cosine).astype(BF16)
        query[head, :, 2 * LANES : 3 * LANES] = (second * sine - first * cosine).astype(BF16)
        query[head, :, 3 * LANES :] = (
            tail * sines[:, 2 * LANES :]
            + pltpu.roll(tail, LANES // 2, 1) * cosines[:, 2 * LANES :] * sign
        ).astype(BF16)


def masked_scores(query, upper, table, clip_rows, clip_columns, scale):
    raw = nn(query[:, : 2 * LANES], upper) + nn(query[:, 2 * LANES :], table[LANES:])
    return jnp.where(clip_rows == clip_columns, raw * (scale / math.log(2.0)), -1e30)


def attend_kernel(scale, count, last, *refs):
    blocks = refs[:count]
    query, w_pair, table, clip_rows, clip_columns = refs[count : count + 5]
    carried = refs[count + 5 : count + 8] if last else None
    outs = refs[count + (8 if last else 5) :]
    rows = blocks[0].shape[1]
    heads = query.shape[0]
    frames_all, pair = outs[-2:]

    @pl.when(pl.program_id(0) == 0)
    def _():
        for step in range(count):
            frames_all[:, step * rows : (step + 1) * rows] = blocks[step][...]

    def scored(head):
        both = tn(w_pair[head], frames_all[...]).astype(BF16)
        pair[head] = both
        upper = jnp.concatenate([both[:LANES], table[:LANES]], axis=0)
        return both[LANES:], masked_scores(
            query[head], upper, table[...], clip_rows[...], clip_columns[...], scale
        )

    following = scored(0)
    for head in range(heads):
        values, scores = following
        if head + 1 < heads:
            following = scored(head + 1)
        lanes = slice(head * LANES, (head + 1) * LANES)
        highest = jnp.max(scores, axis=1, keepdims=True)
        if last:
            highest = jnp.maximum(highest, carried[0][head])
        weights = jnp.exp2(scores - highest)
        total = jnp.sum(weights, axis=1, keepdims=True)
        summed = nt(weights.astype(BF16), values)
        if last:
            fade = jnp.exp2(carried[0][head] - highest)
            total = total + carried[1][head] * fade
            summed = summed + carried[2][:, lanes] * fade
            attended, log_total = outs[:2]
            attended[:, lanes] = summed / total
            log_total[head] = highest + jnp.log2(total)
        else:
            outs[0][head] = highest
            outs[1][head] = total
            outs[2][:, lanes] = summed


def heads_at_once(frames):
    return 2 if frames <= 2048 else 1


def attend(blocks, query, w_pair, table, clip_rows, clip_columns, head_width, carried=()):
    rows = query.shape[1]
    frames = table.shape[1]
    width = w_pair.shape[1]
    per = heads_at_once(frames)
    stat = pl.BlockSpec((per, rows, 1), lambda h: (h, 0, 0))
    head = pl.BlockSpec((rows, per * LANES), lambda h: (0, h))
    stat_shape = struct((HEADS, rows, 1), F32)
    head_shape = struct((rows, HEADS * LANES), F32)
    last = len(carried) > 0
    return pl.pallas_call(
        functools.partial(attend_kernel, 1.0 / math.sqrt(head_width), len(blocks), last),
        grid=(HEADS // per,),
        in_specs=[pl.BlockSpec((width, rows), lambda h: (0, 0)) for _ in blocks]
        + [
            pl.BlockSpec((per, rows, 4 * LANES), lambda h: (h, 0, 0)),
            pl.BlockSpec((per, width, 2 * LANES), lambda h: (h, 0, 0)),
            pl.BlockSpec((WIDE, frames), lambda h: (0, 0)),
            pl.BlockSpec((rows, 1), lambda h: (0, 0)),
            pl.BlockSpec((1, frames), lambda h: (0, 0)),
        ]
        + ([stat, stat, head] if last else []),
        out_specs=((head, stat) if last else (stat, stat, head))
        + (
            pl.BlockSpec((width, frames), lambda h: (0, 0)),
            pl.BlockSpec((per, 2 * LANES, frames), lambda h: (h, 0, 0)),
        ),
        out_shape=((head_shape, stat_shape) if last else (stat_shape, stat_shape, head_shape))
        + (struct((width, frames), BF16), struct((HEADS, 2 * LANES, frames), BF16)),
        compiler_params=pltpu.CompilerParams(vmem_limit_bytes=VMEM_BYTES),
        cost_estimate=cost(5.0 if last else 8.0),
    )(*blocks, query, w_pair, table, clip_rows, clip_columns, *carried)


def early_kernel(block, attended, w_out, gains, biases, ffn_in, ffn_out, gates, first_sum, second_sum, second_norm, left, right, gated, attended_low):
    low = attended[...].astype(BF16)
    attended_low[...] = low
    summed = block[...].astype(F32) + nn(low, w_out[...])
    first_sum[...] = summed
    unit, _ = norm_parts(summed)
    first = unit * gains[0:1] + biases[0:1]
    inner = nn(first.astype(BF16), ffn_in[...])
    act = (inner * sigmoid(inner)).astype(BF16)
    summed = first + nt(act, ffn_out[...])
    second_sum[...] = summed
    unit, _ = norm_parts(summed)
    second = unit * gains[1:2] + biases[1:2]
    second_norm[...] = second
    second_low = second.astype(BF16)
    half = gates.shape[0] // 2
    one = nt(second_low, gates[:half])
    two = nt(second_low, gates[half:])
    left[...] = one
    right[...] = two
    gated[...] = jnp.zeros_like(gated)
    gated[:, : one.shape[1]] = (one * sigmoid(two)).astype(BF16)


def again_kernel(first_sum, second_sum, gains, biases, ffn_in, first_low_out, second_low_out, act_out, slope_out):
    unit, _ = norm_parts(second_sum[...])
    second_low_out[...] = (unit * gains[1:2] + biases[1:2]).astype(BF16)
    unit, _ = norm_parts(first_sum[...])
    first_low = (unit * gains[0:1] + biases[0:1]).astype(BF16)
    first_low_out[...] = first_low
    inner = nn(first_low, ffn_in[...])
    gate = sigmoid(inner)
    act_out[...] = (inner * gate).astype(BF16)
    slope_out[...] = (gate * (1.0 + inner * (1.0 - gate))).astype(BF16)


def lane_blocks(width):
    return [(lane, min(LANES, width - lane)) for lane in range(0, width, LANES)]


def extend(extended, low, middle, high):
    rows, width = middle.shape
    for block, (lane, count) in enumerate(lane_blocks(width)):
        if count < LANES:
            extended[block] = jnp.zeros((rows + 2 * HALO, LANES), F32)
        extended[block, 0:HALO, :count] = low[:, lane : lane + count].astype(F32)
        extended[block, HALO : HALO + rows, :count] = middle[:, lane : lane + count].astype(F32)
        extended[block, HALO + rows :, :count] = high[:, lane : lane + count].astype(F32)


def convolve(extended, clip, depth, mirrored, store):
    taps = depth.shape[0]
    blocks, rows, _ = extended.shape
    rows = rows - 2 * HALO
    step = 64
    for start in range(0, rows, step):
        own = clip[HALO + start : HALO + start + step]
        sums = [jnp.zeros((step, LANES), F32) for _ in range(blocks)]
        for tap in range(taps):
            place = HALO - taps // 2 + tap + start
            same = clip[place : place + step] == own
            row = taps - 1 - tap if mirrored else tap
            for block in range(blocks):
                lanes = slice(block * LANES, (block + 1) * LANES)
                sums[block] = sums[block] + depth[row : row + 1, lanes] * jnp.where(
                    same, extended[block, place : place + step], 0.0
                )
        store(start, step, jnp.concatenate(sums, axis=1))


def conv_kernel(copies, low, middle, high, clip, depth, valid, convolved, tile, extended):
    rows, width = convolved.shape
    extend(extended, low[...], middle[...], high[...])

    def store(start, step, value):
        convolved[start : start + step] = value[:, :width]

    convolve(extended, clip, depth, False, store)
    value = convolved[...]
    kept = value * valid[...]
    count = jnp.zeros((1, width), F32) + jnp.sum(valid[...], axis=0, keepdims=True)
    store_tile(
        tile,
        [
            jnp.sum(kept, axis=0, keepdims=True),
            jnp.sum(kept * value, axis=0, keepdims=True),
            count[:, :LANES],
        ],
        copies,
    )


def taps_kernel(taps, count, low, middle, high, clip, *refs):
    factor, *valid = refs[: 1 if count == 1 else 2]
    outs, extended = refs[len(valid) + 1 : -1], refs[-1]
    rows, width = factor.shape
    extend(extended, low[...], middle[...], high[...])
    step = 64
    sums = [[[None] * 3 for _ in range(taps)] for _ in range(count)]
    for start in range(0, rows, step):
        own = clip[HALO + start : HALO + start + step]
        for block, (lane, lanes) in enumerate(lane_blocks(width)):
            part = factor[start : start + step, lane : lane + lanes]
            if lanes < LANES:
                part = jnp.concatenate([part, jnp.zeros((step, LANES - lanes), F32)], axis=1)
            here = [part]
            if valid:
                kept = valid[0][start : start + step]
                here = [jnp.broadcast_to(kept, (step, LANES)), part * kept]
            for tap in range(taps):
                place = HALO - taps // 2 + tap + start
                same = clip[place : place + step] == own
                there = jnp.where(same, extended[block, place : place + step], 0.0)
                for which in range(count):
                    part = jnp.sum((there * here[which]).reshape(step // 8, 8, LANES), axis=0)
                    old = sums[which][tap][block]
                    sums[which][tap][block] = part if old is None else old + part
    for which in range(count):
        for tap in range(taps):
            outs[which][tap : tap + 1] = jnp.concatenate(
                [jnp.sum(part, axis=0, keepdims=True) for part in sums[which][tap]], axis=1
            )[:, :width]


def late_kernel(copies, arrived, convolved, second_norm, bn_gain, bn_bias, conv_out, gains, biases, ffn_in, ffn_out, cotangent, result, act_out, d_inner_out, third_low_out, fourth_grad_out, swished_out, third_grad_out, third_grad, d_normed_out, unit_out, tile, norm_grads, statistics, edge_low, edge_high):
    width = convolved.shape[1]
    rows = convolved.shape[0]
    sums = jnp.sum(arrived[...], axis=0)
    frames = sums[6:7, 0:1]
    mean = tile_row(sums, 0, width) / frames
    variance = tile_row(sums, 1, width) / frames - mean * mean
    inverse = lax.rsqrt(variance + EPS)
    unit = (convolved[...] - mean) * inverse
    unit_out[...] = unit
    statistics[...] = jnp.zeros_like(statistics)
    statistics[0:1, :width] = inverse
    statistics[1:2, :width] = jnp.broadcast_to(frames, (1, width))
    statistics[2:3, :width] = mean
    normed = unit * bn_gain[...] + bn_bias[...]
    swished = (normed * sigmoid(normed)).astype(BF16)
    swished_out[...] = swished
    third_unit, third_inverse = norm_parts(second_norm[...] + nn(swished, conv_out[...]))
    third = third_unit * gains[2:3] + biases[2:3]
    third_low = third.astype(BF16)
    third_low_out[...] = third_low
    inner = nn(third_low, ffn_in[...])
    gate = sigmoid(inner)
    act = (inner * gate).astype(BF16)
    act_out[...] = act
    fourth_unit, fourth_inverse = norm_parts(third + nt(act, ffn_out[...]))
    result[...] = (fourth_unit * gains[3:4] + biases[3:4]).T
    fourth_grad, gain_three, bias_three = norm_back(
        fourth_unit, fourth_inverse, gains[3:4], cotangent[...].T
    )
    fourth_low = fourth_grad.astype(BF16)
    fourth_grad_out[...] = fourth_low
    d_act = nn(fourth_low, ffn_out[...])
    d_inner = (d_act * (gate * (1.0 + inner * (1.0 - gate)))).astype(BF16)
    d_inner_out[...] = d_inner
    grad, gain_two, bias_two = norm_back(
        third_unit, third_inverse, gains[2:3], fourth_grad + nt(d_inner, ffn_in[...])
    )
    third_grad[...] = grad
    grad_low = grad.astype(BF16)
    third_grad_out[...] = grad_low
    d_normed = nt(grad_low, conv_out[...]) * silu_back(normed)
    d_normed_out[...] = d_normed
    store_tile(
        tile,
        [
            jnp.sum(d_normed * unit, axis=0, keepdims=True),
            jnp.sum(d_normed, axis=0, keepdims=True),
        ],
        copies,
    )
    norm_grads[0:1] = gain_two
    norm_grads[1:2] = gain_three
    norm_grads[2:3] = bias_two
    norm_grads[3:4] = bias_three
    edge_low[0] = d_normed[:HALO]
    edge_low[1] = unit[:HALO]
    edge_high[0] = d_normed[rows - HALO :]
    edge_high[1] = unit[rows - HALO :]


def late_columns(width, inner):
    return (inner, inner, width)


def early_columns(width, inner):
    return (inner, inner, width, width, width)


def last_columns(width):
    return (3 * width, width)


def packed_rows(columns, width, small=0):
    _, blocks = plan_blocks(columns)
    return blocks * block_rows(width) + small


def late_grads_kernel(slots, third_low, d_inner, act, fourth_grad, swished, third_grad, keep, send, packed):
    width = third_low.shape[1]
    runs, _ = plan_blocks(late_columns(width, act.shape[1]))
    store_matrix(packed, runs[0], tn(third_low[...], d_inner[...]))
    store_matrix(packed, runs[1], tn(fourth_grad[...], act[...]))
    store_matrix(packed, runs[2], tn(swished[...], third_grad[...]))
    spread_pieces(slots, packed, keep, send)


def middle_kernel(slots, arrived, statistics, bn_gain, d_normed, unit, from_low, from_high, clip, valid, depth, left, right, gates, third_grad, second_sum, gains, slope, first_sum, ffn_in, ffn_out, w_out, attended, first_low, second_low, act, attended_low, first_grad, d_attended, delta, norm_grads, bn_grads, keep, send, extended, d_gated, packed):
    rows, width = left.shape
    sums = jnp.sum(arrived[...], axis=0)
    gain_sum = tile_row(sums, 0, width)
    bias_sum = tile_row(sums, 1, width)
    bn_grads[0:1] = gain_sum
    bn_grads[1:2] = bias_sum
    gain = bn_gain[...]
    inverse = statistics[0:1, :width]
    frames = statistics[1:2, :width]

    def conv_grad(d_rows, unit_rows, valid_rows):
        return (
            inverse * gain * (d_rows - valid_rows * (bias_sum + unit_rows * gain_sum) / frames)
        ).astype(BF16)

    extend(
        extended,
        conv_grad(from_low[0], from_low[1], valid[0:HALO]),
        conv_grad(d_normed[...], unit[...], valid[HALO : HALO + rows]),
        conv_grad(from_high[0], from_high[1], valid[HALO + rows :]),
    )

    def store(start, step, value):
        d_gated[start : start + step] = value[:, :width]

    convolve(extended, clip, depth, True, store)
    gate = sigmoid(right[...])
    d_left = (d_gated[...] * gate).astype(BF16)
    d_right = (d_gated[...] * left[...] * gate * (1.0 - gate)).astype(BF16)
    second_unit, second_inverse = norm_parts(second_sum[...])
    half = gates.shape[0] // 2
    incoming = third_grad[...] + nn(d_left, gates[:half]) + nn(d_right, gates[half:])
    second_grad, gain_one, bias_one = norm_back(
        second_unit, second_inverse, gains[1:2], incoming
    )
    second_grad_low = second_grad.astype(BF16)
    d_act = nn(second_grad_low, ffn_out[...])
    d_inner = (d_act * slope[...].astype(F32)).astype(BF16)
    first_unit, first_inverse = norm_parts(first_sum[...])
    grad, gain_zero, bias_zero = norm_back(
        first_unit, first_inverse, gains[0:1], second_grad + nt(d_inner, ffn_in[...])
    )
    first_grad[...] = grad
    grad_low = grad.astype(BF16)
    for place, part in enumerate((gain_zero, gain_one, bias_zero, bias_one)):
        norm_grads[place : place + 1] = part
    back = nt(grad_low, w_out[...]).astype(BF16)
    d_attended[...] = back
    product = back.astype(F32) * attended[...]
    for head in range(HEADS):
        delta[head] = jnp.sum(
            product[:, head * LANES : (head + 1) * LANES], axis=1, keepdims=True
        )
    size = width // HEADS
    runs, _ = plan_blocks(early_columns(width, act.shape[1]))
    store_matrix(packed, runs[0], tn(first_low[...], d_inner))
    store_matrix(packed, runs[1], tn(second_grad_low, act[...]))
    store_matrix(packed, runs[2], tn(d_left, second_low[...]))
    store_matrix(packed, runs[3], tn(d_right, second_low[...]))
    d_out = tn(attended_low[...], grad_low)
    store_matrix(
        packed,
        runs[4],
        jnp.concatenate([d_out[head * LANES : head * LANES + size] for head in range(HEADS)], axis=0),
    )
    spread_pieces(slots, packed, keep, send)


def attend_back_kernel(scale, counts, query, pair_one, pair_two, table_one, table_two, clip_rows, clip_one, clip_two, frames_one, frames_two, log_total, delta, d_attended, shift, w_pos, w_query, w_pair, own_cos, own_sin, turned, first_grad, *refs):
    blocks = sum(counts)
    kept, passed = refs[: blocks // 2], refs[blocks // 2 : blocks // 2 + blocks // 4]
    d_pair_weight, d_query_weight, d_pos_weight, d_bias, own_grad, d_frames, d_pair, own_sum = refs[
        blocks // 2 + blocks // 4 :
    ]
    group = pl.program_id(0)
    rows = clip_rows.shape[0]
    heads = query.shape[0]
    cosines, sines = own_cos[...], own_sin[...]
    runs = (
        (pair_one, table_one, clip_one, frames_one),
        (pair_two, table_two, clip_two, frames_two),
    )
    pieces = []
    start = 0
    for run in runs:
        for low in range(0, run[3].shape[1], 5 * rows):
            length = min(5 * rows, run[3].shape[1] - low)
            pieces.append(run + (slice(low, low + length), slice(start, start + length)))
            start = start + length
    work = [(head, piece) for head in range(heads) for piece in pieces]

    def scored(head, piece):
        pair, table, clip_columns, _, here, _ = piece
        lanes = slice(head * LANES, (head + 1) * LANES)
        upper = jnp.concatenate([pair[head, :LANES, here], table[:LANES, here]], axis=0)
        scores = masked_scores(
            query[head], upper, table[:, here], clip_rows[...], clip_columns[:, here], scale
        )
        return upper, scores, nn(d_attended[:, lanes], pair[head, LANES:, here])

    following = scored(*work[0])
    for place, (head, piece) in enumerate(work):
        _, table, _, frames, here, span = piece
        lanes = slice(head * LANES, (head + 1) * LANES)
        upper, scores, slope = following
        if place + 1 < len(work):
            following = scored(*work[place + 1])
        probs = jnp.exp2(scores - log_total[head])
        d_raw = (probs * (slope * scale - delta[head] * scale)).astype(BF16)
        d_pair[:LANES, span] = nn(query[head, :, :LANES].T, d_raw).astype(BF16)
        d_pair[LANES:, span] = nn(d_attended[:, lanes].T, probs.astype(BF16)).astype(BF16)
        first_piece = place % len(pieces) == 0
        unit_part = nt(d_raw, upper)
        rest_part = nt(d_raw, table[LANES:, here])
        weight_part = nt(frames[:, here], d_pair[:, span])
        unit_sum = unit_part if first_piece else unit_sum + unit_part
        rest_sum = rest_part if first_piece else rest_sum + rest_part
        weight_sum = weight_part if first_piece else weight_sum + weight_part
        by_frame = nn(w_pair[head], d_pair[:, span])
        if head > 0:
            d_frames[:, span] += by_frame
        else:

            @pl.when(group == 0)
            def _():
                d_frames[:, span] = by_frame

            @pl.when(group > 0)
            def _():
                d_frames[:, span] += by_frame

        if place % len(pieces) < len(pieces) - 1:
            continue
        d_pair_weight[head] = weight_sum.astype(BF16)
        d_unit = unit_sum[:, :LANES]
        first, second = unit_sum[:, LANES:], rest_sum[:, :LANES]
        tail = rest_sum[:, LANES:]
        sine, cosine = sines[:, :LANES], cosines[:, :LANES]
        d_shifted = jnp.concatenate(
            [
                first * sine - second * cosine,
                first * cosine + second * sine,
                tail * sines[:, 2 * LANES :]
                - pltpu.roll(tail, LANES // 2, 1) * cosines[:, 2 * LANES :] * half_sign(),
            ],
            axis=1,
        ).astype(BF16)
        d_from_pos = nn(d_shifted, w_pos[:, lanes])
        d_query = (d_unit + d_from_pos).astype(BF16)
        d_query_weight[:, lanes] = nn(turned[...], d_query).astype(BF16)
        d_pos_weight[:, lanes] = tn(d_shifted, shift[:, lanes]).astype(BF16)
        d_bias[0:1, lanes] = jnp.sum(d_unit, axis=0, keepdims=True)
        d_bias[1:2, lanes] = jnp.sum(d_from_pos, axis=0, keepdims=True)
        own = nt(d_query, w_query[:, lanes])
        if head > 0:
            own_sum[...] += own
        else:

            @pl.when(group == 0)
            def _():
                own_sum[...] = first_grad[...] + own

            @pl.when(group > 0)
            def _():
                own_sum[...] += own

    @pl.when(group == HEADS // heads - 1)
    def _():
        own_grad[...] = own_sum[...].T
        orders = [0, 1] + list(range(2, blocks, 2)) + list(range(3, blocks, 2))
        for step in range(blocks // 2):
            lanes = orders.index(2 * step) * rows
            kept[step][...] = d_frames[:, lanes : lanes + rows].astype(BF16)
            lanes = orders.index(2 * step + 1) * rows
            place = blocks // 2 - 1 - step
            passed[place // 2][place % 2] = d_frames[:, lanes : lanes + rows].astype(BF16)


def attend_back(counts, query, pairs, tables, clip_rows, clips, frames, log_total, delta, d_attended, shift, w_pos, w_query, w_pair, own_cos, own_sin, turned, first_grad, head_width):
    rows = query.shape[1]
    width = turned.shape[0]
    wide = HEADS * LANES
    blocks = sum(counts)
    total = blocks * rows
    per = heads_at_once(total)

    def whole(array):
        return pl.BlockSpec(
            array.shape, lambda h: (0,) * len(array.shape), pipeline_mode=pl.Buffered(1)
        )

    def by_head(array):
        return pl.BlockSpec((per,) + array.shape[1:], lambda h: (h, 0, 0))

    def head_lanes(array):
        return pl.BlockSpec((array.shape[0], per * LANES), lambda h: (0, h))

    kept = [struct((width, rows), BF16)] * (blocks // 2)
    passed = [struct((2, width, rows), BF16)] * (blocks // 4)
    by_head_shapes = [struct((HEADS, width, 2 * LANES), BF16)]
    by_lane_shapes = [struct((width, wide), BF16), struct((WIDE, wide), BF16), struct((2, wide), F32)]
    own = struct((width, rows), F32)
    return pl.pallas_call(
        functools.partial(attend_back_kernel, 1.0 / math.sqrt(head_width), counts),
        grid=(HEADS // per,),
        in_specs=[by_head(query)]
        + [by_head(pair) for pair in pairs]
        + [whole(table) for table in tables]
        + [whole(clip_rows)]
        + [whole(clip) for clip in clips]
        + [whole(part) for part in frames]
        + [by_head(log_total), by_head(delta), head_lanes(d_attended), head_lanes(shift)]
        + [head_lanes(w_pos), head_lanes(w_query), by_head(w_pair), whole(own_cos)]
        + [whole(own_sin), whole(turned), whole(first_grad)],
        out_specs=tuple(whole(shape) for shape in kept + passed)
        + tuple(by_head(shape) for shape in by_head_shapes)
        + tuple(head_lanes(shape) for shape in by_lane_shapes)
        + (whole(own),),
        out_shape=tuple(kept + passed + by_head_shapes + by_lane_shapes + [own]),
        scratch_shapes=[
            pltpu.VMEM((width, total), F32),
            pltpu.VMEM((2 * LANES, total), BF16),
            pltpu.VMEM((rows, width), F32),
        ],
        compiler_params=pltpu.CompilerParams(vmem_limit_bytes=VMEM_BYTES),
        cost_estimate=cost(20.0),
    )(query, *pairs, *tables, clip_rows, *clips, *frames, log_total, delta, d_attended, shift, w_pos, w_query, w_pair, own_cos, own_sin, turned, first_grad)


def last_pack_kernel(slots, d_query_weight, d_pair_weight, d_pos, d_bias, depth_valid, depth_conv, depth_grad, statistics, bn_grads, bn_gain, late_norms, early_norms, keep, send, packed, natural):
    width = d_query_weight.shape[0]
    size = width // HEADS
    runs, total = plan_blocks(last_columns(width))
    for head in range(HEADS):
        lanes = slice(head * size, (head + 1) * size)
        low = head * LANES
        natural[:width, lanes] = d_query_weight[:, low : low + size].astype(F32)
        natural[:width, width + head * size : width + (head + 1) * size] = d_pair_weight[
            head, :, :size
        ].astype(F32)
        natural[:width, 2 * width + head * size : 2 * width + (head + 1) * size] = d_pair_weight[
            head, :, LANES : LANES + size
        ].astype(F32)
        for start, spread, length in half_pieces(width):
            natural[start : start + length, 3 * width + head * size : 3 * width + (head + 1) * size] = (
                d_pos[spread : spread + length, low : low + size].astype(F32)
            )
        natural[width : width + 2, lanes] = d_bias[:, low : low + size]
    taps = depth_valid.shape[0]
    inverse, frames, mean = (statistics[row : row + 1, :width] for row in range(3))
    gain_sum, bias_sum = bn_grads[0:1], bn_grads[1:2]
    by_unit = (depth_conv[...] - mean * depth_valid[...]) * inverse
    d_depth = (
        inverse
        * bn_gain[...]
        * (depth_grad[...] - (bias_sum * depth_valid[...] + gain_sum * by_unit) / frames)
    )
    natural[width + 2 : width + 6, :width] = early_norms[...]
    natural[width + 6 : width + 10, :width] = late_norms[...]
    natural[width + 10 : width + 10 + taps, :width] = d_depth
    store_matrix(packed, runs[0], natural[:width, : 3 * width])
    store_matrix(packed, runs[1], natural[:width, 3 * width :])
    start = total * block_rows(width)
    for lane in range(0, width, LANES):
        count = min(LANES, width - lane)
        packed[start : start + 10 + taps, :count] = natural[
            width : width + 10 + taps, lane : lane + count
        ].astype(BF16)
        start = start + SMALL
    spread_pieces(slots, packed, keep, send)


def finish_two_kernel(slots, keep, send, ffn_in, ffn_out, conv_in, conv_out, w_out, late, early):
    width, _, inner = ffn_in.shape
    share = late.shape[0] // (2 * keep.shape[0])
    collect_pieces(slots, keep, send, late)
    collect_pieces(slots, keep, send, early, share)
    late_runs, _ = plan_blocks(late_columns(width, inner))
    early_runs, _ = plan_blocks(early_columns(width, inner))
    for place, out in enumerate((ffn_in, ffn_out)):
        load_layer(early, early_runs[place], out, 0)
        load_layer(late, late_runs[place], out, 1)
    load_matrix(late, late_runs[2], conv_out, width)
    load_matrix(early, early_runs[2], conv_in, width)
    load_matrix(early, early_runs[3], conv_in, width, width)
    load_matrix(early, early_runs[4], w_out, width)


def finish_last_kernel(slots, keep, send, w_qkv, w_pos, d_bias, gains, biases, d_depth, packed):
    width = w_pos.shape[1]
    collect_pieces(slots, keep, send, packed)
    runs, total = plan_blocks(last_columns(width))
    load_matrix(packed, runs[0], w_qkv, width)
    load_matrix(packed, runs[1], w_pos, width)
    taps = d_depth.shape[0]
    start = total * block_rows(width)
    for lane in range(0, width, LANES):
        count = min(LANES, width - lane)
        lanes = slice(lane, lane + count)
        small = packed[start : start + SMALL, :count].astype(F32)
        d_bias[:, lanes] = small[0:2]
        gains[0:2, lanes] = small[2:4]
        biases[0:2, lanes] = small[4:6]
        gains[2:4, lanes] = small[6:8]
        biases[2:4, lanes] = small[8:10]
        d_depth[:, lanes] = small[10 : 10 + taps]
        start = start + SMALL


def local(inputs, w_qkv, w_pos, w_out, rel_bias, ffn_in, ffn_out, conv_in, conv_depth, conv_out, bn_gain, bn_bias, norm_gain, norm_bias, lengths, cotangent):
    _, rows, width = inputs.shape
    inner = ffn_in.shape[2]
    taps = conv_depth.shape[0]
    head_width = width // HEADS
    seq_count = lax.axis_size("seq")
    devices = device_count()
    place = lax.axis_index("seq").astype(jnp.int32).reshape(1)
    orders = arrival_order()

    turned = inputs[0].T
    in_both = ffn_in.transpose(1, 0, 2)
    in_early, in_late = in_both[:, 0], in_both[:, 1]
    out_both = ffn_out.transpose(2, 0, 1)
    out_early, out_late = out_both[:, 0], out_both[:, 1]
    gates = conv_in.T

    model = struct((rows, width), F32)
    model_low = struct((rows, width), BF16)
    inner_low = struct((rows, inner), BF16)
    head_low = struct((rows, HEADS * LANES), BF16)
    tile = struct((devices, 8, LANES), F32)
    reached = rows + 2 * HALO
    blocks, (
        block,
        query,
        shift,
        w_query,
        w_pair,
        w_pos_wide,
        w_out_wide,
        depth_wide,
        own_cos,
        own_sin,
        clip_rows,
        clip_wide,
        valid_wide,
        valid_rows,
        *by_order,
    ) = gather_frames(turned, lambda: call(
        functools.partial(prepare_kernel, orders),
        [
            model_low,
            struct((HEADS, rows, 4 * LANES), BF16),
            head_low,
            struct((width, HEADS * LANES), BF16),
            struct((HEADS, width, 2 * LANES), BF16),
            struct((WIDE, HEADS * LANES), BF16),
            struct((HEADS * LANES, width), BF16),
            struct((taps, WIDE), F32),
            struct((rows, WIDE), F32),
            struct((rows, WIDE), F32),
            struct((rows, 1), jnp.int32),
            struct((reached, LANES), jnp.int32),
            struct((reached, 1), F32),
            struct((rows, 1), F32),
        ]
        + [
            struct((high, len(order) * rows), dtype)
            for order in orders
            for high, dtype in ((WIDE, BF16), (1, jnp.int32))
        ],
        [place, lengths, turned, w_qkv, w_pos, w_out, rel_bias, conv_depth]
        + wave_tables(rows, seq_count, width),
        micros=5.5,
        smem=2,
    ))
    tables, clips = by_order[0::2], by_order[1::2]
    first_blocks, last_blocks = ([blocks[step] for step in order] for order in orders)
    blocks = first_blocks + last_blocks
    early_count = len(first_blocks)
    *carried, frames_one, pair_one = attend(
        first_blocks, query, w_pair, tables[0], clip_rows, clips[0], head_width
    )
    last_blocks = [after(last_blocks[0], pair_one)] + last_blocks[1:]
    attended, log_total, frames_two, pair_two = attend(
        last_blocks, query, w_pair, tables[1], clip_rows, clips[1], head_width, carried
    )
    pairs = (pair_one, pair_two)
    first_sum, second_sum, second_norm, left, right, gated, attended_low = call(
        early_kernel,
        [model, model, model, model, model, struct((rows, WIDE), BF16), head_low],
        [block, attended, w_out_wide, norm_gain, norm_bias, in_early, out_early, gates],
        micros=5.0,
    )
    gated_low = shift_seq(gated[rows - HALO :], 1)
    gated_high = shift_seq(gated[:HALO], -1)
    convolved, spread = call(
        functools.partial(conv_kernel, devices),
        [model, tile],
        [gated_low, gated, gated_high, clip_wide, depth_wide, valid_rows],
        scratch=[pltpu.VMEM((3, reached, LANES), F32)],
        micros=3.5,
    )
    arrived = exchange_small(spread)
    bn_gain_row, bn_bias_row = after(bn_gain, convolved)[None], after(bn_bias, convolved)[None]
    cotangent_turned = after(cotangent, convolved)[0].T
    slots = slot_pieces(devices, convolved)
    first_low, second_low, act_early, slope_early = call(
        again_kernel,
        [model_low, model_low, inner_low, inner_low],
        [first_sum, second_sum, norm_gain, norm_bias, in_early],
        micros=3.0,
    )

    def tap_sums(first, count, *factors):
        return call(
            functools.partial(taps_kernel, taps, count),
            [struct((taps, width), F32)] * count,
            [first, gated, gated_high, clip_wide] + list(factors),
            scratch=[pltpu.VMEM((3, reached, LANES), F32)],
            micros=2.5 + 1.0 * count,
        )

    depth_valid, depth_conv = tap_sums(gated_low, 2, convolved, valid_rows)
    arrived = after(arrived, first_low, depth_valid)
    edge = struct((2, HALO, width), F32)
    (
        result,
        act_late,
        d_inner_late,
        third_low,
        fourth_grad,
        swished,
        third_grad_low,
        third_grad,
        d_normed,
        unit,
        spread,
        late_norms,
        statistics,
        edge_low,
        edge_high,
    ) = call(
        functools.partial(late_kernel, devices),
        [struct((width, rows), F32), inner_low, inner_low, model_low, model_low, model_low]
        + [model_low, model, model, model]
        + [tile, struct((4, width), F32), struct((8, WIDE), F32), edge, edge],
        [arrived, convolved, second_norm, bn_gain_row, bn_bias_row, conv_out, norm_gain, norm_bias]
        + [in_late, out_late, cotangent_turned],
        micros=6.4,
    )
    from_low = shift_seq(edge_high, 1)
    from_high = shift_seq(edge_low, -1)
    arrived = exchange_small(spread)
    late_rows = packed_rows(late_columns(width, inner), width)
    outs, late_scratch = half_slots(late_rows, devices)
    late_keep, late_send = call(
        late_grads_kernel,
        outs,
        [slots, third_low, d_inner_late, act_late, fourth_grad, swished, third_grad_low],
        scratch=[late_scratch],
        micros=4.3,
        smem=1,
    )
    late_sum = SlotSum(late_keep, late_send)
    stat = struct((HEADS, rows, 1), F32)
    early_rows = packed_rows(early_columns(width, inner), width)
    outs, early_scratch = half_slots(early_rows, devices)
    result_out = result.T[None]
    arrived = after(arrived, result_out)
    mark = depth_valid
    mark = late_sum.step(mark)
    first_grad, d_attended, delta, early_norms, bn_grads, early_keep, early_send = call(
        middle_kernel,
        [model, head_low, stat, struct((4, width), F32), struct((2, width), F32)] + outs,
        [slots, after(arrived, late_keep, mark), statistics, bn_gain_row, d_normed, unit]
        + [from_low, from_high, clip_wide, valid_wide, depth_wide, left, right, gates, third_grad]
        + [second_sum, norm_gain, slope_early, first_sum, in_early, out_early, w_out_wide, attended]
        + [first_low, second_low, act_early, attended_low],
        scratch=[
            pltpu.VMEM((3, reached, LANES), F32),
            pltpu.VMEM((rows, width), F32),
            early_scratch,
        ],
        micros=12.0,
        smem=1,
    )
    early_sum = SlotSum(early_keep, early_send)
    mark = first_grad
    (depth_grad,) = tap_sums(after(gated_low, mark), 1, d_normed)
    mark = depth_grad
    mark = early_sum.step(mark)
    *d_frames, d_pair_weight, d_query_weight, d_pos_weight, d_bias, own_grad = attend_back(
        [len(order) for order in orders], after(query, mark), pairs, tables, clip_rows, clips,
        (frames_one, frames_two), log_total, delta, d_attended, shift, w_pos_wide, w_query, w_pair,
        own_cos, own_sin, turned, first_grad, head_width,
    )
    mark = own_grad
    late_sum.join(early_sum)
    both_sum = late_sum
    mark = both_sum.step(mark)
    last_rows = packed_rows(last_columns(width), width, 3 * SMALL)
    outs, packed = half_slots(last_rows, devices)
    last_keep, last_send = call(
        last_pack_kernel,
        outs,
        [slots, after(d_query_weight, mark), d_pair_weight, d_pos_weight, d_bias]
        + [depth_valid, depth_conv, depth_grad, statistics, bn_grads, bn_gain_row]
        + [late_norms, early_norms],
        scratch=[packed, pltpu.VMEM((block_rows(width + SMALL), 4 * width), F32)],
        micros=3.0,
        smem=1,
    )
    last_sum = SlotSum(last_keep, last_send)
    mark = last_keep
    frame_sum = FrameSum(d_frames[: seq_count // 2], [after(part, mark) for part in d_frames[seq_count // 2 :]])
    mark = both_sum.step(mark)
    mark = last_sum.step(mark)
    mark = both_sum.step(mark)
    frame_sum.step(mark)
    mark = frame_sum.joined[-1]
    mark = last_sum.step(mark)
    mark = last_sum.step(mark)
    mark = both_sum.step(mark, *frame_sum.arrived)
    input_grad = frame_sum.finish(own_grad)
    mark = last_sum.step(mark, input_grad)
    both_keep, both_send = both_sum.finish()
    square = struct((width, width), F32)
    sum_in, sum_out, sum_conv_in, sum_conv_out, sum_w_out = call(
        finish_two_kernel,
        [struct((width, 2, inner), F32)] * 2 + [struct((2 * width, width), F32), square, square],
        [slots, both_keep, both_send],
        scratch=[late_scratch, early_scratch],
        micros=10.0,
        smem=1,
    )
    mark = last_sum.step(sum_w_out)
    last_keep, last_send = last_sum.finish()
    last_share = share_rows(last_rows, devices) * devices
    sum_qkv, sum_pos, sum_rel, sum_gain, sum_bias, sum_depth = call(
        finish_last_kernel,
        [struct(w_qkv.shape, F32), struct(w_pos.shape, F32), struct(rel_bias.shape, F32)]
        + [struct(norm_gain.shape, F32), struct(norm_bias.shape, F32)]
        + [struct(conv_depth.shape, F32)],
        [slots, last_keep, last_send],
        scratch=[pltpu.VMEM((last_share, LANES), BF16)],
        micros=3.0,
        smem=1,
    )
    return (
        result_out,
        input_grad.T[None],
        sum_qkv,
        sum_pos,
        sum_w_out,
        sum_rel,
        sum_in.transpose(1, 0, 2),
        sum_out.transpose(1, 2, 0),
        sum_conv_in.T,
        sum_depth,
        sum_conv_out,
        bn_grads[0],
        bn_grads[1],
        sum_gain,
        sum_bias,
    )


def solution(mesh):
    whole = P()
    split = P("dp", "seq", None)
    return jax.shard_map(
        local,
        mesh=mesh,
        in_specs=(split,) + (whole,) * 13 + (P("dp", None), split),
        out_specs=(split, split) + (whole,) * 13,
        check_vma=False,
    )
```
